32 devices in a mesh: fsdp: 4 (over y, x), seq: 8 (over z, core).
Axes of the slice: x: 2, y: 2, z: 4, core: 2. Of those that a mesh axis runs over, the one named last changes fastest.
Arguments:
- inputs: bfloat16 [8, 1024, 1024], P('fsdp', 'seq'), may hold values from -6 to 6
- segment_ids: int32 [8, 1024], P('fsdp', 'seq'), may hold values from 0 to 17, as said below
- query_weight: bfloat16 [2, 1024, 1024], P(None, ('fsdp', 'seq')), may hold values from -0.1875 to 0.1875
- key_weight: bfloat16 [2, 1024, 1024], P(None, ('fsdp', 'seq')), may hold values from -0.1875 to 0.1875
- value_weight: bfloat16 [2, 1024, 1024], P(None, ('fsdp', 'seq')), may hold values from -0.1875 to 0.1875
- out_weight: bfloat16 [2, 1024, 1024], P(None, ('fsdp', 'seq')), may hold values from -1 to 1
- fc_in_weight: bfloat16 [2, 1024, 4096], P(None, ('fsdp', 'seq')), may hold values from -0.1875 to 0.1875
- fc_out_weight: bfloat16 [2, 4096, 1024], P(None, ('fsdp', 'seq')), may hold values from -0.09375 to 0.09375
- attn_gain: bfloat16 [2, 1024], P(None, ('fsdp', 'seq')), may hold values from 0.5 to 1.5
- attn_shift: bfloat16 [2, 1024], P(None, ('fsdp', 'seq')), may hold values from -1.5 to 1.5
- ffn_gain: bfloat16 [2, 1024], P(None, ('fsdp', 'seq')), may hold values from 0.5 to 1.5
- ffn_shift: bfloat16 [2, 1024], P(None, ('fsdp', 'seq')), may hold values from -1.5 to 1.5
- cotangent: bfloat16 [8, 1024, 1024], P('fsdp', 'seq'), may hold values from -6 to 6
Outputs:
- outputs: float32 [8, 1024, 1024], P('fsdp', 'seq')
- input_grad: float32 [8, 1024, 1024], P('fsdp', 'seq')
- query_weight_grad: float32 [2, 1024, 1024], P(None, ('fsdp', 'seq'))
- key_weight_grad: float32 [2, 1024, 1024], P(None, ('fsdp', 'seq'))
- value_weight_grad: float32 [2, 1024, 1024], P(None, ('fsdp', 'seq'))
- out_weight_grad: float32 [2, 1024, 1024], P(None, ('fsdp', 'seq'))
- fc_in_weight_grad: float32 [2, 1024, 4096], P(None, ('fsdp', 'seq'))
- fc_out_weight_grad: float32 [2, 4096, 1024], P(None, ('fsdp', 'seq'))
- attn_gain_grad: float32 [2, 1024], P(None, ('fsdp', 'seq'))
- attn_shift_grad: float32 [2, 1024], P(None, ('fsdp', 'seq'))
- ffn_gain_grad: float32 [2, 1024], P(None, ('fsdp', 'seq'))
- ffn_shift_grad: float32 [2, 1024], P(None, ('fsdp', 'seq'))
The draws below stay inside these ranges and needn't reach their ends.
Inputs may be any that keep to these rules, and one draw needn't show every extreme that they name: `segment_ids`: within each sequence the ids start at 0 and rise by one at each document boundary. Of the 2 sequences on each index of fsdp, one drawn from the seed is a single document; the others pack documents of 60 to 800 tokens, the last one cut short by the sequence's end. Exactly one sequence of the batch packs documents of exactly 60 tokens.
All inputs are finite; a program needn't handle non-finite values.
Results may differ from the reference program's by a relative error of at most 0.033.
Values may be sent and summed in bfloat16 or wider, within the bound.
No kernel may reach another device: no remote copies, remote signals or barrier semaphores. Data moves between devices by JAX's collectives and lax.ppermute only.
A program may use at most 320 MiB of HBM per device.

```python
import math
import jax
import jax.numpy as jnp
from jax import lax

D = 1024
HEADS = 16
FF = 4096
LAYERS = 2
MB = 2
DOC_MIN = 60
DOC_MAX = 800
LEN = 1024
SEQS = 8


def draw_segment_ids(key, part):
    key = jax.random.fold_in(key, 11)
    size_key, pick_key, group_key = jax.random.split(key, 3)
    doc_count = LEN // DOC_MIN + 1
    doc_sizes = jax.random.randint(size_key, (SEQS, doc_count), DOC_MIN, DOC_MAX + 1)
    doc_ends = jnp.cumsum(doc_sizes, axis=1)
    positions = jnp.arange(LEN, dtype=jnp.int32)
    doc_numbers = jnp.sum((doc_ends[:, None, :] <= positions[None, :, None]).astype(jnp.int32), axis=2)
    whole_pick = jax.random.randint(pick_key, (SEQS // MB,), 0, MB)
    chosen = jnp.arange(SEQS) % MB == jnp.repeat(whole_pick, MB)
    dense_group = jax.random.randint(group_key, (), 0, SEQS // MB)
    dense_row = dense_group * MB + (whole_pick[dense_group] + 1) % MB
    dense = jnp.arange(SEQS) == dense_row
    dense_numbers = positions // DOC_MIN
    mixed = jnp.where(dense[:, None], dense_numbers[None, :], doc_numbers)
    return jnp.where(chosen[:, None], 0, mixed).astype(jnp.int32)


def levels(key, shape, cuts, smallest, top_value):
    gain, own = 1.0, jax.random.fold_in(key, 6)
    for position, blocks in cuts:
        draws = jnp.exp(jax.random.uniform(jax.random.fold_in(own, position), (blocks,), jnp.float32, smallest / len(cuts), top_value / len(cuts)))
        gain = gain * jnp.repeat(draws, shape[position] // blocks).reshape([-1 if axis == position else 1 for axis in range(len(shape))])
    return gain


def normal_values(stream_key, dims, deviation, limit, pieces=(), kind=jnp.bfloat16):
    drawn = deviation * jax.random.normal(stream_key, dims, jnp.float32)
    if pieces:
        drawn = drawn * levels(stream_key, dims, pieces, -0.22, 0.18)
    return jnp.clip(drawn, -limit, limit).astype(kind)


def setup_inputs(seed: int = 0) -> dict:
    keys = jax.random.split(jax.random.key(seed), 14)
    inputs = normal_values(keys[0], (SEQS, LEN, D), 1.0, 6.0, ((0, 4), (1, 8)))
    segment_ids = draw_segment_ids(jax.random.fold_in(keys[13], 71), 0)
    query_weight = normal_values(keys[2], (LAYERS, D, D), D ** -0.5, 0.1875, ((1, 32),))
    key_weight = normal_values(keys[3], (LAYERS, D, D), D ** -0.5, 0.1875, ((1, 32),))
    value_weight = normal_values(keys[4], (LAYERS, D, D), D ** -0.5, 0.1875, ((1, 32),))
    out_weight = normal_values(keys[5], (LAYERS, D, D), (D // 32) ** -0.5, 1.0, ((1, 32),))
    fc_in_weight = normal_values(keys[6], (LAYERS, D, FF), D ** -0.5, 0.1875, ((1, 32),))
    fc_out_weight = normal_values(keys[7], (LAYERS, FF, D), FF ** -0.5, 0.09375, ((1, 32),))
    attn_gain = jnp.clip(1.0 + 0.1 * jax.random.normal(keys[8], (LAYERS, D), jnp.float32), 0.5, 1.5).astype(jnp.bfloat16)
    attn_shift = normal_values(keys[9], (LAYERS, D), 0.3, 1.5, ((1, 32),))
    ffn_gain = jnp.clip(1.0 + 0.1 * jax.random.normal(keys[10], (LAYERS, D), jnp.float32), 0.5, 1.5).astype(jnp.bfloat16)
    ffn_shift = normal_values(keys[11], (LAYERS, D), 0.3, 1.5, ((1, 32),))
    cotangent = normal_values(keys[12], (SEQS, LEN, D), 1.0, 6.0, ((0, 4), (1, 8)))
    return {"inputs": inputs, "segment_ids": segment_ids, "query_weight": query_weight, "key_weight": key_weight, "value_weight": value_weight, "out_weight": out_weight, "fc_in_weight": fc_in_weight, "fc_out_weight": fc_out_weight, "attn_gain": attn_gain, "attn_shift": attn_shift, "ffn_gain": ffn_gain, "ffn_shift": ffn_shift, "cotangent": cotangent}


HIGHEST = lax.Precision.HIGHEST
NEG_FILL = -1e+30
NORM_EPS = 1e-05

@jax.custom_vjp
def low(v):
    return lax.optimization_barrier(v.astype(jnp.bfloat16)).astype(jnp.float32)

@jax.custom_vjp
def low_back(v):
    return v

def low_keep(v):
    return (low(v), None)

def low_pass(kept, grad):
    return (grad,)

def back_keep(v):
    return (v, None)

def back_low(kept, grad):
    return (low(grad),)
low.defvjp(low_keep, low_pass)
low_back.defvjp(back_keep, back_low)

def project(values, weight):
    return jnp.einsum('gtd,de->gte', values, weight, precision=HIGHEST)

def layer_norm(summed, norm_gain, norm_shift):
    center = lax.optimization_barrier(jnp.mean(summed, axis=-1, keepdims=True))
    offset = summed - center
    spread = lax.optimization_barrier(jnp.mean(offset * offset, axis=-1, keepdims=True))
    return offset * lax.rsqrt(spread + NORM_EPS) * norm_gain + norm_shift

def attend(queries, key_rows, value_rows, doc_ids):
    groups, length = doc_ids.shape
    block_rows = math.gcd(length, 512)
    block_count = length // block_rows
    head_dim = queries.shape[-1] // HEADS
    score_scale = head_dim ** (-0.5)
    query_blocks = queries.reshape(groups, block_count, block_rows, HEADS, head_dim).transpose(1, 0, 2, 3, 4)
    query_ids = doc_ids.reshape(groups, block_count, block_rows).transpose(1, 0, 2)
    key_heads = key_rows.reshape(groups, length, HEADS, head_dim)
    value_heads = value_rows.reshape(groups, length, HEADS, head_dim)

    def one_block(block_pair):
        query_block, block_ids = block_pair
        scores = jnp.einsum('gqhe,gkhe->ghqk', query_block, key_heads, precision=HIGHEST)
        scores = low_back(scores * score_scale)
        allowed = block_ids[:, None, :, None] == doc_ids[:, None, None, :]
        scores = jnp.where(allowed, scores, NEG_FILL)
        largest = lax.optimization_barrier(jnp.max(scores, axis=-1, keepdims=True))
        weights = jnp.exp(scores - largest)
        attn_probs = low(weights / lax.optimization_barrier(jnp.sum(weights, axis=-1, keepdims=True)))
        return jnp.einsum('ghqk,gkhe->gqhe', attn_probs, value_heads, precision=HIGHEST)
    attended = lax.map(jax.checkpoint(one_block), (query_blocks, query_ids))
    return attended.transpose(1, 0, 2, 3, 4).reshape(queries.shape)

def encoder_layer(hidden, params, doc_ids):
    w_query, w_key, w_value, w_out, w_in_ff, w_out_ff, gain_attn, shift_attn, gain_ffn, shift_ffn = params
    lowered = low(hidden)
    queries = low(low_back(project(lowered, w_query)))
    key_rows = low(low_back(project(lowered, w_key)))
    value_rows = low(low_back(project(lowered, w_value)))
    attended = low(low_back(attend(queries, key_rows, value_rows, doc_ids)))
    branch = low_back(project(attended, w_out))
    middle = layer_norm(hidden + branch, gain_attn, shift_attn)
    before = low_back(project(low(middle), w_in_ff))
    active = low(jax.nn.gelu(before, approximate=False))
    ff_branch = low_back(project(active, w_out_ff))
    return layer_norm(middle + ff_branch, gain_ffn, shift_ffn)

def encoder_stack(weight_set, hidden, doc_ids):
    for layer_index in range(LAYERS):
        hidden = encoder_layer(hidden, tuple((weight[layer_index] for weight in weight_set)), doc_ids)
    return hidden

def reference(inputs, segment_ids, query_weight, key_weight, value_weight, out_weight, fc_in_weight, fc_out_weight, attn_gain, attn_shift, ffn_gain, ffn_shift, cotangent):
    weights = tuple((weight.astype(jnp.float32) for weight in (query_weight, key_weight, value_weight, out_weight, fc_in_weight, fc_out_weight, attn_gain, attn_shift, ffn_gain, ffn_shift)))
    group_size = math.gcd(SEQS, max(1, 4096 // LEN))
    batches = SEQS // group_size
    hidden = inputs.astype(jnp.float32).reshape(batches, group_size, LEN, D)
    doc_ids = segment_ids.reshape(batches, group_size, LEN)
    upstream = cotangent.astype(jnp.float32).reshape(batches, group_size, LEN, D)

    def one_group(totals, group_item):
        group_hidden, group_ids, group_grad = group_item
        result, pullback = jax.vjp(lambda weight_set, start_rows: encoder_stack(weight_set, start_rows, group_ids), weights, group_hidden)
        weight_grads, input_grads = pullback(group_grad)
        totals = tuple((running_total + grad_part for running_total, grad_part in zip(totals, weight_grads)))
        return (totals, (result, input_grads))
    zeros_start = tuple((jnp.zeros_like(weight) for weight in weights))
    totals, (results, input_grads) = lax.scan(one_group, zeros_start, (hidden, doc_ids, upstream))
    return (results.reshape(SEQS, LEN, D), input_grads.reshape(SEQS, LEN, D), totals[0], totals[1], totals[2], totals[3], totals[4], totals[5], totals[6], totals[7], totals[8], totals[9])
```

```python
import functools

import jax
import jax.numpy as jnp
from jax import lax
from jax.experimental import pallas as pl
from jax.experimental.pallas import tpu as pltpu
from jax.sharding import PartitionSpec as P

HEADS = 16
NEG_FILL = -1e30
NORM_EPS = 1e-05
inv_root_two = 0.7071067811865476
inv_root_two_pi = 0.3989422804014327
BF = jnp.bfloat16
F32 = jnp.float32
VMEM_BYTES = 48 * 1024 * 1024


def mm(a, b, out=F32):
    return lax.dot_general(a, b, (((1,), (0,)), ((), ())), preferred_element_type=F32).astype(out)


def mm_t(a, b, out=F32):
    return lax.dot_general(a, b, (((1,), (1,)), ((), ())), preferred_element_type=F32).astype(out)


def mm_outer(a, b, out=F32):
    return lax.dot_general(a, b, (((0,), (0,)), ((), ())), preferred_element_type=F32).astype(out)


def pick_head(lanes, head, head_dim):
    return (lanes >= head * head_dim) & (lanes < (head + 1) * head_dim)


def attn_forward_kernel(head_dim, q_ref, k_ref, v_ref, ids_q_ref, ids_k_ref, o_ref):
    queries, keys, values = q_ref[...], k_ref[...], v_ref[...]
    width = queries.shape[1]
    lanes = lax.broadcasted_iota(jnp.int32, (1, width), 1)
    allowed = ids_q_ref[...] == ids_k_ref[...]
    total = jnp.zeros(queries.shape, F32)
    for head in range(width // head_dim):
        here = pick_head(lanes, head, head_dim)
        scores = mm_t(jnp.where(here, queries, jnp.zeros_like(queries)), keys)
        scores = jnp.where(allowed, scores, NEG_FILL)
        weights = jnp.exp(scores - jnp.max(scores, axis=1, keepdims=True))
        norm = 1.0 / jnp.sum(weights, axis=1, keepdims=True)
        out = mm(weights.astype(BF), values) * norm
        total = jnp.where(here, out, total)
    o_ref[...] = total.astype(BF)


def attn_forward(qkv, ids, head_dim):
    tokens, width = qkv.shape[0], qkv.shape[1] // 3
    rows = min(256, tokens)
    return pl.pallas_call(
        functools.partial(attn_forward_kernel, head_dim),
        grid=(tokens // rows,),
        in_specs=[
            pl.BlockSpec((rows, width), lambda i: (i, 0)),
            pl.BlockSpec((tokens, width), lambda i: (0, 1)),
            pl.BlockSpec((tokens, width), lambda i: (0, 2)),
            pl.BlockSpec((rows, 1), lambda i: (i, 0)),
            pl.BlockSpec((1, tokens), lambda i: (0, 0)),
        ],
        out_specs=pl.BlockSpec((rows, width), lambda i: (i, 0)),
        out_shape=jax.ShapeDtypeStruct((tokens, width), BF),
        compiler_params=pltpu.CompilerParams(vmem_limit_bytes=VMEM_BYTES),
        cost_estimate=pl.CostEstimate(
            flops=4 * tokens * tokens * width * (width // head_dim),
            bytes_accessed=8 * tokens * width,
            transcendentals=tokens * tokens * (width // head_dim),
        ),
    )(qkv, qkv, qkv, ids.reshape(tokens, 1), ids.reshape(1, tokens))


def attn_backward_kernel(
    head_dim, q_ref, k_ref, v_ref, g_ref, ids_q_ref, ids_k_ref, out_ref, dk_ref, dv_ref
):
    step = pl.program_id(0)
    queries, keys, values, grads = q_ref[...], k_ref[...], v_ref[...], g_ref[...]
    rows, width = queries.shape
    lanes = lax.broadcasted_iota(jnp.int32, (1, width), 1)
    allowed = ids_q_ref[...] == ids_k_ref[...]
    dq = jnp.zeros(queries.shape, F32)

    @pl.when(step == 0)
    def _():
        dk_ref[...] = jnp.zeros_like(dk_ref)
        dv_ref[...] = jnp.zeros_like(dv_ref)

    for head in range(width // head_dim):
        here = pick_head(lanes, head, head_dim)
        q_head = jnp.where(here, queries, jnp.zeros_like(queries))
        g_head = jnp.where(here, grads, jnp.zeros_like(grads))
        scores = mm_t(q_head, keys)
        scores = jnp.where(allowed, scores, NEG_FILL)
        weights = jnp.exp(scores - jnp.max(scores, axis=1, keepdims=True))
        probs = weights * (1.0 / jnp.sum(weights, axis=1, keepdims=True))
        prob_grad = mm_t(g_head, values)
        product = probs * prob_grad
        delta = jnp.sum(product, axis=1, keepdims=True)
        score_grad = (product - probs * delta).astype(BF)
        dq = jnp.where(here, mm(score_grad, keys), dq)
        dk_ref[...] += mm_outer(score_grad, q_head)
        dv_ref[...] += mm_outer(probs.astype(BF), g_head)
    out_ref[pl.ds(pl.multiple_of(step * rows, rows), rows), :width] = (
        dq * head_dim**-0.5
    ).astype(BF)

    @pl.when(step == pl.num_programs(0) - 1)
    def _():
        out_ref[:, width : 2 * width] = dk_ref[...].astype(BF)
        out_ref[:, 2 * width :] = dv_ref[...].astype(BF)


def attn_backward(qkv, grads, ids, head_dim):
    tokens, width = grads.shape
    rows = min(256, tokens)
    return pl.pallas_call(
        functools.partial(attn_backward_kernel, head_dim),
        grid=(tokens // rows,),
        in_specs=[
            pl.BlockSpec((rows, width), lambda i: (i, 0)),
            pl.BlockSpec((tokens, width), lambda i: (0, 1)),
            pl.BlockSpec((tokens, width), lambda i: (0, 2)),
            pl.BlockSpec((rows, width), lambda i: (i, 0)),
            pl.BlockSpec((rows, 1), lambda i: (i, 0)),
            pl.BlockSpec((1, tokens), lambda i: (0, 0)),
        ],
        out_specs=pl.BlockSpec((tokens, 3 * width), lambda i: (0, 0)),
        out_shape=jax.ShapeDtypeStruct((tokens, 3 * width), BF),
        scratch_shapes=[pltpu.VMEM((tokens, width), F32), pltpu.VMEM((tokens, width), F32)],
        compiler_params=pltpu.CompilerParams(vmem_limit_bytes=VMEM_BYTES),
        cost_estimate=pl.CostEstimate(
            flops=10 * tokens * tokens * width * (width // head_dim),
            bytes_accessed=14 * tokens * width,
            transcendentals=tokens * tokens * (width // head_dim),
        ),
    )(qkv, qkv, qkv, grads, ids.reshape(tokens, 1), ids.reshape(1, tokens))


def norm_forward(summed, norm_gain, norm_shift):
    center = jnp.mean(summed, axis=-1, keepdims=True)
    offset = summed - center
    spread = jnp.mean(offset * offset, axis=-1, keepdims=True)
    inverse = lax.rsqrt(spread + NORM_EPS)
    normed = offset * inverse
    return (normed * norm_gain + norm_shift, normed, inverse)


def norm_backward(upstream, normed, inverse, norm_gain):
    gain_grad = jnp.sum(upstream * normed, axis=0)
    shift_grad = jnp.sum(upstream, axis=0)
    scaled = upstream * norm_gain
    inner = (
        scaled
        - jnp.mean(scaled, axis=-1, keepdims=True)
        - normed * jnp.mean(scaled * normed, axis=-1, keepdims=True)
    )
    return (inner * inverse, gain_grad, shift_grad)


class Plan:
    def __init__(self, mesh_shape):
        self.n_f, self.n_s = mesh_shape["fsdp"], mesh_shape["seq"]
        self.ranks = self.n_s // 2
        self.blocks = 2 * self.n_f
        self.f = lax.axis_index("fsdp")
        self.s = lax.axis_index("seq")
        self.half = self.s // self.ranks
        self.rank = self.s % self.ranks
        self.core = self.s % 2
        self.own = self.f * 2 + self.half
        self.f_bits = [1 << k for k in range(self.n_f.bit_length() - 1)]
        self.z_bits = [1 << k for k in range(1, self.ranks.bit_length() - 1)]
        self.block_bits = [1] + [2 * b for b in self.f_bits]

    def swap(self, value, axis_name, bit):
        count = self.n_f if axis_name == "fsdp" else self.n_s
        return lax.ppermute(value, axis_name, [(i, i ^ bit) for i in range(count)])

    def swap_block(self, value, block_bit):
        if block_bit == 1:
            return self.swap(value, "seq", self.ranks)
        return self.swap(value, "fsdp", block_bit // 2)


def bit_of(index, bit):
    return (index // bit) % 2


def flip_bit(value, axis, bit):
    shape = value.shape
    size = shape[axis]
    split = value.reshape(shape[:axis] + (size // (2 * bit), 2, bit) + shape[axis + 1 :])
    low = lax.slice_in_dim(split, 0, 1, axis=axis + 1)
    high = lax.slice_in_dim(split, 1, 2, axis=axis + 1)
    return jnp.concatenate([high, low], axis=axis + 1).reshape(shape)


def xor_order(value, axis, own, bits):
    for bit in bits:
        value = jnp.where(bit_of(own, bit) == 1, flip_bit(value, axis, bit), value)
    return value


def features(plan, value):
    shape = value.shape
    view = value.reshape(shape[:-1] + (plan.blocks, shape[-1] // plan.blocks))
    return xor_order(view, len(shape) - 1, plan.own, plan.block_bits).reshape(shape)


def stack_by(mine, here, there, axis):
    return jnp.where(
        mine == 0, jnp.stack([here, there], axis=axis), jnp.stack([there, here], axis=axis)
    )


def choose(mine, value, axis):
    first = lax.index_in_dim(value, 0, axis, keepdims=False)
    second = lax.index_in_dim(value, 1, axis, keepdims=False)
    return jnp.where(mine == 0, first, second), jnp.where(mine == 0, second, first)


def spread(plan, value, order, column_axis=None):
    have = []
    for bit in order:
        there = plan.swap_block(value, bit)
        if column_axis is not None:
            there = flip_bit(there, column_axis + len(have), bit)
        place = sum(1 for b in have if b > bit)
        value = jnp.stack([value, there], axis=place)
        have.append(bit)
    return value.reshape((plan.blocks,) + value.shape[len(have) :])


def collect(plan, value, order, column_axis=None):
    rest = value.shape[1:]
    left = sorted(plan.block_bits, reverse=True)
    value = value.reshape((2,) * len(left) + rest)
    for bit in order:
        place = left.index(bit)
        here = lax.index_in_dim(value, 0, place, keepdims=False)
        there = plan.swap_block(lax.index_in_dim(value, 1, place, keepdims=False), bit)
        left.remove(bit)
        if column_axis is not None:
            there = flip_bit(there, column_axis - 1 + len(left), bit)
        value = here.astype(F32) + there.astype(F32)
        if left:
            value = value.astype(BF)
    return value


def group_gather(plan, value):
    for bit in plan.z_bits:
        value = jnp.concatenate([value, plan.swap(value, "seq", bit)], axis=0)
    return jnp.concatenate([value, plan.swap(value, "seq", 1)], axis=0)


def group_scatter(plan, left, right):
    tokens = left.shape[0] // 2
    other = mm(left[tokens:], right, BF)
    total = mm(left[:tokens], right) + plan.swap(other, "seq", 1).astype(F32)
    for bit in reversed(plan.z_bits):
        tokens = tokens // 2
        total = total[:tokens] + plan.swap(total[tokens:].astype(BF), "seq", bit).astype(F32)
    return total


def group_ids(plan, doc_ids):
    offsets = [0, plan.ranks]
    for bit in plan.z_bits + [1]:
        offsets = offsets + [o ^ bit for o in offsets]
    chunks = doc_ids.reshape(2, plan.n_s, -1)
    mine, _ = choose(plan.half, chunks, 0)
    return jnp.concatenate(
        [lax.dynamic_index_in_dim(mine, plan.s ^ o, 0, keepdims=False) for o in offsets]
    )


def gather_qkv(plan, parts, groups, order):
    rows, cols = parts[0].shape
    rank_bits = list(reversed([1] + plan.z_bits))
    value = jnp.stack([p.reshape(rows, groups, plan.ranks, -1) for p in parts], axis=1)
    lead = 0
    for bit in rank_bits:
        size = value.shape
        view = value.reshape(size[: lead + 3] + (2, size[lead + 3] // 2) + size[lead + 4 :])
        mine = bit_of(plan.s, bit)
        here, send = choose(mine, view, lead + 3)
        value = stack_by(mine, here, plan.swap(send, "seq", bit), lead)
        lead += 1
    value = value.reshape(plan.ranks * rows, 3 * cols // plan.ranks)
    value = spread(plan, value, order)
    return value.reshape(-1, value.shape[-1])


def scatter_qkv(plan, grad, groups, order):
    total_rows, width = grad.shape
    rows = total_rows // plan.blocks // plan.ranks
    value = collect(plan, grad.reshape(plan.blocks, -1, width), order)
    value = value.astype(BF)
    bits = [1] + plan.z_bits
    value = value.reshape((2,) * len(bits) + (rows, 3, groups, 1, width // 3 // groups))
    lead = len(bits)
    for bit in bits:
        lead -= 1
        mine = bit_of(plan.s, bit)
        here, send = choose(mine, value, lead)
        there = plan.swap(send, "seq", bit)
        value = stack_by(mine, here, there, lead + 3)
        size = value.shape
        value = value.reshape(
            size[: lead + 3] + (size[lead + 3] * size[lead + 4],) + size[lead + 5 :]
        )
    value = value.astype(F32)
    return [value[:, k].reshape(rows, -1) for k in range(3)]


def out_pairs(plan, turn):
    return [
        (h * plan.ranks + r, 2 * r + (h + turn) % 2) for h in range(2) for r in range(plan.ranks)
    ]


def gather_out(plan, part, groups):
    rows, cols = part.shape
    if groups == 1:
        whole = lax.all_gather(part, ("fsdp", "seq"), axis=0, tiled=True)
        size = whole.shape[0] // plan.ranks
        return features(plan, lax.dynamic_slice_in_dim(whole, plan.rank * size, size, 0))
    turns = [
        lax.ppermute(part, "seq", [(b, a) for a, b in out_pairs(plan, turn)]) for turn in range(2)
    ]
    value = stack_by(plan.half, turns[0], turns[1], 0).reshape(1, 2 * rows, cols)
    for bit in reversed(plan.f_bits):
        there = plan.swap(value, "fsdp", bit)
        mine = bit_of(plan.f, bit)
        value = stack_by(mine, value, there, 0)
        if bit != plan.f_bits[-1]:
            value = jnp.swapaxes(value, 0, 1)
        value = value.reshape((-1,) + value.shape[2:])
    return features(plan, value.reshape(-1, cols))


def scatter_out(plan, grad, groups):
    grad = features(plan, grad)
    total_rows, cols = grad.shape
    if groups == 1:
        whole = jnp.zeros((plan.ranks,) + grad.shape, grad.dtype)
        whole = lax.dynamic_update_slice_in_dim(whole, grad[None], plan.rank, 0)
        whole = whole.reshape(-1, cols).astype(F32)
        return lax.psum_scatter(whole, ("fsdp", "seq"), scatter_dimension=0, tiled=True)
    value = grad.reshape((2,) * len(plan.f_bits) + (total_rows // plan.n_f, cols))
    for bit in reversed(plan.f_bits):
        here, send = choose(bit_of(plan.f, bit), value, 0)
        there = plan.swap(send, "fsdp", bit)
        value = (here.astype(F32) + there.astype(F32)).astype(BF)
    halves = value.reshape(2, -1, cols)
    first, second = choose(plan.half, halves, 0)
    one = lax.ppermute(first, "seq", out_pairs(plan, 0))
    two = lax.ppermute(second, "seq", out_pairs(plan, 1))
    return one.astype(F32) + two.astype(F32)


def gather_fc_in(plan, part, order):
    rows, cols = part.shape
    value = part.reshape(rows, plan.blocks, plan.ranks // 2, 2, -1)
    here, send = choose(plan.core, value, 3)
    here = xor_order(here, 1, plan.own, plan.block_bits)
    send = xor_order(send, 1, plan.own, plan.block_bits)
    value = stack_by(plan.core, here, plan.swap(send, "seq", 1), 0)
    value = value.reshape(2 * rows, plan.blocks, cols // plan.blocks // 2)
    for bit in plan.z_bits:
        there = plan.swap(value, "seq", bit)
        value = stack_by(bit_of(plan.s, bit), value, there, 0)
        value = value.reshape((-1,) + value.shape[2:])
    value = spread(plan, value, order, column_axis=1)
    return value.reshape(-1, cols // 2)


def scatter_fc_in(plan, grad, order):
    total_rows, width = grad.shape
    value = grad.reshape(plan.blocks, total_rows // plan.blocks, plan.blocks, -1)
    value = collect(plan, value, order, column_axis=2)
    for bit in reversed(plan.z_bits):
        value = value.astype(BF)
        value = value.reshape((2, value.shape[0] // 2) + value.shape[1:])
        here, send = choose(bit_of(plan.s, bit), value, 0)
        value = here.astype(F32) + plan.swap(send, "seq", bit).astype(F32)
    value = xor_order(value, 1, plan.own, plan.block_bits).astype(BF)
    value = value.reshape((2, value.shape[0] // 2) + value.shape[1:])
    here, send = choose(plan.core, value, 0)
    there = plan.swap(send, "seq", 1)
    rows = here.shape[0]
    parts = (rows, plan.blocks, plan.ranks // 2, -1)
    value = stack_by(plan.core, here.reshape(parts), there.reshape(parts), 3)
    return value.reshape(rows, 2 * width).astype(F32)


def gather_fc_out(plan, part, order):
    rows, cols = part.shape
    value = part.reshape(rows, plan.blocks, cols // plan.blocks)
    value = xor_order(value, 1, plan.own, plan.block_bits)
    for bit in plan.z_bits:
        there = plan.swap(value, "seq", bit)
        value = stack_by(bit_of(plan.s, bit), value, there, 0)
        value = value.reshape((-1,) + value.shape[2:])
    value = spread(plan, value, order, column_axis=1)
    return value.reshape(-1, cols)


def scatter_fc_out(plan, grad, order):
    total_rows, cols = grad.shape
    value = grad.reshape(plan.blocks, total_rows // plan.blocks, plan.blocks, -1)
    value = collect(plan, value, order, column_axis=2)
    for bit in reversed(plan.z_bits):
        value = value.astype(BF)
        value = value.reshape((2, value.shape[0] // 2) + value.shape[1:])
        here, send = choose(bit_of(plan.s, bit), value, 0)
        value = here.astype(F32) + plan.swap(send, "seq", bit).astype(F32)
    value = xor_order(value, 1, plan.own, plan.block_bits)
    return value.reshape(value.shape[0], cols)


def sum_vectors(plan, vectors):
    count, width = vectors.shape
    bits = [("fsdp", b) for b in plan.f_bits] + [("seq", b) for b in [1] + plan.z_bits + [plan.ranks]]
    order = [("fsdp", b) for b in reversed(plan.f_bits)]
    order += [("seq", b) for b in reversed([1] + plan.z_bits + [plan.ranks])]
    value = jnp.moveaxis(vectors.reshape((count,) + (2,) * len(bits) + (-1,)), 0, -2)
    for axis_name, bit in order:
        index = plan.f if axis_name == "fsdp" else plan.s
        here, send = choose(bit_of(index, bit), value, 0)
        value = here + plan.swap(send, axis_name, bit)
    return value


def core_pair(plan, value):
    return jnp.concatenate([value, plan.swap(value, "seq", 1)], axis=0)


def core_sum(plan, own, other):
    return own + plan.swap(other, "seq", 1).astype(F32)


def layer_forward(plan, hidden, weights, gains, ids, head_dim):
    w_qkv, w_out, w_in_ff, w_out_ff = weights
    gain_attn, shift_attn, gain_ffn, shift_ffn = gains
    tokens = hidden.shape[0]
    x_all = group_gather(plan, hidden.astype(BF))
    qkv = mm(x_all, w_qkv)
    width = qkv.shape[1] // 3
    scale = jnp.where(jnp.arange(3 * width) < width, head_dim**-0.5, 1.0).astype(F32)
    qkv = (qkv.astype(BF).astype(F32) * scale[None]).astype(BF)
    attended = attn_forward(qkv, ids, head_dim)
    branch = group_scatter(plan, attended, w_out)
    middle, normed_attn, inverse_attn = norm_forward(hidden + branch, gain_attn, shift_attn)
    mid_all = core_pair(plan, middle.astype(BF))
    before = mm(mid_all, w_in_ff)
    bell = 0.5 * (1.0 + lax.erf(before * inv_root_two))
    active = (before * bell).astype(BF)
    slope = (bell + before * jnp.exp(-0.5 * before * before) * inv_root_two_pi).astype(BF)
    other = mm(active[tokens:], w_out_ff, BF)
    ff_branch = core_sum(plan, mm(active[:tokens], w_out_ff), other)
    result, normed_ffn, inverse_ffn = norm_forward(middle + ff_branch, gain_ffn, shift_ffn)
    saved = (
        x_all, qkv, attended, normed_attn, inverse_attn, mid_all, active, slope,
        normed_ffn, inverse_ffn,
    )
    return result, saved


def layer_backward(plan, upstream, saved, weights, gains, ids, head_dim, groups, order_a, order_b):
    w_qkv, w_out, w_in_ff, w_out_ff = weights
    gain_attn, _, gain_ffn, _ = gains
    (
        x_all, qkv, attended, normed_attn, inverse_attn, mid_all, active, slope,
        normed_ffn, inverse_ffn,
    ) = saved
    tokens = upstream.shape[0]
    sum_grad, gain_ffn_grad, shift_ffn_grad = norm_backward(
        upstream, normed_ffn, inverse_ffn, gain_ffn
    )
    ff_all = core_pair(plan, sum_grad.astype(BF))
    before_grad = (mm_t(ff_all, w_out_ff) * slope.astype(F32)).astype(BF)
    other = mm_t(before_grad[tokens:], w_in_ff, BF)
    middle_grad = sum_grad + core_sum(plan, mm_t(before_grad[:tokens], w_in_ff), other)
    fc_out_grad = scatter_fc_out(plan, mm_outer(active, ff_all, BF), order_b)
    fc_in_grad = scatter_fc_in(plan, mm_outer(mid_all, before_grad, BF), order_a)
    attn_sum_grad, gain_attn_grad, shift_attn_grad = norm_backward(
        middle_grad, normed_attn, inverse_attn, gain_attn
    )
    branch_all = group_gather(plan, attn_sum_grad.astype(BF))
    attended_grad = mm_t(branch_all, w_out, BF)
    out_grad = scatter_out(plan, mm_outer(attended, branch_all, BF), groups)
    dqkv = attn_backward(qkv, attended_grad, ids, head_dim)
    input_grad = attn_sum_grad + group_scatter(plan, dqkv, w_qkv.T)
    qkv_grads = scatter_qkv(plan, mm_outer(x_all, dqkv, BF), groups, order_b)
    vector_grads = (gain_attn_grad, shift_attn_grad, gain_ffn_grad, shift_ffn_grad)
    return input_grad, (*qkv_grads, out_grad, fc_in_grad, fc_out_grad), vector_grads


def local(
    mesh_shape,
    inputs,
    segment_ids,
    query_weight,
    key_weight,
    value_weight,
    out_weight,
    fc_in_weight,
    fc_out_weight,
    attn_gain,
    attn_shift,
    ffn_gain,
    ffn_shift,
    cotangent,
):
    plan = Plan(mesh_shape)
    layers, _, width = query_weight.shape
    head_dim = width // HEADS
    groups = plan.n_f if (width // (plan.n_f * plan.ranks)) % head_dim == 0 else 1
    f_blocks = [2 * b for b in plan.f_bits]
    up, down = [1] + f_blocks, [1] + f_blocks[::-1]

    def to_halves(value):
        mine, other = choose(plan.half, value, 0)
        there = plan.swap(other, "seq", plan.ranks)
        return features(plan, jnp.concatenate([mine, there], axis=0))

    def from_halves(value):
        value = features(plan, value)
        size = value.shape[0] // 2
        mine, other = value[:size], value[size:]
        there = plan.swap(other.astype(BF), "seq", plan.ranks).astype(F32)
        return stack_by(plan.half, mine, there, 0)

    def fetch(layer):
        parts = [w[layer] for w in (query_weight, key_weight, value_weight)]
        return (
            gather_qkv(plan, parts, groups, up),
            gather_out(plan, out_weight[layer], groups),
            gather_fc_in(plan, fc_in_weight[layer], up),
            gather_fc_out(plan, fc_out_weight[layer], down),
        )

    hidden = to_halves(inputs).astype(F32)
    doc_ids = lax.all_gather(segment_ids, "seq", axis=1, tiled=True)
    ids = group_ids(plan, doc_ids)
    vectors = jnp.stack([attn_gain, attn_shift, ffn_gain, ffn_shift], axis=1)
    vectors = lax.all_gather(vectors.reshape(1, -1), ("fsdp", "seq"), axis=0, tiled=True)
    vectors = jnp.transpose(vectors.reshape(-1, layers, 4, attn_gain.shape[1]), (1, 2, 0, 3))
    vectors = features(plan, vectors.reshape(layers, 4, width)).astype(F32)

    weights = [fetch(layer) for layer in range(layers)]
    gains = [tuple(vectors[layer, k] for k in range(4)) for layer in range(layers)]
    upstream = to_halves(cotangent).astype(F32)
    records = []
    for layer in range(layers):
        hidden, saved = layer_forward(plan, hidden, weights[layer], gains[layer], ids, head_dim)
        records.append(saved)
    outputs = from_halves(hidden)
    grads, vector_grads = [None] * layers, [None] * layers
    for layer in reversed(range(layers)):
        upstream, grads[layer], vector_grads[layer] = layer_backward(
            plan, upstream, records[layer], weights[layer], gains[layer], ids, head_dim,
            groups, up[::-1], down[::-1],
        )
    input_grad = from_halves(upstream)
    summed = jnp.stack([v for member in vector_grads for v in member])
    summed = sum_vectors(plan, features(plan, summed)).reshape(layers, 4, -1)
    merged = [jnp.stack([g[k] for g in grads]) for k in range(6)]
    return (outputs, input_grad, *merged, *(summed[:, k] for k in range(4)))


def solution(mesh):
    tokens = P("fsdp", "seq", None)
    matrix = P(None, ("fsdp", "seq"), None)
    vector = P(None, ("fsdp", "seq"))
    return jax.shard_map(
        functools.partial(local, dict(mesh.shape)),
        mesh=mesh,
        in_specs=(tokens, P("fsdp", "seq"), *[matrix] * 6, *[vector] * 4, tokens),
        out_specs=(tokens, tokens, *[matrix] * 6, *[vector] * 4),
        check_vma=False,
    )
```

```python
import functools

import jax
import jax.numpy as jnp
from jax import lax
from jax.experimental import pallas as pl
from jax.experimental.pallas import tpu as pltpu
from jax.sharding import PartitionSpec as P

HEADS = 16
NEG_FILL = -1e30
NORM_EPS = 1e-05
inv_root_two = 0.7071067811865476
inv_root_two_pi = 0.3989422804014327
BF = jnp.bfloat16
F32 = jnp.float32
ALL = ("fsdp", "seq")
PARAMS = pltpu.CompilerParams(vmem_limit_bytes=56 * 1024 * 1024)


def mm(a, b, out=F32):
    return lax.dot_general(a, b, (((1,), (0,)), ((), ())), preferred_element_type=F32).astype(out)


def mm_t(a, b, out=F32):
    return lax.dot_general(a, b, (((1,), (1,)), ((), ())), preferred_element_type=F32).astype(out)


def mm_outer(a, b, out=F32):
    return lax.dot_general(a, b, (((0,), (0,)), ((), ())), preferred_element_type=F32).astype(out)


def struct(shape, dtype):
    return jax.ShapeDtypeStruct(shape, dtype)


def whole(shape):
    return pl.BlockSpec(shape, lambda *_: (0,) * len(shape))


def cost(flops, bytes_accessed, exps=0):
    return pl.CostEstimate(flops=flops, bytes_accessed=bytes_accessed, transcendentals=exps)


class Plan:
    def __init__(self, mesh_shape, width, hidden_units):
        self.n_f, self.n_s = mesh_shape["fsdp"], mesh_shape["seq"]
        self.n = self.n_f * self.n_s
        self.ranks = self.n_s // 2
        self.f = lax.axis_index("fsdp")
        self.s = lax.axis_index("seq")
        self.half = self.s // self.ranks
        self.rank = self.s % self.ranks
        self.core = self.s % 2
        self.f_bits = [1 << k for k in range(self.n_f.bit_length() - 1)]
        self.z_bits = [1 << k for k in range(1, self.ranks.bit_length() - 1)]
        self.hi, self.lo = self.f_bits[-1], self.f_bits[-2]
        self.f_hi, self.f_lo = bit_of(self.f, self.hi), bit_of(self.f, self.lo)
        self.fast = (
            self.n_f == 4
            and self.n_s == 8
            and (width // self.n) % 32 == 0
            and (hidden_units // self.n) % 128 == 0
        )

    def swap(self, value, axis_name, bit):
        count = self.n_f if axis_name == "fsdp" else self.n_s
        return lax.ppermute(value, axis_name, [(i, i ^ bit) for i in range(count)])

    def scalars(self):
        return jnp.stack([self.core, self.f_hi, self.f_lo, self.f * 2 + self.half, self.rank]).astype(
            jnp.int32
        )


def bit_of(index, bit):
    return (index // bit) % 2


def stack_by(mine, here, there, axis):
    return jnp.where(
        mine == 0, jnp.stack([here, there], axis=axis), jnp.stack([there, here], axis=axis)
    )


def choose(mine, value, axis):
    first = lax.index_in_dim(value, 0, axis, keepdims=False)
    second = lax.index_in_dim(value, 1, axis, keepdims=False)
    return jnp.where(mine == 0, first, second), jnp.where(mine == 0, second, first)


def group_pieces(plan, value):
    pieces = [value]
    for bit in plan.z_bits:
        pieces = pieces + [plan.swap(p, "seq", bit) for p in pieces]
    return pieces + [plan.swap(p, "seq", 1) for p in pieces]


def group_sum(plan, keep, send):
    parts = [keep, plan.swap(send, "seq", 1)]
    size = keep.shape[0]
    for bit in reversed(plan.z_bits):
        size = size // 2
        out = sum(p[size : 2 * size].astype(F32) for p in parts).astype(BF)
        parts = parts + [plan.swap(out, "seq", bit)]
    return parts


def add_parts(parts, rows):
    return sum(p[:rows].astype(F32) for p in parts)


class Sum:
    def __init__(self, parts):
        self.parts = list(parts)

    def step(self, plan, axis_name, bit, axis):
        mine = bit_of(plan.f if axis_name == "fsdp" else plan.s, bit)
        pairs = [choose(mine, p, axis) for p in self.parts]
        send = sum(b.astype(F32) for _, b in pairs).astype(BF)
        self.parts = [a for a, _ in pairs] + [plan.swap(send, axis_name, bit)]
        return self

    def total(self):
        return sum(p.astype(F32) for p in self.parts)

    def reshape(self, *shape):
        return Sum([p.reshape(shape) for p in self.parts])


def norm_rows(summed):
    center = jnp.mean(summed, axis=-1, keepdims=True)
    offset = summed - center
    spread = jnp.mean(offset * offset, axis=-1, keepdims=True)
    inverse = lax.rsqrt(spread + NORM_EPS)
    return offset * inverse, inverse


def norm_backward_kernel(count, *refs):
    parts, (normed_ref, inverse_ref, gain_ref) = refs[:count], refs[count : count + 3]
    out_ref, low_ref, gain_grad_ref, shift_grad_ref = refs[count + 3 :]
    upstream = parts[0][...].astype(F32)
    for part in parts[1:]:
        upstream = upstream + part[...].astype(F32)
    normed = normed_ref[...]
    gain_grad_ref[...] = jnp.sum(upstream * normed, axis=0, keepdims=True)
    shift_grad_ref[...] = jnp.sum(upstream, axis=0, keepdims=True)
    scaled = upstream * gain_ref[...]
    inner = (
        scaled
        - jnp.mean(scaled, axis=-1, keepdims=True)
        - normed * jnp.mean(scaled * normed, axis=-1, keepdims=True)
    )
    result = inner * inverse_ref[...]
    out_ref[...] = result
    low_ref[...] = result.astype(BF)


def norm_backward(parts, normed, inverse, gain):
    rows, width = normed.shape
    return pl.pallas_call(
        functools.partial(norm_backward_kernel, len(parts)),
        grid=(1,),
        in_specs=[whole((rows, width))] * (len(parts) + 1) + [whole((rows, 1)), whole((1, width))],
        out_specs=[whole((rows, width))] * 2 + [whole((1, width))] * 2,
        out_shape=[
            struct((rows, width), F32), struct((rows, width), BF),
            struct((1, width), F32), struct((1, width), F32),
        ],
        compiler_params=PARAMS,
        cost_estimate=cost(10 * rows * width, 20 * rows * width),
    )(*parts, normed, inverse, gain)


def pick_head(lanes, head, head_dim):
    return (lanes >= head * head_dim) & (lanes < (head + 1) * head_dim)


def attn_forward_kernel(head_dim, count, *refs):
    pieces = refs[:count]
    w_qkv_ref, w_out_ref, ids_q_ref, ids_k_ref = refs[count : count + 4]
    qkv_ref, att_ref, keep_ref, send_ref = refs[count + 4 :]
    step = pl.program_id(0)
    rows, width = att_ref.shape

    @pl.when(step == 0)
    def _():
        w_qkv = w_qkv_ref[...]
        for index, piece in enumerate(pieces):
            qkv = mm(piece[...], w_qkv).astype(BF)
            part = pl.ds(index * rows, rows)
            qkv_ref[part, :width] = (qkv[:, :width].astype(F32) * head_dim**-0.5).astype(BF)
            qkv_ref[part, width:] = qkv[:, width:]

    queries = qkv_ref[pl.ds(pl.multiple_of(step * rows, rows), rows), :width]
    keys, values = qkv_ref[:, width : 2 * width], qkv_ref[:, 2 * width :]
    lanes = lax.broadcasted_iota(jnp.int32, (1, width), 1)
    allowed = ids_q_ref[...] == ids_k_ref[...]
    total = jnp.zeros((rows, width), F32)
    for head in range(width // head_dim):
        here = pick_head(lanes, head, head_dim)
        scores = mm_t(jnp.where(here, queries, jnp.zeros_like(queries)), keys)
        scores = jnp.where(allowed, scores, NEG_FILL)
        weights = jnp.exp(scores - jnp.max(scores, axis=1, keepdims=True))
        norm = 1.0 / jnp.sum(weights, axis=1, keepdims=True)
        total = jnp.where(here, mm(weights.astype(BF), values) * norm, total)
    attended = total.astype(BF)
    att_ref[...] = attended
    branch = mm(attended, w_out_ref[...])

    @pl.when(step < count // 2)
    def _():
        keep_ref[...] = branch

    @pl.when(step >= count // 2)
    def _():
        send_ref[...] = branch.astype(BF)


def attn_forward(pieces, w_qkv, w_out, ids, head_dim):
    count = len(pieces)
    rows, features = pieces[0].shape
    tokens, width = count * rows, w_out.shape[0]
    half = count // 2
    heads = width // head_dim
    return pl.pallas_call(
        functools.partial(attn_forward_kernel, head_dim, count),
        grid=(count,),
        in_specs=[whole((rows, features))] * count
        + [
            whole(w_qkv.shape),
            whole(w_out.shape),
            pl.BlockSpec((rows, 1), lambda i: (i, 0)),
            whole((1, tokens)),
        ],
        out_specs=[
            whole((tokens, 3 * width)),
            pl.BlockSpec((rows, width), lambda i: (i, 0)),
            pl.BlockSpec((rows, features), lambda i: (jnp.minimum(i, half - 1), 0)),
            pl.BlockSpec((rows, features), lambda i: (jnp.maximum(i - half, 0), 0)),
        ],
        out_shape=[
            struct((tokens, 3 * width), BF),
            struct((tokens, width), BF),
            struct((half * rows, features), F32),
            struct((half * rows, features), BF),
        ],
        compiler_params=PARAMS,
        cost_estimate=cost(
            4 * tokens * tokens * width * heads + 8 * tokens * width * features,
            6 * tokens * features,
            tokens * tokens * heads,
        ),
    )(*pieces, w_qkv, w_out, ids.reshape(tokens, 1), ids.reshape(1, tokens))


def attn_backward_kernel(head_dim, count, *refs):
    pieces = refs[:count]
    qkv_ref, w_qkv_ref, w_out_ref, ids_q_ref, ids_k_ref = refs[count : count + 5]
    dqkv_ref, keep_ref, send_ref, grad_ref, dk_ref, dv_ref = refs[count + 5 :]
    step = pl.program_id(0)
    rows = pieces[0].shape[0]
    width = grad_ref.shape[1]

    @pl.when(step == 0)
    def _():
        w_out = w_out_ref[...]
        for index, piece in enumerate(pieces):
            grad_ref[pl.ds(index * rows, rows), :] = mm_t(piece[...], w_out, BF)
        dk_ref[...] = jnp.zeros_like(dk_ref)
        dv_ref[...] = jnp.zeros_like(dv_ref)

    place = pl.ds(pl.multiple_of(step * rows, rows), rows)
    queries, grads = qkv_ref[place, :width], grad_ref[place, :]
    keys, values = qkv_ref[:, width : 2 * width], qkv_ref[:, 2 * width :]
    lanes = lax.broadcasted_iota(jnp.int32, (1, width), 1)
    allowed = ids_q_ref[...] == ids_k_ref[...]
    dq = jnp.zeros((rows, width), F32)
    for head in range(width // head_dim):
        here = pick_head(lanes, head, head_dim)
        q_head = jnp.where(here, queries, jnp.zeros_like(queries))
        g_head = jnp.where(here, grads, jnp.zeros_like(grads))
        scores = mm_t(q_head, keys)
        scores = jnp.where(allowed, scores, NEG_FILL)
        weights = jnp.exp(scores - jnp.max(scores, axis=1, keepdims=True))
        probs = weights * (1.0 / jnp.sum(weights, axis=1, keepdims=True))
        prob_grad = mm_t(g_head, values)
        product = probs * prob_grad
        delta = jnp.sum(product, axis=1, keepdims=True)
        score_grad = (product - probs * delta).astype(BF)
        dq = jnp.where(here, mm(score_grad, keys), dq)
        dk_ref[...] += mm_outer(score_grad, q_head)
        dv_ref[...] += mm_outer(probs.astype(BF), g_head)
    dqkv_ref[place, :width] = (dq * head_dim**-0.5).astype(BF)

    @pl.when(step == count - 1)
    def _():
        dqkv_ref[:, width : 2 * width] = dk_ref[...].astype(BF)
        dqkv_ref[:, 2 * width :] = dv_ref[...].astype(BF)
        w_qkv = w_qkv_ref[...]
        half = count // 2
        for index in range(count):
            part = mm_t(dqkv_ref[pl.ds(index * rows, rows), :], w_qkv)
            if index < half:
                keep_ref[pl.ds(index * rows, rows), :] = part
            else:
                send_ref[pl.ds((index - half) * rows, rows), :] = part.astype(BF)


def attn_backward(pieces, qkv, w_qkv, w_out, ids, head_dim):
    count = len(pieces)
    rows, features = pieces[0].shape
    tokens, width = count * rows, w_out.shape[0]
    heads = width // head_dim
    half = tokens // 2
    return pl.pallas_call(
        functools.partial(attn_backward_kernel, head_dim, count),
        grid=(count,),
        in_specs=[whole((rows, features))] * count
        + [
            whole(qkv.shape),
            whole(w_qkv.shape),
            whole(w_out.shape),
            pl.BlockSpec((rows, 1), lambda i: (i, 0)),
            whole((1, tokens)),
        ],
        out_specs=[
            whole((tokens, 3 * width)), whole((half, features)), whole((half, features)),
        ],
        out_shape=[
            struct((tokens, 3 * width), BF), struct((half, features), F32),
            struct((half, features), BF),
        ],
        scratch_shapes=[
            pltpu.VMEM((tokens, width), BF),
            pltpu.VMEM((tokens, width), F32),
            pltpu.VMEM((tokens, width), F32),
        ],
        compiler_params=PARAMS,
        cost_estimate=cost(
            10 * tokens * tokens * width * heads + 8 * tokens * width * features,
            8 * tokens * features,
            tokens * tokens * heads,
        ),
    )(*pieces, qkv, w_qkv, w_out, ids.reshape(tokens, 1), ids.reshape(1, tokens))


def attn_weights_kernel(count, place_ref, *refs):
    x_refs, g_refs = refs[:count], refs[count : 2 * count]
    dqkv_ref, att_ref = refs[2 * count : 2 * count + 2]
    a_send, a_keep, b_send, b_keep, out_ref = refs[2 * count + 2 :]
    block = pl.program_id(0)
    rows = x_refs[0].shape[0]
    width = att_ref.shape[1]
    height = a_send.shape[1] // 2
    small = out_ref.shape[0] // pl.num_programs(0)

    @pl.when(block == 0)
    def _():
        total = None
        for index in range(count):
            part = mm_outer(att_ref[pl.ds(index * rows, rows), :], g_refs[index][...])
            total = part if total is None else total + part
        out_ref[...] = total.astype(BF)

    lanes = pl.ds(pl.multiple_of(block * height, height), height)
    grad = None
    for index in range(count):
        part = mm_outer(x_refs[index][:, lanes], dqkv_ref[pl.ds(index * rows, rows), :])
        grad = part if grad is None else grad + part
    grad = grad.astype(BF)
    hi, lo, low = block // 4, (block // 2) % 2, block % 2

    def put_a(ref):
        ref[lo * 2 + low, :height, :] = grad[:, :width]
        ref[lo * 2 + low, height:, :] = grad[:, width : 2 * width]

    def put_b(ref):
        ref[hi * 2 + low, :height, :] = grad[:, 2 * width :]
        part = out_ref[pl.ds(pl.multiple_of(block * small, small), small), :]
        for piece in range(height // small):
            start = height + piece * small
            ref[hi * 2 + low, start : start + small, :] = part[:, piece * width : (piece + 1) * width]

    pl.when(hi != place_ref[1])(lambda: put_a(a_send))
    pl.when(hi == place_ref[1])(lambda: put_a(a_keep))
    pl.when(lo != place_ref[2])(lambda: put_b(b_send))
    pl.when(lo == place_ref[2])(lambda: put_b(b_keep))


def attn_weights(places, x_pieces, g_pieces, dqkv, att):
    count = len(x_pieces)
    rows, features = x_pieces[0].shape
    tokens, width = att.shape
    part = (4, 2 * features // 8, width)
    return pl.pallas_call(
        functools.partial(attn_weights_kernel, count),
        grid_spec=pltpu.PrefetchScalarGridSpec(
            num_scalar_prefetch=1,
            grid=(8,),
            in_specs=[whole((rows, features))] * (2 * count) + [whole(dqkv.shape), whole(att.shape)],
            out_specs=[whole(part)] * 4,
            scratch_shapes=[pltpu.VMEM((width, features), BF)],
        ),
        out_shape=[struct(part, BF)] * 4,
        compiler_params=PARAMS,
        cost_estimate=cost(8 * tokens * width * features, 8 * tokens * features),
    )(places, *x_pieces, *g_pieces, dqkv, att)


def assemble_kernel(place_ref, a_own, a_other, b_own, b_other, qkv_ref, out_ref):
    own, rank = place_ref[3], place_ref[4]
    height, width = a_own.shape[1] // 8, a_own.shape[2]
    ranks = 4
    for block in range(8):
        a_ref = a_own if block < 4 else a_other
        b_ref = b_own if block < 4 else b_other
        b_block = (block % 4) // 2 * 4 + block // 4 * 2 + block % 2
        for inner in range(4):
            rank_there = rank ^ ((inner // 2) + (inner % 2) * 2)
            start = ((own ^ block) * ranks + rank_there) * height
            place = pl.ds(pl.multiple_of(start, height), height)
            qkv_ref[place, :width] = a_ref[block % 4, inner * height : (inner + 1) * height, :]
            first = (4 + inner) * height
            qkv_ref[place, width : 2 * width] = a_ref[block % 4, first : first + height, :]
            start = ((own ^ b_block) * ranks + rank_there) * height
            place = pl.ds(pl.multiple_of(start, height), height)
            qkv_ref[place, 2 * width :] = b_ref[block % 4, inner * height : (inner + 1) * height, :]
            place = pl.ds(pl.multiple_of((own ^ b_block) * height, height), height)
            out_ref[place, inner * width : (inner + 1) * width] = b_ref[
                block % 4, first : first + height, :
            ]


def assemble(places, a_own, a_other, b_own, b_other):
    _, high, width = a_own.shape
    features = 4 * high
    return pl.pallas_call(
        assemble_kernel,
        grid_spec=pltpu.PrefetchScalarGridSpec(
            num_scalar_prefetch=1,
            grid=(1,),
            in_specs=[whole(a_own.shape)] * 4,
            out_specs=[whole((features, 3 * width)), whole((width, features))],
        ),
        out_shape=[struct((features, 3 * width), BF), struct((width, features), BF)],
        compiler_params=PARAMS,
        cost_estimate=cost(0, 16 * features * width),
    )(places, a_own, a_other, b_own, b_other)


def spread_pairs(plan):
    pairs = []
    for shard in range(plan.n):
        rank, block = shard // (2 * plan.n_f), shard % (2 * plan.n_f)
        pairs.append((shard, block // 2 * plan.n_s + block % 2 * plan.ranks + rank))
    return pairs


def gather_attention(plan, places, matrices):
    query, key, value, out = matrices
    layers, rows, cols = query.shape
    if not plan.fast:
        size = cols // plan.ranks
        result = []
        for layer in range(layers):
            full = [lax.all_gather(m[layer], ALL, axis=0, tiled=True) for m in matrices]
            qkv = [lax.dynamic_slice_in_dim(m, plan.rank * size, size, 1) for m in full[:3]]
            w_out = lax.dynamic_slice_in_dim(full[3], plan.rank * size, size, 0)
            result.append((jnp.concatenate(qkv, axis=1), w_out))
        return result
    half = cols // 2
    stacked = jnp.stack([query, key, value], axis=1)
    upper = bit_of(plan.s, 2) == 1
    send = jnp.where(upper, stacked[..., :half], stacked[..., half:])
    here = jnp.where(upper, stacked[..., half:], stacked[..., :half])
    there = plan.swap(send, "seq", 2)
    both = jnp.stack([here, there], axis=2)
    quarter = half // 2
    upper = plan.core == 1
    send = jnp.where(upper, both[..., :quarter], both[..., quarter:])
    here = jnp.where(upper, both[..., quarter:], both[..., :quarter])
    there = plan.swap(send, "seq", 1)
    out = lax.ppermute(out, ALL, spread_pairs(plan))
    result = []
    for layer in range(layers):
        qkv = jnp.stack([here[layer], there[layer]], axis=1)
        w_out = jnp.stack([out[layer, :, k * quarter : (k + 1) * quarter] for k in range(4)])
        bundle = jnp.concatenate([qkv.reshape(-1, quarter), w_out.reshape(-1, quarter)], axis=0)
        other = plan.swap(bundle, "seq", plan.ranks)
        size = bundle.shape[0] // 2
        part_a = jnp.stack([bundle[:size], other[:size]])
        part_b = jnp.stack([bundle[size:], other[size:]])
        part_a = jnp.concatenate([part_a, plan.swap(part_a, "fsdp", plan.lo)], axis=0)
        part_b = jnp.concatenate([part_b, plan.swap(part_b, "fsdp", plan.hi)], axis=0)
        other_a = plan.swap(part_a, "fsdp", plan.hi)
        other_b = plan.swap(part_b, "fsdp", plan.lo)
        result.append(assemble(places, part_a, other_a, part_b, other_b))
    return result


def scatter_attention(plan, places, x_pieces, g_pieces, dqkv, att):
    if not plan.fast:
        w_qkv = sum(mm_outer(x, d) for x, d in zip(x_pieces, jnp.split(dqkv, len(x_pieces))))
        w_out = sum(mm_outer(a, g) for a, g in zip(jnp.split(att, len(g_pieces)), g_pieces))
        width, features = w_out.shape
        grads = []
        for grad, axis in [(g, 1) for g in jnp.split(w_qkv, 3, axis=1)] + [(w_out, 0)]:
            full = jnp.zeros((features, features), F32)
            full = lax.dynamic_update_slice_in_dim(full, grad, plan.rank * width, axis)
            grads.append(lax.psum_scatter(full, ALL, scatter_dimension=0, tiled=True))
        return grads
    a_send, a_keep, b_send, b_keep = attn_weights(places, x_pieces, g_pieces, dqkv, att)
    high, width = a_send.shape[1:]
    part_a = Sum([a_keep, plan.swap(a_send, "fsdp", plan.hi)]).reshape(2, 2, high, width)
    part_b = Sum([b_keep, plan.swap(b_send, "fsdp", plan.lo)]).reshape(2, 2, high, width)
    part_a.step(plan, "fsdp", plan.lo, 0)
    part_b.step(plan, "fsdp", plan.hi, 0)
    part_a.step(plan, "seq", plan.ranks, 0)
    part_b.step(plan, "seq", plan.ranks, 0)
    part_a = part_a.total().astype(BF).reshape(2, 2, 2, high // 8, width)
    part_b = part_b.total().astype(BF).reshape(2, 4, high // 8, width)
    out = jnp.concatenate([part_b[1, k] for k in range(4)], axis=1)
    out = lax.ppermute(out, ALL, [(b, a) for a, b in spread_pairs(plan)])
    qkv = jnp.concatenate([part_a, part_b[:1].reshape(1, 2, 2, high // 8, width)], axis=0)
    here, send = choose(bit_of(plan.s, 2), qkv, 1)
    qkv = stack_by(bit_of(plan.s, 2), here, plan.swap(send, "seq", 2), 0)
    here, send = choose(plan.core, qkv, 2)
    qkv = stack_by(plan.core, here, plan.swap(send, "seq", 1), 1)
    qkv = jnp.concatenate([qkv[0, 0], qkv[0, 1], qkv[1, 0], qkv[1, 1]], axis=2).astype(F32)
    return [qkv[0], qkv[1], qkv[2], out.astype(F32)]


class Packed:
    def __init__(self, plan, fc_in, fc_out):
        rows, units = fc_in.shape
        width = fc_out.shape[1]
        own = units // plan.n
        split = fc_in.reshape(rows, plan.n // 2, 2, own)
        split = jnp.transpose(split, (2, 0, 1, 3)).reshape(2, rows, 2, units // 4)
        split = jnp.transpose(split, (0, 2, 1, 3))
        self.width, self.units = rows * plan.n, units
        self.fast = plan.fast and units // 4 == width
        if self.fast:
            flat = jnp.concatenate([split.reshape(4 * rows, width), fc_out], axis=0)
            full = lax.all_gather(flat, ALL, axis=0, tiled=True)
            self.fc_in = full.reshape(plan.n, 8, rows, width)
            self.fc_out = full.reshape(plan.n // 2, 2, 8, rows, width)
        else:
            full = lax.all_gather(split, ALL, axis=2, tiled=True)
            self.fc_in = full.reshape(1, 4, self.width, units // 4)
            full = lax.all_gather(fc_out, ALL, axis=0, tiled=True)
            full = full.reshape(plan.n // 2, 2, own, width)
            self.fc_out = jnp.transpose(full, (1, 0, 2, 3)).reshape(2, units // 2, width)

    def in_spec(self, parts, index):
        shape = self.fc_in.shape

        def place(step, places):
            core, upper, part = index(step, places)
            return (0, core * 2 + upper, 0, part)

        return pl.BlockSpec((shape[0], 1, shape[2], shape[3] // parts), place)

    def out_spec(self, parts, index):
        shape = self.fc_out.shape

        def place(step, places):
            core, upper, part = index(step, places)
            where = upper * parts + part
            return (where, core, 1, 0, 0) if self.fast else (core, where, 0)

        if self.fast:
            return pl.BlockSpec((shape[0] // 2 // parts, 1, 4, shape[3], shape[4]), place)
        return pl.BlockSpec((1, shape[1] // 2 // parts, shape[2]), place)


def ffn_forward_kernel(count, place_ref, *refs):
    parts = refs[:count]
    vectors_ref, w_in_ref, w_out_ref = refs[count : count + 3]
    (
        result_ref, low_ref, mid_low_ref, normed_attn_ref, inverse_attn_ref, normed_ffn_ref,
        inverse_ffn_ref, send_ref, keep_ref, mid_ref, total_ref,
    ) = refs[count + 3 :]
    step = pl.program_id(0)
    width = mid_ref.shape[1]
    chunk = send_ref.shape[2]

    @pl.when(step == 0)
    def _():
        summed = parts[0][...].astype(F32)
        for part in parts[1:]:
            summed = summed + part[...].astype(F32)
        normed, inverse = norm_rows(summed)
        normed_attn_ref[...] = normed
        inverse_attn_ref[...] = inverse
        middle = normed * vectors_ref[0:1, :] + vectors_ref[1:2, :]
        mid_ref[...] = middle
        mid_low_ref[...] = middle.astype(BF)
        total_ref[...] = middle

    before = mm(mid_low_ref[...], w_in_ref[...].reshape(width, chunk))
    bell = 0.5 * (1.0 + lax.erf(before * inv_root_two))
    active = (before * bell).astype(BF)
    slope = (bell + before * jnp.exp(-0.5 * before * before) * inv_root_two_pi).astype(BF)

    @pl.when(step < 2)
    def _():
        send_ref[0] = active
        send_ref[1] = slope

    @pl.when(step >= 2)
    def _():
        keep_ref[0] = active
        keep_ref[1] = slope

    total_ref[...] += mm(active, w_out_ref[...].reshape(chunk, width))

    @pl.when(step == 3)
    def _():
        normed, inverse = norm_rows(total_ref[...])
        normed_ffn_ref[...] = normed
        inverse_ffn_ref[...] = inverse
        result = normed * vectors_ref[2:3, :] + vectors_ref[3:4, :]
        result_ref[...] = result
        low_ref[...] = result.astype(BF)


def ffn_forward(places, parts, vectors, packed):
    rows = parts[0].shape[0]
    width, chunk = packed.width, packed.units // 4

    def chunks(step, places):
        return ((step // 2 + 1 + places[0]) % 2, step % 2, 0)

    block = (rows, width)
    kept = (2, rows, chunk)
    return pl.pallas_call(
        functools.partial(ffn_forward_kernel, len(parts)),
        grid_spec=pltpu.PrefetchScalarGridSpec(
            num_scalar_prefetch=1,
            grid=(4,),
            in_specs=[whole(block)] * len(parts)
            + [whole(vectors.shape), packed.in_spec(1, chunks), packed.out_spec(1, chunks)],
            out_specs=[
                whole(block), whole(block), whole(block),
                whole(block), whole((rows, 1)), whole(block), whole((rows, 1)),
                pl.BlockSpec(kept, lambda i, p: (0, 0, jnp.minimum(i, 1))),
                pl.BlockSpec(kept, lambda i, p: (0, 0, jnp.maximum(i - 2, 0))),
            ],
            scratch_shapes=[pltpu.VMEM(block, F32), pltpu.VMEM(block, F32)],
        ),
        out_shape=[
            struct(block, F32), struct(block, BF), struct(block, BF),
            struct(block, F32), struct((rows, 1), F32), struct(block, F32), struct((rows, 1), F32),
            struct((2, rows, 2 * chunk), BF), struct((2, rows, 2 * chunk), BF),
        ],
        compiler_params=PARAMS,
        cost_estimate=cost(
            16 * rows * width * chunk, 16 * width * chunk + 16 * rows * chunk, 8 * rows * chunk
        ),
    )(places, *parts, vectors, packed.fc_in, packed.fc_out)


def ffn_backward_kernel(place_ref, *refs):
    g_own, g_sib, m_own, m_sib, a_own, a_sib, w_in_ref, w_out_ref = refs[:8]
    own_ref, sib_ref, in_send, in_keep, out_send, out_keep, total_ref = refs[8:]
    step = pl.program_id(0)
    rows, width = g_own.shape
    chunk = a_own.shape[2]
    grads = jnp.concatenate([g_own[...], g_sib[...]], axis=0)
    w_in = w_in_ref[...].reshape(width, chunk)
    slope = jnp.concatenate([a_own[1], a_sib[1]], axis=0).astype(F32)
    before_grad = (mm_t(grads, w_out_ref[...].reshape(chunk, width)) * slope).astype(BF)
    part = mm_t(before_grad, w_in)

    @pl.when(step == 0)
    def _():
        total_ref[...] = part

    @pl.when(step > 0)
    def _():
        total_ref[...] += part

    half = width // 2
    for mine, ref in ((1 - place_ref[1], in_send), (place_ref[1], in_keep)):
        lanes = pl.ds(pl.multiple_of(mine * half, half), half)
        middle = jnp.concatenate([m_own[:, lanes], m_sib[:, lanes]], axis=0)
        ref[...] = mm_outer(middle, before_grad, BF)
    active = jnp.concatenate([a_own[0], a_sib[0]], axis=0)
    out_grad = mm_outer(active, grads, BF)

    @pl.when(step < 2)
    def _():
        out_send[0] = out_grad

    @pl.when(step >= 2)
    def _():
        out_keep[0] = out_grad

    @pl.when(step == 3)
    def _():
        own_ref[...] = total_ref[:rows, :]
        sib_ref[...] = total_ref[rows:, :].astype(BF)


def ffn_backward(places, grads, middles, actives, packed):
    rows, width = grads[0].shape
    chunk = packed.units // 8

    def chunks(step, places):
        return (places[0], step % 2, (step // 2 + 1 + places[2]) % 2)

    def column(step, places):
        return step % 2 * 2 + (step // 2 + 1 + places[2]) % 2

    block = (rows, width)
    kept = pl.BlockSpec((2, rows, chunk), lambda i, p: (0, 0, column(i, p)))
    side = pl.BlockSpec((width // 2, chunk), lambda i, p: (0, column(i, p)))
    return pl.pallas_call(
        ffn_backward_kernel,
        grid_spec=pltpu.PrefetchScalarGridSpec(
            num_scalar_prefetch=1,
            grid=(4,),
            in_specs=[whole(block)] * 4
            + [kept, kept, packed.in_spec(2, chunks), packed.out_spec(2, chunks)],
            out_specs=[
                whole(block), whole(block), side, side,
                pl.BlockSpec((1, chunk, width), lambda i, p: (jnp.minimum(i, 1), 0, 0)),
                pl.BlockSpec((1, chunk, width), lambda i, p: (jnp.maximum(i - 2, 0), 0, 0)),
            ],
            scratch_shapes=[pltpu.VMEM((2 * rows, width), F32)],
        ),
        out_shape=[
            struct(block, F32), struct(block, BF),
            struct((width // 2, 4 * chunk), BF), struct((width // 2, 4 * chunk), BF),
            struct((2, chunk, width), BF), struct((2, chunk, width), BF),
        ],
        compiler_params=PARAMS,
        cost_estimate=cost(64 * rows * width * chunk, 40 * width * chunk),
    )(places, *grads, *middles, *actives, packed.fc_in, packed.fc_out)


def scatter_ffn(plan, in_send, in_keep, out_send, out_keep):
    inner = [b for b in reversed(plan.f_bits) if b not in (plan.hi, plan.lo)]
    z_count = plan.ranks // 2
    tail = (2,) * len(inner) + (2, z_count)
    first = Sum([in_keep, plan.swap(in_send, "fsdp", plan.hi)])
    first = first.reshape(2, *tail, -1, in_keep.shape[1])
    second = Sum([out_keep, plan.swap(out_send, "fsdp", plan.lo)])
    second = second.reshape(2, *tail, -1, out_keep.shape[2])
    first.step(plan, "fsdp", plan.lo, 0)
    second.step(plan, "fsdp", plan.hi, 0)
    for bit in inner:
        first.step(plan, "fsdp", bit, 0)
        second.step(plan, "fsdp", bit, 0)
    for member in (first, second):
        count = z_count
        for bit in reversed(plan.z_bits):
            count = count // 2
            member.parts = [p.reshape((2, 2, count) + p.shape[2:]) for p in member.parts]
            member.step(plan, "seq", bit, 1)
        member.parts = [p.reshape((2,) + p.shape[2:]) for p in member.parts]
        member.step(plan, "seq", plan.ranks, 0)
    fc_out = second.total()
    fc_in = first.total().astype(BF)
    fc_in = fc_in.reshape(2, fc_in.shape[0] // 2, -1)
    here, send = choose(plan.core, fc_in, 0)
    there = plan.swap(send, "seq", 1)
    rows = here.shape[0]
    parts = (rows, plan.n // 2, -1)
    fc_in = stack_by(plan.core, here.reshape(parts), there.reshape(parts), 2)
    return fc_in.reshape(rows, -1).astype(F32), fc_out


def gather_vectors(plan, vectors):
    layers, count, own = vectors.shape
    value = vectors.reshape(1, -1)
    for bit in [1] + plan.z_bits + [plan.ranks]:
        value = stack_by(bit_of(plan.s, bit), value, plan.swap(value, "seq", bit), 0)
        value = value.reshape(-1, value.shape[-1])
    for bit in plan.f_bits:
        value = stack_by(bit_of(plan.f, bit), value, plan.swap(value, "fsdp", bit), 0)
        value = value.reshape(-1, value.shape[-1])
    value = value.reshape(plan.n, layers, count, own)
    return jnp.transpose(value, (1, 2, 0, 3)).reshape(layers, count, -1)


def sum_vectors(plan, vectors):
    count, width = vectors.shape
    value = vectors.reshape(count, plan.n, width // plan.n)
    value = jnp.transpose(value, (1, 0, 2)).reshape(plan.n, -1)
    order = [("fsdp", b) for b in reversed(plan.f_bits)]
    order += [("seq", b) for b in reversed([1] + plan.z_bits + [plan.ranks])]
    for axis_name, bit in order:
        value = value.reshape(2, value.shape[0] // 2, -1)
        here, send = choose(bit_of(plan.f if axis_name == "fsdp" else plan.s, bit), value, 0)
        value = here + plan.swap(send, axis_name, bit)
    return value.reshape(count, width // plan.n)


def local(
    mesh_shape,
    inputs,
    segment_ids,
    query_weight,
    key_weight,
    value_weight,
    out_weight,
    fc_in_weight,
    fc_out_weight,
    attn_gain,
    attn_shift,
    ffn_gain,
    ffn_shift,
    cotangent,
):
    layers, _, width = query_weight.shape
    plan = Plan(mesh_shape, width, fc_in_weight.shape[2])
    places = plan.scalars()
    head_dim = width // HEADS

    def to_halves(value):
        mine, other = choose(plan.half, value, 0)
        return jnp.concatenate([mine, plan.swap(other, "seq", plan.ranks)], axis=0)

    def from_halves(value):
        size = value.shape[0] // 2
        there = plan.swap(value[size:].astype(BF), "seq", plan.ranks).astype(F32)
        return stack_by(plan.half, value[:size], there, 0)

    x_low = to_halves(inputs)
    attention = gather_attention(
        plan, places, (query_weight, key_weight, value_weight, out_weight)
    )
    packed = [Packed(plan, fc_in_weight[k], fc_out_weight[k]) for k in range(layers)]
    ids = jnp.concatenate(group_pieces(plan, to_halves(segment_ids)), axis=0)
    vectors = jnp.stack([attn_gain, attn_shift, ffn_gain, ffn_shift], axis=1)
    vectors = gather_vectors(plan, vectors).astype(F32)
    upstream = [to_halves(cotangent)]
    tokens = x_low.shape[0]

    hidden = x_low
    records = []
    for layer in range(layers):
        x_pieces = group_pieces(plan, x_low)
        qkv, att, keep, send = attn_forward(x_pieces, *attention[layer], ids, head_dim)
        parts = [hidden] + group_sum(plan, keep, send)
        (
            hidden, x_low, mid_low, normed_attn, inverse_attn, normed_ffn, inverse_ffn, send, keep,
        ) = ffn_forward(places, parts, vectors[layer], packed[layer])
        actives = (keep, plan.swap(send, "seq", 1))
        middles = (mid_low, plan.swap(mid_low, "seq", 1))
        records.append(
            (x_pieces, qkv, att, normed_attn, inverse_attn, normed_ffn, inverse_ffn, actives, middles)
        )
    outputs = from_halves(hidden)

    grads, vector_grads = [None] * layers, [None] * layers
    for layer in reversed(range(layers)):
        (
            x_pieces, qkv, att, normed_attn, inverse_attn, normed_ffn, inverse_ffn, actives, middles,
        ) = records[layer]
        gains = vectors[layer]
        sum_grad, ff_grad, gain_ffn_grad, shift_ffn_grad = norm_backward(
            upstream, normed_ffn, inverse_ffn, gains[2:3]
        )
        ff_grads = (ff_grad, plan.swap(ff_grad, "seq", 1))
        own, sibling, *ffn_grads = ffn_backward(places, ff_grads, middles, actives, packed[layer])
        attn_sum_grad, branch_grad, gain_attn_grad, shift_attn_grad = norm_backward(
            [sum_grad, own, plan.swap(sibling, "seq", 1)], normed_attn, inverse_attn, gains[0:1]
        )
        g_pieces = group_pieces(plan, branch_grad)
        dqkv, keep, send = attn_backward(g_pieces, qkv, *attention[layer], ids, head_dim)
        upstream = [attn_sum_grad] + group_sum(plan, keep, send)
        fc_in_grad, fc_out_grad = scatter_ffn(plan, *ffn_grads)
        attn_grads = scatter_attention(plan, places, x_pieces, g_pieces, dqkv, att)
        grads[layer] = (*attn_grads, fc_in_grad, fc_out_grad)
        vector_grads[layer] = (gain_attn_grad, shift_attn_grad, gain_ffn_grad, shift_ffn_grad)
    input_grad = from_halves(add_parts(upstream, tokens))
    summed = jnp.concatenate([v for member in vector_grads for v in member], axis=0)
    summed = sum_vectors(plan, summed).reshape(layers, 4, -1)
    merged = [jnp.stack([g[k] for g in grads]) for k in range(6)]
    return (outputs, input_grad, *merged, *(summed[:, k] for k in range(4)))


def solution(mesh):
    tokens = P("fsdp", "seq", None)
    matrix = P(None, ("fsdp", "seq"), None)
    vector = P(None, ("fsdp", "seq"))
    return jax.shard_map(
        functools.partial(local, dict(mesh.shape)),
        mesh=mesh,
        in_specs=(tokens, P("fsdp", "seq"), *[matrix] * 6, *[vector] * 4, tokens),
        out_specs=(tokens, tokens, *[matrix] * 6, *[vector] * 4),
        check_vma=False,
    )
```

```python
import functools

import jax
import jax.numpy as jnp
from jax import lax
from jax.experimental import pallas as pl
from jax.experimental.pallas import tpu as pltpu
from jax.sharding import PartitionSpec as P

HEADS = 16
NEG_FILL = -1e30
NORM_EPS = 1e-05
inv_root_two = 0.7071067811865476
inv_root_two_pi = 0.3989422804014327
BF = jnp.bfloat16
F32 = jnp.float32
ALL = ("fsdp", "seq")
PARAMS = pltpu.CompilerParams(vmem_limit_bytes=56 * 1024 * 1024)


def mm(a, b, out=F32):
    return lax.dot_general(a, b, (((1,), (0,)), ((), ())), preferred_element_type=F32).astype(out)


def mm_t(a, b, out=F32):
    return lax.dot_general(a, b, (((1,), (1,)), ((), ())), preferred_element_type=F32).astype(out)


def mm_outer(a, b, out=F32):
    return lax.dot_general(a, b, (((0,), (0,)), ((), ())), preferred_element_type=F32).astype(out)


def struct(shape, dtype):
    return jax.ShapeDtypeStruct(shape, dtype)


def whole(shape):
    return pl.BlockSpec(shape, lambda *_: (0,) * len(shape))


FREE = pl.CostEstimate(flops=0, bytes_accessed=0, transcendentals=0)


class Plan:
    def __init__(self, mesh_shape, width, hidden_units):
        self.n_f, self.n_s = mesh_shape["fsdp"], mesh_shape["seq"]
        self.n = self.n_f * self.n_s
        self.ranks = self.n_s // 2
        self.f = lax.axis_index("fsdp")
        self.s = lax.axis_index("seq")
        self.half = self.s // self.ranks
        self.rank = self.s % self.ranks
        self.core = self.s % 2
        self.f_bits = [1 << k for k in range(self.n_f.bit_length() - 1)]
        self.z_bits = [1 << k for k in range(1, self.ranks.bit_length() - 1)]
        self.hi, self.lo = self.f_bits[-1], self.f_bits[-2]
        self.f_hi, self.f_lo = bit_of(self.f, self.hi), bit_of(self.f, self.lo)
        self.fast = (
            self.n_f == 4
            and self.n_s == 8
            and (width // self.n) % 32 == 0
            and (hidden_units // self.n) % 128 == 0
        )

    def swap(self, value, axis_name, bit):
        count = self.n_f if axis_name == "fsdp" else self.n_s
        return lax.ppermute(value, axis_name, [(i, i ^ bit) for i in range(count)])

    def scalars(self):
        return jnp.stack([self.core, self.f_hi, self.f_lo, self.f * 2 + self.half, self.rank]).astype(
            jnp.int32
        )


def bit_of(index, bit):
    return (index // bit) % 2


def stack_by(mine, here, there, axis):
    return jnp.where(
        mine == 0, jnp.stack([here, there], axis=axis), jnp.stack([there, here], axis=axis)
    )


def choose(mine, value, axis):
    first = lax.index_in_dim(value, 0, axis, keepdims=False)
    second = lax.index_in_dim(value, 1, axis, keepdims=False)
    return jnp.where(mine == 0, first, second), jnp.where(mine == 0, second, first)


def group_pieces(plan, value):
    pieces = [value]
    for bit in plan.z_bits:
        pieces = pieces + [plan.swap(p, "seq", bit) for p in pieces]
    return pieces + [plan.swap(p, "seq", 1) for p in pieces]


def group_sum(plan, order, keep, send):
    parts = [keep, plan.swap(send, "seq", 1)]
    size = keep.shape[0]
    for bit in reversed(plan.z_bits):
        size = size // 2
        tied = order.tie(*parts)
        out = sum(p[size : 2 * size].astype(F32) for p in tied).astype(BF)
        parts = parts + [plan.swap(order.done(out), "seq", bit)]
    return parts


def add_parts(parts, rows):
    return sum(p[:rows].astype(F32) for p in parts)


class Order:
    def __init__(self):
        self.last = None

    def tie(self, *values):
        if self.last is None:
            return values
        return lax.optimization_barrier((*values, self.last))[:-1]

    def done(self, value):
        self.last = value
        return value


class Task:
    def __init__(self, steps):
        self.steps, self.result, self.running = steps, None, True
        self.run()

    @staticmethod
    def finished(result):
        task = Task(iter(()))
        task.result = result
        return task

    def run(self):
        if self.running:
            try:
                next(self.steps)
            except StopIteration as stop:
                self.running, self.result = False, stop.value


class Tasks:
    def __init__(self):
        self.open = []

    def add(self, steps):
        task = Task(steps)
        self.open.append(task)
        return task

    def run(self, task):
        task.run()

    def drain(self, task):
        while task.running:
            task.run()

    def slot(self, count):
        self.open = [t for t in self.open if t.running]
        for task in self.open[:count]:
            task.run()

    def finish(self):
        while self.open:
            self.slot(len(self.open))


class Sum:
    def __init__(self, plan, order, names, parts):
        self.plan, self.order, self.names = plan, order, tuple(names)
        self.parts = [(p, self.names) for p in parts]
        self.chosen = {}

    def pick(self, part, chosen):
        value, names = part
        rest = value.shape[len(names) :]
        zero = jnp.zeros((), jnp.int32)
        start = [chosen.get(n, zero) for n in names] + [zero] * len(rest)
        size = [1 if n in chosen else 2 for n in names] + list(rest)
        left = [d for n, d in zip(names, size) if n not in chosen]
        return lax.dynamic_slice(value, start, size).reshape(*left, *rest)

    def tie(self):
        tied = self.order.tie(*[p for p, _ in self.parts])
        self.parts = [(p, names) for p, (_, names) in zip(tied, self.parts)]

    def sending(self, name, kind=BF):
        plan = self.plan
        mine = bit_of(plan.f if name[0] == "fsdp" else plan.s, name[1]).astype(jnp.int32)
        there = {**self.chosen, name: 1 - mine}
        out = sum(self.pick(p, there).astype(F32) for p in self.parts).astype(kind)
        self.chosen[name] = mine
        return out

    def receive(self, value):
        left = [n for n in self.names if n not in self.chosen]
        self.parts.append((value, tuple(left)))

    def step(self, name):
        self.tie()
        send = self.order.done(self.sending(name))
        self.receive(self.plan.swap(send, *name))

    def total(self):
        return sum(self.pick(p, self.chosen).astype(F32) for p in self.parts)


def norm_rows(summed):
    center = jnp.mean(summed, axis=-1, keepdims=True)
    offset = summed - center
    spread = jnp.mean(offset * offset, axis=-1, keepdims=True)
    inverse = lax.rsqrt(spread + NORM_EPS)
    return offset * inverse, inverse


def norm_backward_kernel(count, *refs):
    parts, (normed_ref, inverse_ref, gain_ref) = refs[:count], refs[count : count + 3]
    out_ref, low_ref, gain_grad_ref, shift_grad_ref = refs[count + 3 :]
    upstream = parts[0][...].astype(F32)
    for part in parts[1:]:
        upstream = upstream + part[...].astype(F32)
    normed = normed_ref[...]
    gain_grad_ref[...] = jnp.sum(upstream * normed, axis=0, keepdims=True)
    shift_grad_ref[...] = jnp.sum(upstream, axis=0, keepdims=True)
    scaled = upstream * gain_ref[...]
    inner = (
        scaled
        - jnp.mean(scaled, axis=-1, keepdims=True)
        - normed * jnp.mean(scaled * normed, axis=-1, keepdims=True)
    )
    result = inner * inverse_ref[...]
    out_ref[...] = result
    low_ref[...] = result.astype(BF)


def norm_backward(parts, normed, inverse, gain):
    rows, width = normed.shape
    return pl.pallas_call(
        functools.partial(norm_backward_kernel, len(parts)),
        grid=(1,),
        in_specs=[whole((rows, width))] * (len(parts) + 1) + [whole((rows, 1)), whole((1, width))],
        out_specs=[whole((rows, width))] * 2 + [whole((1, width))] * 2,
        out_shape=[
            struct((rows, width), F32), struct((rows, width), BF),
            struct((1, width), F32), struct((1, width), F32),
        ],
        compiler_params=PARAMS,
        cost_estimate=FREE,
    )(*parts, normed, inverse, gain)


def pick_head(lanes, head, head_dim):
    return (lanes >= head * head_dim) & (lanes < (head + 1) * head_dim)


def attn_forward_kernel(head_dim, count, *refs):
    pieces = refs[:count]
    w_qkv_ref, w_out_ref, ids_q_ref, ids_k_ref = refs[count : count + 4]
    qkv_ref, att_ref, keep_ref, send_ref = refs[count + 4 :]
    step = pl.program_id(0)
    rows, width = att_ref.shape

    @pl.when(step == 0)
    def _():
        w_qkv = w_qkv_ref[...]
        for index, piece in enumerate(pieces):
            qkv = mm(piece[...], w_qkv).astype(BF)
            part = pl.ds(index * rows, rows)
            qkv_ref[part, :width] = (qkv[:, :width].astype(F32) * head_dim**-0.5).astype(BF)
            qkv_ref[part, width:] = qkv[:, width:]

    queries = qkv_ref[pl.ds(pl.multiple_of(step * rows, rows), rows), :width]
    keys, values = qkv_ref[:, width : 2 * width], qkv_ref[:, 2 * width :]
    lanes = lax.broadcasted_iota(jnp.int32, (1, width), 1)
    allowed = ids_q_ref[...] == ids_k_ref[...]
    total = jnp.zeros((rows, width), F32)
    for head in range(width // head_dim):
        here = pick_head(lanes, head, head_dim)
        scores = mm_t(jnp.where(here, queries, jnp.zeros_like(queries)), keys)
        scores = jnp.where(allowed, scores, NEG_FILL)
        weights = jnp.exp(scores - jnp.max(scores, axis=1, keepdims=True))
        norm = 1.0 / jnp.sum(weights, axis=1, keepdims=True)
        total = jnp.where(here, mm(weights.astype(BF), values) * norm, total)
    attended = total.astype(BF)
    att_ref[...] = attended
    branch = mm(attended, w_out_ref[...])

    @pl.when(step < count // 2)
    def _():
        keep_ref[...] = branch

    @pl.when(step >= count // 2)
    def _():
        send_ref[...] = branch.astype(BF)


def attn_forward(pieces, w_qkv, w_out, ids, head_dim):
    count = len(pieces)
    rows, features = pieces[0].shape
    tokens, width = count * rows, w_out.shape[0]
    half = count // 2
    heads = width // head_dim
    return pl.pallas_call(
        functools.partial(attn_forward_kernel, head_dim, count),
        grid=(count,),
        in_specs=[whole((rows, features))] * count
        + [
            whole(w_qkv.shape),
            whole(w_out.shape),
            pl.BlockSpec((rows, 1), lambda i: (i, 0)),
            whole((1, tokens)),
        ],
        out_specs=[
            whole((tokens, 3 * width)),
            pl.BlockSpec((rows, width), lambda i: (i, 0)),
            pl.BlockSpec((rows, features), lambda i: (jnp.minimum(i, half - 1), 0)),
            pl.BlockSpec((rows, features), lambda i: (jnp.maximum(i - half, 0), 0)),
        ],
        out_shape=[
            struct((tokens, 3 * width), BF),
            struct((tokens, width), BF),
            struct((half * rows, features), F32),
            struct((half * rows, features), BF),
        ],
        compiler_params=PARAMS,
        cost_estimate=FREE,
    )(*pieces, w_qkv, w_out, ids.reshape(tokens, 1), ids.reshape(1, tokens))


def attn_backward_kernel(head_dim, count, *refs):
    pieces = refs[:count]
    qkv_ref, w_qkv_ref, w_out_ref, ids_q_ref, ids_k_ref = refs[count : count + 5]
    dqkv_ref, keep_ref, send_ref, grad_ref, dk_ref, dv_ref = refs[count + 5 :]
    step = pl.program_id(0)
    rows = pieces[0].shape[0]
    width = grad_ref.shape[1]

    @pl.when(step == 0)
    def _():
        w_out = w_out_ref[...]
        for index, piece in enumerate(pieces):
            grad_ref[pl.ds(index * rows, rows), :] = mm_t(piece[...], w_out, BF)
        dk_ref[...] = jnp.zeros_like(dk_ref)
        dv_ref[...] = jnp.zeros_like(dv_ref)

    place = pl.ds(pl.multiple_of(step * rows, rows), rows)
    queries, grads = qkv_ref[place, :width], grad_ref[place, :]
    keys, values = qkv_ref[:, width : 2 * width], qkv_ref[:, 2 * width :]
    lanes = lax.broadcasted_iota(jnp.int32, (1, width), 1)
    allowed = ids_q_ref[...] == ids_k_ref[...]
    dq = jnp.zeros((rows, width), F32)
    for head in range(width // head_dim):
        here = pick_head(lanes, head, head_dim)
        q_head = jnp.where(here, queries, jnp.zeros_like(queries))
        g_head = jnp.where(here, grads, jnp.zeros_like(grads))
        scores = mm_t(q_head, keys)
        scores = jnp.where(allowed, scores, NEG_FILL)
        weights = jnp.exp(scores - jnp.max(scores, axis=1, keepdims=True))
        probs = weights * (1.0 / jnp.sum(weights, axis=1, keepdims=True))
        prob_grad = mm_t(g_head, values)
        product = probs * prob_grad
        delta = jnp.sum(product, axis=1, keepdims=True)
        score_grad = (product - probs * delta).astype(BF)
        dq = jnp.where(here, mm(score_grad, keys), dq)
        dk_ref[...] += mm_outer(score_grad, q_head)
        dv_ref[...] += mm_outer(probs.astype(BF), g_head)
    dqkv_ref[place, :width] = (dq * head_dim**-0.5).astype(BF)

    @pl.when(step == count - 1)
    def _():
        dqkv_ref[:, width : 2 * width] = dk_ref[...].astype(BF)
        dqkv_ref[:, 2 * width :] = dv_ref[...].astype(BF)
        w_qkv = w_qkv_ref[...]
        half = count // 2
        for index in range(count):
            part = mm_t(dqkv_ref[pl.ds(index * rows, rows), :], w_qkv)
            if index < half:
                keep_ref[pl.ds(index * rows, rows), :] = part
            else:
                send_ref[pl.ds((index - half) * rows, rows), :] = part.astype(BF)


def attn_backward(pieces, qkv, w_qkv, w_out, ids, head_dim):
    count = len(pieces)
    rows, features = pieces[0].shape
    tokens, width = count * rows, w_out.shape[0]
    heads = width // head_dim
    half = tokens // 2
    return pl.pallas_call(
        functools.partial(attn_backward_kernel, head_dim, count),
        grid=(count,),
        in_specs=[whole((rows, features))] * count
        + [
            whole(qkv.shape),
            whole(w_qkv.shape),
            whole(w_out.shape),
            pl.BlockSpec((rows, 1), lambda i: (i, 0)),
            whole((1, tokens)),
        ],
        out_specs=[
            whole((tokens, 3 * width)), whole((half, features)), whole((half, features)),
        ],
        out_shape=[
            struct((tokens, 3 * width), BF), struct((half, features), F32),
            struct((half, features), BF),
        ],
        scratch_shapes=[
            pltpu.VMEM((tokens, width), BF),
            pltpu.VMEM((tokens, width), F32),
            pltpu.VMEM((tokens, width), F32),
        ],
        compiler_params=PARAMS,
        cost_estimate=FREE,
    )(*pieces, qkv, w_qkv, w_out, ids.reshape(tokens, 1), ids.reshape(1, tokens))


def attn_weights_kernel(count, place_ref, *refs):
    x_refs, g_refs = refs[:count], refs[count : 2 * count]
    dqkv_ref, att_ref = refs[2 * count : 2 * count + 2]
    outputs, out_ref = refs[2 * count + 2 : -1], refs[-1]
    block = pl.program_id(0)
    rows = x_refs[0].shape[0]
    width = att_ref.shape[1]
    small = out_ref.shape[0] // pl.num_programs(0)
    height = 4 * small

    @pl.when(block == 0)
    def _():
        total = None
        for index in range(count):
            part = mm_outer(att_ref[pl.ds(index * rows, rows), :], g_refs[index][...])
            total = part if total is None else total + part
        out_ref[...] = total.astype(BF)

    lanes = pl.ds(pl.multiple_of(block * height, height), height)
    grad = None
    for index in range(count):
        part = mm_outer(x_refs[index][:, lanes], dqkv_ref[pl.ds(index * rows, rows), :])
        grad = part if grad is None else grad + part
    grad = grad.astype(BF)
    hi, lo, low = block // 4, (block // 2) % 2, block % 2

    def put_a(ref, place):
        ref[place, :height, :] = grad[:, :width]
        ref[place, height : 2 * height, :] = grad[:, width : 2 * width]

    def put_b(ref, place, first):
        ref[place, first : first + height, :] = grad[:, 2 * width :]
        part = out_ref[pl.ds(pl.multiple_of(block * small, small), small), :]
        for piece in range(4):
            start = first + height + piece * small
            ref[place, start : start + small, :] = part[:, piece * width : (piece + 1) * width]

    if len(outputs) == 1:
        put_a(outputs[0], block)
        put_b(outputs[0], block, 2 * height)
        return
    a_send, a_keep, b_send, b_keep = outputs
    pl.when(hi != place_ref[1])(lambda: put_a(a_send, lo * 2 + low))
    pl.when(hi == place_ref[1])(lambda: put_a(a_keep, lo * 2 + low))
    pl.when(lo != place_ref[2])(lambda: put_b(b_send, hi * 2 + low, 0))
    pl.when(lo == place_ref[2])(lambda: put_b(b_keep, hi * 2 + low, 0))


def attn_weights(places, x_pieces, g_pieces, dqkv, att, cut):
    count = len(x_pieces)
    rows, features = x_pieces[0].shape
    width = att.shape[1]
    high = 2 * features // 8
    parts = [(4, high, width)] * 4 if cut else [(8, 2 * high, width)]
    return pl.pallas_call(
        functools.partial(attn_weights_kernel, count),
        grid_spec=pltpu.PrefetchScalarGridSpec(
            num_scalar_prefetch=1,
            grid=(8,),
            in_specs=[whole((rows, features))] * (2 * count) + [whole(dqkv.shape), whole(att.shape)],
            out_specs=[whole(p) for p in parts],
            scratch_shapes=[pltpu.VMEM((width, features), BF)],
        ),
        out_shape=[struct(p, BF) for p in parts],
        compiler_params=PARAMS,
        cost_estimate=FREE,
    )(places, *x_pieces, *g_pieces, dqkv, att)


def assemble_kernel(place_ref, a_own, a_other, b_own, b_other, qkv_ref, out_ref):
    own, rank = place_ref[3], place_ref[4]
    height, width = a_own.shape[1] // 8, a_own.shape[2]
    ranks = 4
    for block in range(8):
        a_ref = a_own if block < 4 else a_other
        b_ref = b_own if block < 4 else b_other
        b_block = (block % 4) // 2 * 4 + block // 4 * 2 + block % 2
        for inner in range(4):
            rank_there = rank ^ ((inner // 2) + (inner % 2) * 2)
            start = ((own ^ block) * ranks + rank_there) * height
            place = pl.ds(pl.multiple_of(start, height), height)
            qkv_ref[place, :width] = a_ref[block % 4, inner * height : (inner + 1) * height, :]
            first = (4 + inner) * height
            qkv_ref[place, width : 2 * width] = a_ref[block % 4, first : first + height, :]
            start = ((own ^ b_block) * ranks + rank_there) * height
            place = pl.ds(pl.multiple_of(start, height), height)
            qkv_ref[place, 2 * width :] = b_ref[block % 4, inner * height : (inner + 1) * height, :]
            place = pl.ds(pl.multiple_of((own ^ b_block) * height, height), height)
            out_ref[place, inner * width : (inner + 1) * width] = b_ref[
                block % 4, first : first + height, :
            ]


def assemble(places, a_own, a_other, b_own, b_other):
    _, high, width = a_own.shape
    features = 4 * high
    return pl.pallas_call(
        assemble_kernel,
        grid_spec=pltpu.PrefetchScalarGridSpec(
            num_scalar_prefetch=1,
            grid=(1,),
            in_specs=[whole(a_own.shape)] * 4,
            out_specs=[whole((features, 3 * width)), whole((width, features))],
        ),
        out_shape=[struct((features, 3 * width), BF), struct((width, features), BF)],
        compiler_params=PARAMS,
        cost_estimate=FREE,
    )(places, a_own, a_other, b_own, b_other)


def spread_pairs(plan):
    pairs = []
    for shard in range(plan.n):
        rank, block = shard // (2 * plan.n_f), shard % (2 * plan.n_f)
        pairs.append((shard, block // 2 * plan.n_s + block % 2 * plan.ranks + rank))
    return pairs


def gather_attention_whole(plan, matrices):
    layers, _, cols = matrices[0].shape
    size = cols // plan.ranks
    result = []
    for layer in range(layers):
        full = [lax.all_gather(m[layer], ALL, axis=0, tiled=True) for m in matrices]
        qkv = [lax.dynamic_slice_in_dim(m, plan.rank * size, size, 1) for m in full[:3]]
        w_out = lax.dynamic_slice_in_dim(full[3], plan.rank * size, size, 0)
        result.append((jnp.concatenate(qkv, axis=1), w_out))
    return result


def rank_columns(plan, order, matrices):
    query, key, value, out = matrices
    layers, rows, cols = query.shape
    half = cols // 2
    upper = bit_of(plan.s, 2) == 1
    send = [jnp.where(upper, m[..., :half], m[..., half:]) for m in (query, key, value)]
    there = plan.swap(order.done(jnp.stack(send, axis=1)), "seq", 2)
    out = lax.ppermute(out, ALL, spread_pairs(plan))
    yield
    query, key, value, there = order.tie(query, key, value, there)
    here = [jnp.where(upper, m[..., half:], m[..., :half]) for m in (query, key, value)]
    both = jnp.stack([jnp.stack(here, axis=1), there], axis=2)
    quarter = half // 2
    upper = plan.core == 1
    send = jnp.where(upper, both[..., :quarter], both[..., quarter:])
    there = plan.swap(order.done(send), "seq", 1)
    here = jnp.where(upper, both[..., quarter:], both[..., :quarter])
    yield
    return here, there, out


def gather_attention(plan, order, places, columns):
    here, there, out = order.tie(*columns)
    quarter = here.shape[-1]
    qkv = jnp.stack([here, there], axis=1)
    w_out = jnp.stack([out[:, k * quarter : (k + 1) * quarter] for k in range(4)])
    bundle = jnp.concatenate([qkv.reshape(-1, quarter), w_out.reshape(-1, quarter)], axis=0)
    other = plan.swap(order.done(bundle), "seq", plan.ranks)
    yield
    bundle, other = order.tie(bundle, other)
    size = bundle.shape[0] // 2
    part_a = order.done(jnp.stack([bundle[:size], other[:size]]))
    part_b = order.done(jnp.stack([bundle[size:], other[size:]]))
    other_a = plan.swap(part_a, "fsdp", plan.lo)
    other_b = plan.swap(part_b, "fsdp", plan.hi)
    yield
    part_a, other_a, part_b, other_b = order.tie(part_a, other_a, part_b, other_b)
    part_a = order.done(jnp.concatenate([part_a, other_a], axis=0))
    part_b = order.done(jnp.concatenate([part_b, other_b], axis=0))
    other_a = plan.swap(part_a, "fsdp", plan.hi)
    other_b = plan.swap(part_b, "fsdp", plan.lo)
    yield
    result = assemble(places, *order.tie(part_a, other_a, part_b, other_b))
    order.done(result[1])
    return result


def scatter_attention(plan, order, places, x_pieces, g_pieces, dqkv, att, cut):
    if not plan.fast:
        w_qkv = sum(mm_outer(x, d) for x, d in zip(x_pieces, jnp.split(dqkv, len(x_pieces))))
        w_out = sum(mm_outer(a, g) for a, g in zip(jnp.split(att, len(g_pieces)), g_pieces))
        width, features = w_out.shape
        grads = []
        for grad, axis in [(g, 1) for g in jnp.split(w_qkv, 3, axis=1)] + [(w_out, 0)]:
            full = jnp.zeros((features, features), F32)
            full = lax.dynamic_update_slice_in_dim(full, grad, plan.rank * width, axis)
            grads.append(lax.psum_scatter(full, ALL, scatter_dimension=0, tiled=True))
        return grads
    count = len(x_pieces)
    tied = order.tie(*x_pieces, *g_pieces, dqkv, att)
    grads = attn_weights(
        places, tied[:count], tied[count : 2 * count], *tied[2 * count :], cut
    )
    order.done(grads[-1])
    half = ("seq", plan.ranks)
    if cut:
        a_send, a_keep, b_send, b_keep = grads
        high, width = a_send.shape[1:]
        hi, lo = ("fsdp", plan.hi), ("fsdp", plan.lo)
        parts = [a_keep, plan.swap(a_send, *hi)]
        part_a = Sum(plan, order, (lo, half), [p.reshape(2, 2, high, width) for p in parts])
        parts = [b_keep, plan.swap(b_send, *lo)]
        part_b = Sum(plan, order, (hi, half), [p.reshape(2, 2, high, width) for p in parts])
        yield
        part_a.step(lo)
        part_b.step(hi)
        yield
        part_a.tie()
        part_b.tie()
        send = jnp.stack([part_a.sending(half), part_b.sending(half)])
        there = plan.swap(order.done(send), *half)
        part_a.receive(there[0])
        part_b.receive(there[1])
        yield
        part_a.tie()
        part_b.tie()
        total_a = part_a.total().astype(BF)
        total_b = part_b.total().astype(BF)
    else:
        _, high, width = grads[0].shape
        high = high // 2
        groups = [
            [f * plan.n_s + h * plan.ranks + r for f in range(plan.n_f) for h in range(2)]
            for r in range(plan.ranks)
        ]
        total = lax.psum_scatter(
            grads[0].reshape(-1, width), ALL, scatter_dimension=0, tiled=True,
            axis_index_groups=groups,
        )
        yield
        (total,) = order.tie(total)
        total_a, total_b = total[:high], total[high:]
    total_a = total_a.reshape(2, 2, 2, high // 8, width)
    total_b = total_b.reshape(2, 4, high // 8, width)
    out = jnp.concatenate([total_b[1, k] for k in range(4)], axis=1)
    out = lax.ppermute(out, ALL, [(b, a) for a, b in spread_pairs(plan)])
    qkv = jnp.concatenate([total_a, total_b[:1].reshape(1, 2, 2, high // 8, width)], axis=0)
    here, send = choose(bit_of(plan.s, 2), qkv, 1)
    there = plan.swap(order.done(send), "seq", 2)
    yield
    here, there = order.tie(here, there)
    qkv = stack_by(bit_of(plan.s, 2), here, there, 0)
    here, send = choose(plan.core, qkv, 2)
    there = plan.swap(order.done(send), "seq", 1)
    yield
    here, there, out = order.tie(here, there, out)
    qkv = stack_by(plan.core, here, there, 1)
    qkv = jnp.concatenate([qkv[0, 0], qkv[0, 1], qkv[1, 0], qkv[1, 1]], axis=2).astype(F32)
    order.done(qkv)
    return [qkv[0], qkv[1], qkv[2], out.astype(F32)]


class Packed:
    def __init__(self, plan, fc_in, fc_out):
        rows, units = fc_in.shape
        width = fc_out.shape[1]
        own = units // plan.n
        split = fc_in.reshape(rows, plan.n // 2, 2, own)
        split = jnp.transpose(split, (2, 0, 1, 3)).reshape(2, rows, 2, units // 4)
        split = jnp.transpose(split, (0, 2, 1, 3))
        self.rows, self.width, self.units = rows, rows * plan.n, units
        self.fast = plan.fast and units // 4 == width
        if self.fast:
            flat = jnp.concatenate([split.reshape(4 * rows, width), fc_out], axis=0)
            full = lax.all_gather(flat, ALL, axis=0, tiled=True)
            self.fc_in = full.reshape(plan.n, 8, rows, width)
            self.fc_out = full.reshape(plan.n // 2, 2, 8, rows, width)
        else:
            full = lax.all_gather(split, ALL, axis=2, tiled=True)
            self.fc_in = full.reshape(1, 4, self.width, units // 4)
            full = lax.all_gather(fc_out, ALL, axis=0, tiled=True)
            full = full.reshape(plan.n // 2, 2, own, width)
            self.fc_out = jnp.transpose(full, (1, 0, 2, 3)).reshape(2, units // 2, width)

    def in_spec(self, parts, index):
        shape = self.fc_in.shape

        def place(step, places):
            core, upper, part = index(step, places)
            return (0, core * 2 + upper, 0, part)

        return pl.BlockSpec((shape[0], 1, shape[2], shape[3] // parts), place)

    def out_spec(self, parts, index):
        shape = self.fc_out.shape

        def place(step, places):
            core, upper, part = index(step, places)
            where = upper * parts + part
            return (where, core, 1, 0, 0) if self.fast else (core, where, 0)

        if self.fast:
            return pl.BlockSpec((shape[0] // 2 // parts, 1, 4, shape[3], shape[4]), place)
        return pl.BlockSpec((1, shape[1] // 2 // parts, shape[2]), place)


def ffn_forward_kernel(count, place_ref, *refs):
    parts = refs[:count]
    vectors_ref, w_in_ref, w_out_ref = refs[count : count + 3]
    (
        result_ref, low_ref, mid_low_ref, normed_attn_ref, inverse_attn_ref, normed_ffn_ref,
        inverse_ffn_ref, send_ref, keep_ref, mid_ref, total_ref,
    ) = refs[count + 3 :]
    step = pl.program_id(0)
    width = mid_ref.shape[1]
    chunk = send_ref.shape[2]

    @pl.when(step == 0)
    def _():
        summed = parts[0][...].astype(F32)
        for part in parts[1:]:
            summed = summed + part[...].astype(F32)
        normed, inverse = norm_rows(summed)
        normed_attn_ref[...] = normed
        inverse_attn_ref[...] = inverse
        middle = normed * vectors_ref[0:1, :] + vectors_ref[1:2, :]
        mid_ref[...] = middle
        mid_low_ref[...] = middle.astype(BF)
        total_ref[...] = middle

    before = mm(mid_low_ref[...], w_in_ref[...].reshape(width, chunk))
    bell = 0.5 * (1.0 + lax.erf(before * inv_root_two))
    active = (before * bell).astype(BF)
    slope = (bell + before * jnp.exp(-0.5 * before * before) * inv_root_two_pi).astype(BF)

    @pl.when(step < 2)
    def _():
        send_ref[0] = active
        send_ref[1] = slope

    @pl.when(step >= 2)
    def _():
        keep_ref[0] = active
        keep_ref[1] = slope

    total_ref[...] += mm(active, w_out_ref[...].reshape(chunk, width))

    @pl.when(step == 3)
    def _():
        normed, inverse = norm_rows(total_ref[...])
        normed_ffn_ref[...] = normed
        inverse_ffn_ref[...] = inverse
        result = normed * vectors_ref[2:3, :] + vectors_ref[3:4, :]
        result_ref[...] = result
        low_ref[...] = result.astype(BF)


def ffn_forward(places, parts, vectors, packed):
    rows = parts[0].shape[0]
    width, chunk = packed.width, packed.units // 4

    def chunks(step, places):
        return ((step // 2 + 1 + places[0]) % 2, step % 2, 0)

    block = (rows, width)
    kept = (2, rows, chunk)
    return pl.pallas_call(
        functools.partial(ffn_forward_kernel, len(parts)),
        grid_spec=pltpu.PrefetchScalarGridSpec(
            num_scalar_prefetch=1,
            grid=(4,),
            in_specs=[whole(block)] * len(parts)
            + [whole(vectors.shape), packed.in_spec(1, chunks), packed.out_spec(1, chunks)],
            out_specs=[
                whole(block), whole(block), whole(block),
                whole(block), whole((rows, 1)), whole(block), whole((rows, 1)),
                pl.BlockSpec(kept, lambda i, p: (0, 0, jnp.minimum(i, 1))),
                pl.BlockSpec(kept, lambda i, p: (0, 0, jnp.maximum(i - 2, 0))),
            ],
            scratch_shapes=[pltpu.VMEM(block, F32), pltpu.VMEM(block, F32)],
        ),
        out_shape=[
            struct(block, F32), struct(block, BF), struct(block, BF),
            struct(block, F32), struct((rows, 1), F32), struct(block, F32), struct((rows, 1), F32),
            struct((2, rows, 2 * chunk), BF), struct((2, rows, 2 * chunk), BF),
        ],
        compiler_params=PARAMS,
        cost_estimate=FREE,
    )(places, *parts, vectors, packed.fc_in, packed.fc_out)


def ffn_backward_kernel(place_ref, *refs):
    g_own, g_sib, m_own, m_sib, a_own, a_sib, w_in_ref, w_out_ref = refs[:8]
    own_ref, sib_ref, in_send, in_keep, out_send, out_keep, total_ref = refs[8:]
    step = pl.program_id(0)
    rows, width = g_own.shape
    chunk = a_own.shape[2]
    grads = jnp.concatenate([g_own[...], g_sib[...]], axis=0)
    w_in = w_in_ref[...].reshape(width, chunk)
    slope = jnp.concatenate([a_own[1], a_sib[1]], axis=0).astype(F32)
    before_grad = (mm_t(grads, w_out_ref[...].reshape(chunk, width)) * slope).astype(BF)
    part = mm_t(before_grad, w_in)

    @pl.when(step == 0)
    def _():
        total_ref[...] = part

    @pl.when(step > 0)
    def _():
        total_ref[...] += part

    half = width // 2
    for mine, ref in ((1 - place_ref[1], in_send), (place_ref[1], in_keep)):
        lanes = pl.ds(pl.multiple_of(mine * half, half), half)
        middle = jnp.concatenate([m_own[:, lanes], m_sib[:, lanes]], axis=0)
        ref[...] = mm_outer(middle, before_grad, BF).reshape(ref.shape)
    active = jnp.concatenate([a_own[0], a_sib[0]], axis=0)
    out_grad = mm_outer(active, grads, BF)

    @pl.when(step < 2)
    def _():
        out_send[0] = out_grad

    @pl.when(step >= 2)
    def _():
        out_keep[0] = out_grad

    @pl.when(step == 3)
    def _():
        own_ref[...] = total_ref[:rows, :]
        sib_ref[...] = total_ref[rows:, :].astype(BF)


def ffn_backward(places, grads, middles, actives, packed):
    rows, width = grads[0].shape
    chunk = packed.units // 8

    def chunks(step, places):
        return (places[0], step % 2, (step // 2 + 1 + places[2]) % 2)

    def column(step, places):
        return step % 2 * 2 + (step // 2 + 1 + places[2]) % 2

    block = (rows, width)
    kept = pl.BlockSpec((2, rows, chunk), lambda i, p: (0, 0, column(i, p)))
    rows_each = packed.rows * 2
    groups = width // 2 // rows_each if rows_each % 16 == 0 else 1
    tall = (groups, 2, width // 2 // groups, 2 * chunk)
    side = pl.BlockSpec(
        (groups, 1, tall[2], chunk), lambda i, p: (0, column(i, p) // 2, 0, column(i, p) % 2)
    )
    return pl.pallas_call(
        ffn_backward_kernel,
        grid_spec=pltpu.PrefetchScalarGridSpec(
            num_scalar_prefetch=1,
            grid=(4,),
            in_specs=[whole(block)] * 4
            + [kept, kept, packed.in_spec(2, chunks), packed.out_spec(2, chunks)],
            out_specs=[
                whole(block), whole(block), side, side,
                pl.BlockSpec((1, chunk, width), lambda i, p: (jnp.minimum(i, 1), 0, 0)),
                pl.BlockSpec((1, chunk, width), lambda i, p: (jnp.maximum(i - 2, 0), 0, 0)),
            ],
            scratch_shapes=[pltpu.VMEM((2 * rows, width), F32)],
        ),
        out_shape=[
            struct(block, F32), struct(block, BF),
            struct(tall, BF), struct(tall, BF),
            struct((2, chunk, width), BF), struct((2, chunk, width), BF),
        ],
        compiler_params=PARAMS,
        cost_estimate=FREE,
    )(places, *grads, *middles, *actives, packed.fc_in, packed.fc_out)


def scatter_ffn(plan, order, early, in_send, in_keep, out_send, out_keep):
    hi, lo, half = ("fsdp", plan.hi), ("fsdp", plan.lo), ("seq", plan.ranks)
    inner = [("fsdp", b) for b in reversed(plan.f_bits) if b not in (plan.hi, plan.lo)]
    z_names = [("seq", b) for b in reversed(plan.z_bits)]
    tail = (*inner, half, *z_names)
    width = out_keep.shape[-1]
    count = 2 ** (1 + len(tail))
    if in_keep.shape[0] == 1:
        shape = in_keep.shape

        def spread_rows(value):
            value = value.reshape(2, count, shape[2] // count, width)
            return jnp.swapaxes(value, 0, 1)

        in_send, in_keep = spread_rows(in_send), spread_rows(in_keep)

    def summed(first, keep, there):
        shape = (2,) * (1 + len(tail)) + (-1, width)
        return Sum(plan, order, (first, *tail), [keep.reshape(shape), there.reshape(shape)])

    first = summed(lo, in_keep, plan.swap(in_send, *hi))
    second = summed(hi, out_keep, plan.swap(out_send, *lo))
    yield
    first_names = [lo, *inner, *z_names]
    if early:
        first_names = [*z_names, lo, *inner]
    steps = list(zip(first_names, [hi, *inner, *z_names])) + [(half, half)]
    for one, two in steps:
        if one == two:
            first.tie()
            second.tie()
            send = jnp.stack([first.sending(one), second.sending(one)])
            there = plan.swap(order.done(send), *one)
            first.receive(there[0])
            second.receive(there[1])
        else:
            first.step(one)
            second.step(two)
        yield
        if not early and one in z_names:
            first.tie()
            second.tie()
            order.done(second.parts[-1][0])
            yield
    first.tie()
    second.tie()
    fc_in = first.total().astype(BF).reshape(2, 2, -1, width)
    here, send = choose(plan.core, fc_in, 1)
    there = plan.swap(order.done(send), "seq", 1)
    fc_out = order.done(second.total())
    yield
    here, there = order.tie(here, there)
    rows = here.shape[1]
    pair = [jnp.swapaxes(v, 0, 1).reshape(rows, plan.n // 2, -1) for v in (here, there)]
    fc_in = stack_by(plan.core, *pair, 2)
    return order.done(fc_in.reshape(rows, -1).astype(F32)), fc_out


def gather_vectors(plan, order, vectors):
    layers, count, own = vectors.shape
    value = order.done(vectors.reshape(1, -1))
    names = [("seq", b) for b in [1] + plan.z_bits + [plan.ranks]]
    names += [("fsdp", b) for b in plan.f_bits]
    for name in names:
        there = plan.swap(value, *name)
        yield
        value, there = order.tie(value, there)
        mine = bit_of(plan.f if name[0] == "fsdp" else plan.s, name[1])
        value = order.done(stack_by(mine, value, there, 0).reshape(-1, value.shape[-1]))
    value = value.reshape(plan.n, layers, count, own)
    return jnp.transpose(value, (1, 2, 0, 3)).reshape(layers, count, -1).astype(F32)


def sum_vectors(plan, vectors):
    count, width = vectors.shape
    value = vectors.reshape(count, plan.n, width // plan.n)
    value = jnp.transpose(value, (1, 0, 2)).reshape(plan.n, -1)
    value = lax.all_to_all(value, ALL, split_axis=0, concat_axis=0, tiled=True)
    return jnp.sum(value, axis=0).reshape(count, width // plan.n)


def local(
    mesh_shape,
    inputs,
    segment_ids,
    query_weight,
    key_weight,
    value_weight,
    out_weight,
    fc_in_weight,
    fc_out_weight,
    attn_gain,
    attn_shift,
    ffn_gain,
    ffn_shift,
    cotangent,
):
    layers, _, width = query_weight.shape
    plan = Plan(mesh_shape, width, fc_in_weight.shape[2])
    places = plan.scalars()
    head_dim = width // HEADS

    def to_halves(value):
        mine, other = choose(plan.half, value, 0)
        return jnp.concatenate([mine, plan.swap(other, "seq", plan.ranks)], axis=0)

    def from_halves(value):
        size = value.shape[0] // 2
        there = plan.swap(value[size:].astype(BF), "seq", plan.ranks).astype(F32)
        return stack_by(plan.half, value[:size], there, 0)

    order, tasks = Order(), Tasks()
    matrices = (query_weight, key_weight, value_weight, out_weight)
    if plan.fast:
        columns = tasks.add(rank_columns(plan, order, matrices))
    x_low = to_halves(inputs)
    packed = [Packed(plan, fc_in_weight[k], fc_out_weight[k]) for k in range(layers)]
    if plan.fast:
        tasks.drain(columns)
        here, there, out = columns.result

        def fetch(layer):
            parts = (here[layer], there[layer], out[layer])
            return tasks.add(gather_attention(plan, order, places, parts))

        attention = [fetch(0)]
    (x_low,) = order.tie(x_low)
    x_pieces = group_pieces(plan, order.done(x_low))
    ids = jnp.concatenate(group_pieces(plan, to_halves(segment_ids)), axis=0)
    vectors = jnp.stack([attn_gain, attn_shift, ffn_gain, ffn_shift], axis=1)
    vectors = tasks.add(gather_vectors(plan, order, vectors))
    upstream = [to_halves(cotangent)]
    tokens = x_low.shape[0]
    if plan.fast:
        tasks.run(attention[0])
        tasks.run(vectors)
        tasks.drain(attention[0])
        attention += [fetch(k) for k in range(1, layers)]
    else:
        attention = [Task.finished(m) for m in gather_attention_whole(plan, matrices)]

    hidden = x_low
    records = []
    for layer in range(layers):
        tasks.drain(attention[layer])
        w_qkv, w_out = attention[layer].result
        tied = order.tie(*x_pieces, w_qkv, w_out, ids)
        x_pieces = tied[:-3]
        qkv, att, keep, send = attn_forward(x_pieces, *tied[-3:], head_dim)
        order.done(send)
        parts = group_sum(plan, order, keep, send)
        tasks.drain(vectors)
        if layer + 1 < layers:
            tasks.run(attention[layer + 1])
        tied = order.tie(hidden, *parts, *upstream)
        upstream = tied[1 + len(parts) :]
        (
            hidden, x_low, mid_low, normed_attn, inverse_attn, normed_ffn, inverse_ffn, send, keep,
        ) = ffn_forward(places, tied[: 1 + len(parts)], vectors.result[layer], packed[layer])
        order.done(x_low)
        next_pieces = group_pieces(plan, x_low) if layer + 1 < layers else None
        middles = (mid_low, plan.swap(mid_low, "seq", 1))
        actives = (keep, plan.swap(send, "seq", 1))
        records.append(
            (x_pieces, qkv, att, normed_attn, inverse_attn, normed_ffn, inverse_ffn, actives, middles)
        )
        x_pieces = next_pieces
    outputs = from_halves(hidden)

    grads, vector_grads = [None] * layers, [None] * layers
    older = ()
    for layer in reversed(range(layers)):
        (
            x_pieces, qkv, att, normed_attn, inverse_attn, normed_ffn, inverse_ffn, actives, middles,
        ) = records[layer]
        gains = vectors.result[layer]
        w_qkv, w_out = attention[layer].result
        sum_grad, ff_grad, gain_ffn_grad, shift_ffn_grad = norm_backward(
            order.tie(*upstream), normed_ffn, inverse_ffn, gains[2:3]
        )
        order.done(ff_grad)
        ff_sibling = plan.swap(ff_grad, "seq", 1)
        if older:
            older[0].run()
        tied = order.tie(ff_grad, ff_sibling, *middles, *actives)
        own, sibling, *ffn_grads = ffn_backward(
            places, tied[:2], tied[2:4], tied[4:], packed[layer]
        )
        order.done(sibling)
        ffn_task = tasks.add(scatter_ffn(plan, order, layer == 0, *ffn_grads))
        sibling = plan.swap(sibling, "seq", 1)
        if older:
            older[0].run()
            older[1].run()
        tied = order.tie(sum_grad, own, sibling)
        attn_sum_grad, branch_grad, gain_attn_grad, shift_attn_grad = norm_backward(
            tied, normed_attn, inverse_attn, gains[0:1]
        )
        order.done(branch_grad)
        g_pieces = group_pieces(plan, branch_grad)
        vector_grads[layer] = (gain_attn_grad, shift_attn_grad, gain_ffn_grad, shift_ffn_grad)
        g_pieces = order.tie(*g_pieces)
        order.done(g_pieces[-1])
        if older:
            older[0].run()
        else:
            (outputs,) = order.tie(outputs)
            order.done(outputs)
        tied = order.tie(*g_pieces, qkv)
        g_pieces = tied[:-1]
        dqkv, keep, send = attn_backward(g_pieces, tied[-1], w_qkv, w_out, ids, head_dim)
        order.done(send)
        ffn_task.run()
        upstream = [attn_sum_grad] + group_sum(plan, order, keep, send)
        attn_task = tasks.add(
            scatter_attention(plan, order, places, x_pieces, g_pieces, dqkv, att, plan.fast)
        )
        grads[layer] = (ffn_task, attn_task)
        if layer > 0:
            older = grads[layer]
    rows_grad = add_parts(order.tie(*upstream), tokens)
    order.done(rows_grad)
    input_grad = from_halves(rows_grad)
    summed = jnp.concatenate([v for member in vector_grads for v in member], axis=0)
    (summed,) = order.tie(summed)
    summed = order.done(sum_vectors(plan, summed))
    if older:
        older[0].run()
    ffn_task.run()
    if older:
        older[1].run()
    attn_task.run()
    (input_grad,) = order.tie(input_grad)
    order.done(input_grad)
    ffn_task.run()
    tasks.finish()
    grads = [(*a.result, *f.result) for f, a in grads]
    summed = summed.reshape(layers, 4, -1)
    merged = [jnp.stack([g[k] for g in grads]) for k in range(6)]
    return (outputs, input_grad, *merged, *(summed[:, k] for k in range(4)))


def solution(mesh):
    tokens = P("fsdp", "seq", None)
    matrix = P(None, ("fsdp", "seq"), None)
    vector = P(None, ("fsdp", "seq"))
    return jax.shard_map(
        functools.partial(local, dict(mesh.shape)),
        mesh=mesh,
        in_specs=(tokens, P("fsdp", "seq"), *[matrix] * 6, *[vector] * 4, tokens),
        out_specs=(tokens, tokens, *[matrix] * 6, *[vector] * 4),
        check_vma=False,
    )
```

```python
import functools

import jax
import jax.numpy as jnp
from jax import lax
from jax.experimental import pallas as pl
from jax.experimental.pallas import tpu as pltpu
from jax.sharding import PartitionSpec as P

HEADS = 16
NEG_FILL = -1e30
NORM_EPS = 1e-05
inv_root_two = 0.7071067811865476
inv_root_two_pi = 0.3989422804014327
BF = jnp.bfloat16
F32 = jnp.float32
ALL = ("fsdp", "seq")
PARAMS = pltpu.CompilerParams(vmem_limit_bytes=56 * 1024 * 1024)


def mm(a, b, out=F32):
    return lax.dot_general(a, b, (((1,), (0,)), ((), ())), preferred_element_type=F32).astype(out)


def mm_t(a, b, out=F32):
    return lax.dot_general(a, b, (((1,), (1,)), ((), ())), preferred_element_type=F32).astype(out)


def mm_outer(a, b, out=F32):
    return lax.dot_general(a, b, (((0,), (0,)), ((), ())), preferred_element_type=F32).astype(out)


def struct(shape, dtype):
    return jax.ShapeDtypeStruct(shape, dtype)


def whole(shape):
    return pl.BlockSpec(shape, lambda *_: (0,) * len(shape))


FREE = pl.CostEstimate(flops=0, bytes_accessed=0, transcendentals=0)


class Plan:
    def __init__(self, mesh_shape, width, hidden_units):
        self.n_f, self.n_s = mesh_shape["fsdp"], mesh_shape["seq"]
        self.n = self.n_f * self.n_s
        self.ranks = self.n_s // 2
        self.f = lax.axis_index("fsdp")
        self.s = lax.axis_index("seq")
        self.half = self.s // self.ranks
        self.rank = self.s % self.ranks
        self.core = self.s % 2
        self.f_bits = [1 << k for k in range(self.n_f.bit_length() - 1)]
        self.z_bits = [1 << k for k in range(1, self.ranks.bit_length() - 1)]
        self.hi, self.lo = self.f_bits[-1], self.f_bits[-2]
        self.f_hi, self.f_lo = bit_of(self.f, self.hi), bit_of(self.f, self.lo)
        self.fast = (
            self.n_f == 4
            and self.n_s == 8
            and (width // self.n) % 32 == 0
            and (hidden_units // self.n) % 128 == 0
        )

    def swap(self, value, axis_name, bit):
        count = self.n_f if axis_name == "fsdp" else self.n_s
        return lax.ppermute(value, axis_name, [(i, i ^ bit) for i in range(count)])

    def scalars(self):
        return jnp.stack([self.core, self.f_hi, self.f_lo, self.f * 2 + self.half, self.rank]).astype(
            jnp.int32
        )


def bit_of(index, bit):
    return (index // bit) % 2


def stack_by(mine, here, there, axis):
    return jnp.where(
        mine == 0, jnp.stack([here, there], axis=axis), jnp.stack([there, here], axis=axis)
    )


def choose(mine, value, axis):
    first = lax.index_in_dim(value, 0, axis, keepdims=False)
    second = lax.index_in_dim(value, 1, axis, keepdims=False)
    return jnp.where(mine == 0, first, second), jnp.where(mine == 0, second, first)


def group_pieces(plan, value):
    pieces = [value]
    for bit in plan.z_bits:
        pieces = pieces + [plan.swap(p, "seq", bit) for p in pieces]
    return pieces + [plan.swap(p, "seq", 1) for p in pieces]


def group_sum(plan, order, keep, there):
    parts = [keep, there]
    size = keep.shape[0]
    for bit in reversed(plan.z_bits):
        size = size // 2
        tied = order.tie(*parts)
        out = sum(p[size : 2 * size].astype(F32) for p in tied).astype(BF)
        parts = parts + [plan.swap(order.done(out), "seq", bit)]
    return parts


def add_parts(parts, rows):
    return sum(p[:rows].astype(F32) for p in parts)


class Order:
    def __init__(self):
        self.last = None

    def tie(self, *values):
        if self.last is None:
            return values
        return lax.optimization_barrier((*values, self.last))[:-1]

    def done(self, value):
        self.last = value
        return value


class Task:
    def __init__(self, steps):
        self.steps, self.result, self.running = steps, None, True
        self.run()

    @staticmethod
    def finished(result):
        task = Task(iter(()))
        task.result = result
        return task

    def run(self):
        if self.running:
            try:
                next(self.steps)
            except StopIteration as stop:
                self.running, self.result = False, stop.value


class Tasks:
    def __init__(self):
        self.open = []

    def add(self, steps):
        task = Task(steps)
        self.open.append(task)
        return task

    def run(self, task):
        task.run()

    def drain(self, task):
        while task.running:
            task.run()

    def slot(self, count):
        self.open = [t for t in self.open if t.running]
        for task in self.open[:count]:
            task.run()

    def finish(self):
        while self.open:
            self.slot(len(self.open))


class Sum:
    def __init__(self, plan, order, names, parts):
        self.plan, self.order, self.names = plan, order, tuple(names)
        self.parts = [(p, self.names) for p in parts]
        self.chosen = {}

    def pick(self, part, chosen):
        value, names = part
        rest = value.shape[len(names) :]
        zero = jnp.zeros((), jnp.int32)
        start = [chosen.get(n, zero) for n in names] + [zero] * len(rest)
        size = [1 if n in chosen else 2 for n in names] + list(rest)
        left = [d for n, d in zip(names, size) if n not in chosen]
        return lax.dynamic_slice(value, start, size).reshape(*left, *rest)

    def tie(self):
        tied = self.order.tie(*[p for p, _ in self.parts])
        self.parts = [(p, names) for p, (_, names) in zip(tied, self.parts)]

    def sending(self, name, kind=BF):
        plan = self.plan
        mine = bit_of(plan.f if name[0] == "fsdp" else plan.s, name[1]).astype(jnp.int32)
        there = {**self.chosen, name: 1 - mine}
        out = sum(self.pick(p, there).astype(F32) for p in self.parts).astype(kind)
        self.chosen[name] = mine
        return out

    def receive(self, value):
        left = [n for n in self.names if n not in self.chosen]
        self.parts.append((value, tuple(left)))

    def step(self, name):
        self.tie()
        send = self.order.done(self.sending(name))
        self.receive(self.plan.swap(send, *name))

    def settle(self):
        self.tie()
        self.order.done(self.parts[-1][0])

    def total(self):
        return sum(self.pick(p, self.chosen).astype(F32) for p in self.parts)


def norm_rows(summed):
    center = jnp.mean(summed, axis=-1, keepdims=True)
    offset = summed - center
    spread = jnp.mean(offset * offset, axis=-1, keepdims=True)
    inverse = lax.rsqrt(spread + NORM_EPS)
    return offset * inverse, inverse


def norm_backward_kernel(count, *refs):
    parts, (normed_ref, inverse_ref, gain_ref) = refs[:count], refs[count : count + 3]
    out_ref, low_ref, gain_grad_ref, shift_grad_ref = refs[count + 3 :]
    upstream = parts[0][...].astype(F32)
    for part in parts[1:]:
        upstream = upstream + part[...].astype(F32)
    normed = normed_ref[...]
    gain_grad_ref[...] = jnp.sum(upstream * normed, axis=0, keepdims=True)
    shift_grad_ref[...] = jnp.sum(upstream, axis=0, keepdims=True)
    scaled = upstream * gain_ref[...]
    inner = (
        scaled
        - jnp.mean(scaled, axis=-1, keepdims=True)
        - normed * jnp.mean(scaled * normed, axis=-1, keepdims=True)
    )
    result = inner * inverse_ref[...]
    out_ref[...] = result
    low_ref[...] = result.astype(BF)


def norm_backward(parts, normed, inverse, gain):
    rows, width = normed.shape
    return pl.pallas_call(
        functools.partial(norm_backward_kernel, len(parts)),
        grid=(1,),
        in_specs=[whole((rows, width))] * (len(parts) + 1) + [whole((rows, 1)), whole((1, width))],
        out_specs=[whole((rows, width))] * 2 + [whole((1, width))] * 2,
        out_shape=[
            struct((rows, width), F32), struct((rows, width), BF),
            struct((1, width), F32), struct((1, width), F32),
        ],
        compiler_params=PARAMS,
        cost_estimate=FREE,
    )(*parts, normed, inverse, gain)


def pick_head(lanes, head, head_dim):
    return (lanes >= head * head_dim) & (lanes < (head + 1) * head_dim)


def attn_forward_kernel(head_dim, count, *refs):
    pieces = refs[:count]
    w_qkv_ref, w_out_ref, ids_q_ref, ids_k_ref = refs[count : count + 4]
    qkv_ref, att_ref, keep_ref, send_ref = refs[count + 4 :]
    step = pl.program_id(0)
    rows, width = att_ref.shape

    @pl.when(step == 0)
    def _():
        w_qkv = w_qkv_ref[...]
        for index, piece in enumerate(pieces):
            qkv = mm(piece[...], w_qkv).astype(BF)
            part = pl.ds(index * rows, rows)
            qkv_ref[part, :width] = (qkv[:, :width].astype(F32) * head_dim**-0.5).astype(BF)
            qkv_ref[part, width:] = qkv[:, width:]

    queries = qkv_ref[pl.ds(pl.multiple_of(step * rows, rows), rows), :width]
    keys, values = qkv_ref[:, width : 2 * width], qkv_ref[:, 2 * width :]
    lanes = lax.broadcasted_iota(jnp.int32, (1, width), 1)
    allowed = ids_q_ref[...] == ids_k_ref[...]
    total = jnp.zeros((rows, width), F32)
    for head in range(width // head_dim):
        here = pick_head(lanes, head, head_dim)
        scores = mm_t(jnp.where(here, queries, jnp.zeros_like(queries)), keys)
        scores = jnp.where(allowed, scores, NEG_FILL)
        weights = jnp.exp(scores - jnp.max(scores, axis=1, keepdims=True))
        norm = 1.0 / jnp.sum(weights, axis=1, keepdims=True)
        total = jnp.where(here, mm(weights.astype(BF), values) * norm, total)
    attended = total.astype(BF)
    att_ref[...] = attended
    branch = mm(attended, w_out_ref[...])

    @pl.when(step < count // 2)
    def _():
        keep_ref[...] = branch

    @pl.when(step >= count // 2)
    def _():
        send_ref[...] = branch.astype(BF)


def attn_forward(pieces, w_qkv, w_out, ids, head_dim):
    count = len(pieces)
    rows, features = pieces[0].shape
    tokens, width = count * rows, w_out.shape[0]
    half = count // 2
    heads = width // head_dim
    return pl.pallas_call(
        functools.partial(attn_forward_kernel, head_dim, count),
        grid=(count,),
        in_specs=[whole((rows, features))] * count
        + [
            whole(w_qkv.shape),
            whole(w_out.shape),
            pl.BlockSpec((rows, 1), lambda i: (i, 0)),
            whole((1, tokens)),
        ],
        out_specs=[
            whole((tokens, 3 * width)),
            pl.BlockSpec((rows, width), lambda i: (i, 0)),
            pl.BlockSpec((rows, features), lambda i: (jnp.minimum(i, half - 1), 0)),
            pl.BlockSpec((rows, features), lambda i: (jnp.maximum(i - half, 0), 0)),
        ],
        out_shape=[
            struct((tokens, 3 * width), BF),
            struct((tokens, width), BF),
            struct((half * rows, features), F32),
            struct((half * rows, features), BF),
        ],
        compiler_params=PARAMS,
        cost_estimate=FREE,
    )(*pieces, w_qkv, w_out, ids.reshape(tokens, 1), ids.reshape(1, tokens))


def attn_backward_kernel(head_dim, count, *refs):
    pieces = refs[:count]
    qkv_ref, w_qkv_ref, w_out_ref, ids_q_ref, ids_k_ref = refs[count : count + 5]
    dqkv_ref, keep_ref, send_ref, grad_ref, dk_ref, dv_ref = refs[count + 5 :]
    step = pl.program_id(0)
    rows = pieces[0].shape[0]
    width = grad_ref.shape[1]

    @pl.when(step == 0)
    def _():
        w_out = w_out_ref[...]
        for index, piece in enumerate(pieces):
            grad_ref[pl.ds(index * rows, rows), :] = mm_t(piece[...], w_out, BF)
        dk_ref[...] = jnp.zeros_like(dk_ref)
        dv_ref[...] = jnp.zeros_like(dv_ref)

    place = pl.ds(pl.multiple_of(step * rows, rows), rows)
    queries, grads = qkv_ref[place, :width], grad_ref[place, :]
    keys, values = qkv_ref[:, width : 2 * width], qkv_ref[:, 2 * width :]
    lanes = lax.broadcasted_iota(jnp.int32, (1, width), 1)
    allowed = ids_q_ref[...] == ids_k_ref[...]
    dq = jnp.zeros((rows, width), F32)
    for head in range(width // head_dim):
        here = pick_head(lanes, head, head_dim)
        q_head = jnp.where(here, queries, jnp.zeros_like(queries))
        g_head = jnp.where(here, grads, jnp.zeros_like(grads))
        scores = mm_t(q_head, keys)
        scores = jnp.where(allowed, scores, NEG_FILL)
        weights = jnp.exp(scores - jnp.max(scores, axis=1, keepdims=True))
        probs = weights * (1.0 / jnp.sum(weights, axis=1, keepdims=True))
        prob_grad = mm_t(g_head, values)
        product = probs * prob_grad
        delta = jnp.sum(product, axis=1, keepdims=True)
        score_grad = (product - probs * delta).astype(BF)
        dq = jnp.where(here, mm(score_grad, keys), dq)
        dk_ref[...] += mm_outer(score_grad, q_head)
        dv_ref[...] += mm_outer(probs.astype(BF), g_head)
    dqkv_ref[place, :width] = (dq * head_dim**-0.5).astype(BF)

    @pl.when(step == count - 1)
    def _():
        dqkv_ref[:, width : 2 * width] = dk_ref[...].astype(BF)
        dqkv_ref[:, 2 * width :] = dv_ref[...].astype(BF)
        w_qkv = w_qkv_ref[...]
        half = count // 2
        for index in range(count):
            part = mm_t(dqkv_ref[pl.ds(index * rows, rows), :], w_qkv)
            if index < half:
                keep_ref[pl.ds(index * rows, rows), :] = part
            else:
                send_ref[pl.ds((index - half) * rows, rows), :] = part.astype(BF)


def attn_backward(pieces, qkv, w_qkv, w_out, ids, head_dim):
    count = len(pieces)
    rows, features = pieces[0].shape
    tokens, width = count * rows, w_out.shape[0]
    heads = width // head_dim
    half = tokens // 2
    return pl.pallas_call(
        functools.partial(attn_backward_kernel, head_dim, count),
        grid=(count,),
        in_specs=[whole((rows, features))] * count
        + [
            whole(qkv.shape),
            whole(w_qkv.shape),
            whole(w_out.shape),
            pl.BlockSpec((rows, 1), lambda i: (i, 0)),
            whole((1, tokens)),
        ],
        out_specs=[
            whole((tokens, 3 * width)), whole((half, features)), whole((half, features)),
        ],
        out_shape=[
            struct((tokens, 3 * width), BF), struct((half, features), F32),
            struct((half, features), BF),
        ],
        scratch_shapes=[
            pltpu.VMEM((tokens, width), BF),
            pltpu.VMEM((tokens, width), F32),
            pltpu.VMEM((tokens, width), F32),
        ],
        compiler_params=PARAMS,
        cost_estimate=FREE,
    )(*pieces, qkv, w_qkv, w_out, ids.reshape(tokens, 1), ids.reshape(1, tokens))


def attn_weights_kernel(count, place_ref, *refs):
    x_refs, g_refs = refs[:count], refs[count : 2 * count]
    dqkv_ref, att_ref, extra_ref = refs[2 * count : 2 * count + 3]
    a_send, a_keep, b_send, b_keep, out_ref = refs[2 * count + 3 :]
    block = pl.program_id(0)
    rows = x_refs[0].shape[0]
    width = att_ref.shape[1]
    small = out_ref.shape[0] // pl.num_programs(0)
    height = 4 * small

    @pl.when(block == 0)
    def _():
        total = None
        for index in range(count):
            part = mm_outer(att_ref[pl.ds(index * rows, rows), :], g_refs[index][...])
            total = part if total is None else total + part
        out_ref[...] = total.astype(BF)

    lanes = pl.ds(pl.multiple_of(block * height, height), height)
    grad = None
    for index in range(count):
        part = mm_outer(x_refs[index][:, lanes], dqkv_ref[pl.ds(index * rows, rows), :])
        grad = part if grad is None else grad + part
    grad = grad.astype(BF)
    hi, lo, low = block // 4, (block // 2) % 2, block % 2

    def put_a(ref, place):
        ref[place, :height, :] = grad[:, :width]
        ref[place, height : 2 * height, :] = grad[:, width : 2 * width]

    def put_b(ref, place):
        ref[place, :height, :] = grad[:, 2 * width :]
        part = out_ref[pl.ds(pl.multiple_of(block * small, small), small), :]
        for piece in range(4):
            start = height + piece * small
            ref[place, start : start + small, :] = part[:, piece * width : (piece + 1) * width]
        ref[place, 2 * height :, :] = extra_ref[0]

    pl.when(hi != place_ref[1])(lambda: put_a(a_send, lo * 2 + low))
    pl.when(hi == place_ref[1])(lambda: put_a(a_keep, lo * 2 + low))
    pl.when(lo != place_ref[2])(lambda: put_b(b_send, hi * 2 + low))
    pl.when(lo == place_ref[2])(lambda: put_b(b_keep, hi * 2 + low))


def attn_weights(places, x_pieces, g_pieces, dqkv, att, extra):
    count = len(x_pieces)
    rows, features = x_pieces[0].shape
    width = att.shape[1]
    high = 2 * features // 8
    parts = [(4, high, width)] * 2 + [(4, high + extra.shape[1], width)] * 2
    return pl.pallas_call(
        functools.partial(attn_weights_kernel, count),
        grid_spec=pltpu.PrefetchScalarGridSpec(
            num_scalar_prefetch=1,
            grid=(8,),
            in_specs=[whole((rows, features))] * (2 * count)
            + [
                whole(dqkv.shape),
                whole(att.shape),
                pl.BlockSpec((1,) + extra.shape[1:], lambda i, p: (i, 0, 0)),
            ],
            out_specs=[whole(p) for p in parts],
            scratch_shapes=[pltpu.VMEM((width, features), BF)],
        ),
        out_shape=[struct(p, BF) for p in parts],
        compiler_params=PARAMS,
        cost_estimate=FREE,
    )(places, *x_pieces, *g_pieces, dqkv, att, extra)


def assemble_kernel(place_ref, a_own, a_other, b_own, b_other, qkv_ref, out_ref):
    own, rank = place_ref[3], place_ref[4]
    height, width = a_own.shape[1] // 8, a_own.shape[2]
    ranks = 4
    for block in range(8):
        a_ref = a_own if block < 4 else a_other
        b_ref = b_own if block < 4 else b_other
        b_block = (block % 4) // 2 * 4 + block // 4 * 2 + block % 2
        for inner in range(4):
            rank_there = rank ^ ((inner // 2) + (inner % 2) * 2)
            start = ((own ^ block) * ranks + rank_there) * height
            place = pl.ds(pl.multiple_of(start, height), height)
            qkv_ref[place, :width] = a_ref[block % 4, inner * height : (inner + 1) * height, :]
            first = (4 + inner) * height
            qkv_ref[place, width : 2 * width] = a_ref[block % 4, first : first + height, :]
            start = ((own ^ b_block) * ranks + rank_there) * height
            place = pl.ds(pl.multiple_of(start, height), height)
            qkv_ref[place, 2 * width :] = b_ref[block % 4, inner * height : (inner + 1) * height, :]
            place = pl.ds(pl.multiple_of((own ^ b_block) * height, height), height)
            out_ref[place, inner * width : (inner + 1) * width] = b_ref[
                block % 4, first : first + height, :
            ]


def assemble(places, a_own, a_other, b_own, b_other):
    _, high, width = a_own.shape
    features = 4 * high
    return pl.pallas_call(
        assemble_kernel,
        grid_spec=pltpu.PrefetchScalarGridSpec(
            num_scalar_prefetch=1,
            grid=(1,),
            in_specs=[whole(a_own.shape)] * 4,
            out_specs=[whole((features, 3 * width)), whole((width, features))],
        ),
        out_shape=[struct((features, 3 * width), BF), struct((width, features), BF)],
        compiler_params=PARAMS,
        cost_estimate=FREE,
    )(places, a_own, a_other, b_own, b_other)


def spread_pairs(plan):
    pairs = []
    for shard in range(plan.n):
        rank, block = shard // (2 * plan.n_f), shard % (2 * plan.n_f)
        pairs.append((shard, block // 2 * plan.n_s + block % 2 * plan.ranks + rank))
    return pairs


def gather_attention_whole(plan, matrices):
    layers, _, cols = matrices[0].shape
    size = cols // plan.ranks
    result = []
    for layer in range(layers):
        full = [lax.all_gather(m[layer], ALL, axis=0, tiled=True) for m in matrices]
        qkv = [lax.dynamic_slice_in_dim(m, plan.rank * size, size, 1) for m in full[:3]]
        w_out = lax.dynamic_slice_in_dim(full[3], plan.rank * size, size, 0)
        result.append((jnp.concatenate(qkv, axis=1), w_out))
    return result


def rank_columns(plan, order, matrices):
    query, key, value, out = matrices
    layers, rows, cols = query.shape
    half = cols // 2
    upper = bit_of(plan.s, 2) == 1
    send = [jnp.where(upper, m[..., :half], m[..., half:]) for m in (query, key, value)]
    there = plan.swap(order.done(jnp.stack(send, axis=1)), "seq", 2)
    out = lax.ppermute(out, ALL, spread_pairs(plan))
    yield
    query, key, value, there = order.tie(query, key, value, there)
    here = [jnp.where(upper, m[..., half:], m[..., :half]) for m in (query, key, value)]
    both = jnp.stack([jnp.stack(here, axis=1), there], axis=2)
    quarter = half // 2
    upper = plan.core == 1
    send = jnp.where(upper, both[..., :quarter], both[..., quarter:])
    there = plan.swap(order.done(send), "seq", 1)
    here = jnp.where(upper, both[..., quarter:], both[..., :quarter])
    yield
    return here, there, out


def gather_attention(plan, order, places, columns):
    here, there, out = order.tie(*columns)
    quarter = here.shape[-1]
    qkv = jnp.stack([here, there], axis=1)
    w_out = jnp.stack([out[:, k * quarter : (k + 1) * quarter] for k in range(4)])
    bundle = jnp.concatenate([qkv.reshape(-1, quarter), w_out.reshape(-1, quarter)], axis=0)
    other = plan.swap(order.done(bundle), "seq", plan.ranks)
    yield
    bundle, other = order.tie(bundle, other)
    size = bundle.shape[0] // 2
    part_a = order.done(jnp.stack([bundle[:size], other[:size]]))
    part_b = order.done(jnp.stack([bundle[size:], other[size:]]))
    other_a = plan.swap(part_a, "fsdp", plan.lo)
    other_b = plan.swap(part_b, "fsdp", plan.hi)
    yield
    part_a, other_a, part_b, other_b = order.tie(part_a, other_a, part_b, other_b)
    part_a = order.done(jnp.concatenate([part_a, other_a], axis=0))
    part_b = order.done(jnp.concatenate([part_b, other_b], axis=0))
    other_a = plan.swap(part_a, "fsdp", plan.hi)
    other_b = plan.swap(part_b, "fsdp", plan.lo)
    yield
    result = assemble(places, *order.tie(part_a, other_a, part_b, other_b))
    order.done(result[1])
    return result


def scatter_attention_whole(plan, x_pieces, g_pieces, dqkv, att):
    w_qkv = sum(mm_outer(x, d) for x, d in zip(x_pieces, jnp.split(dqkv, len(x_pieces))))
    w_out = sum(mm_outer(a, g) for a, g in zip(jnp.split(att, len(g_pieces)), g_pieces))
    width, features = w_out.shape
    grads = []
    for grad, axis in [(g, 1) for g in jnp.split(w_qkv, 3, axis=1)] + [(w_out, 0)]:
        full = jnp.zeros((features, features), F32)
        full = lax.dynamic_update_slice_in_dim(full, grad, plan.rank * width, axis)
        grads.append(lax.psum_scatter(full, ALL, scatter_dimension=0, tiled=True))
    return grads


def scatter_attention(plan, order, places, x_pieces, g_pieces, dqkv, att, extra, last):
    count = len(x_pieces)
    tied = order.tie(*x_pieces, *g_pieces, dqkv, att)
    grads = attn_weights(places, tied[:count], tied[count : 2 * count], *tied[2 * count :], extra)
    order.done(grads[-1])
    half = ("seq", plan.ranks)
    a_send, a_keep, b_send, b_keep = grads
    hi, lo = ("fsdp", plan.hi), ("fsdp", plan.lo)

    def summed(first, keep, there):
        parts = [p.reshape(2, 2, *keep.shape[1:]) for p in (keep, there)]
        return Sum(plan, order, (first, half), parts)

    part_a = summed(lo, a_keep, plan.swap(a_send, *hi))
    part_b = summed(hi, b_keep, plan.swap(b_send, *lo))
    yield
    part_a.step(lo)
    part_b.step(hi)
    yield
    part_a.tie()
    part_b.tie()
    send = jnp.concatenate([part_a.sending(half), part_b.sending(half)], axis=0)
    there = plan.swap(order.done(send), *half)
    high = a_send.shape[1]
    part_a.receive(there[:high])
    part_b.receive(there[high:])
    yield
    if not last:
        part_a.settle()
        yield
    part_a.tie()
    part_b.tie()
    total_b = order.done(part_b.total().astype(BF))
    return part_a.total().astype(BF), total_b


def finish_attention(plan, order, totals):
    layers = len(totals)
    high, width = totals[0][0].shape
    rows = high // 8
    parts_a = jnp.stack([a for a, _ in totals]).reshape(layers, 2, 2, 2, rows, width)
    parts_b = jnp.stack([b[:high] for _, b in totals]).reshape(layers, 2, 4, rows, width)
    out = jnp.concatenate([parts_b[:, 1, k] for k in range(4)], axis=2)
    out = lax.ppermute(out, ALL, [(b, a) for a, b in spread_pairs(plan)])
    value = parts_b[:, 0].reshape(layers, 1, 2, 2, rows, width)
    qkv = jnp.concatenate([parts_a, value], axis=1)
    extra = totals[0][1][high : high + 4].reshape(2, 2, width)

    def trade(qkv, extra, mine, axis, bit):
        here, send = choose(mine, qkv, axis)
        extra, extra_send = choose(mine, extra, 0)
        extra_send = extra_send.reshape(-1, width)
        pad = jnp.zeros((16 - extra_send.shape[0], width), BF)
        send_all = jnp.concatenate([send.reshape(-1, width), extra_send, pad], axis=0)
        there = plan.swap(order.done(send_all), "seq", bit)
        return here, extra, there

    def take(here, extra, there):
        here, extra, there = order.tie(here, extra, there)
        size = here.size // width
        count = extra.size // width
        more = there[size : size + count].reshape(extra.shape)
        return here, there[:size].reshape(here.shape), extra.astype(F32) + more.astype(F32)

    upper = bit_of(plan.s, 2)
    traded = trade(qkv, extra, upper, 2, 2)
    yield
    here, there, extra = take(*traded)
    qkv = stack_by(upper, here, there, 0)
    traded = trade(qkv, extra.astype(BF), plan.core, 3, 1)
    yield
    here, there, extra = take(*traded)
    (out,) = order.tie(out)
    qkv = stack_by(plan.core, here, there, 1)
    qkv = jnp.concatenate([qkv[0, 0], qkv[0, 1], qkv[1, 0], qkv[1, 1]], axis=3).astype(F32)
    return [qkv[:, 0], qkv[:, 1], qkv[:, 2], out.astype(F32)], extra


class Packed:
    def __init__(self, plan, fc_in, fc_out):
        rows, units = fc_in.shape
        width = fc_out.shape[1]
        own = units // plan.n
        split = fc_in.reshape(rows, plan.n // 2, 2, own)
        split = jnp.transpose(split, (2, 0, 1, 3)).reshape(2, rows, 2, units // 4)
        split = jnp.transpose(split, (0, 2, 1, 3))
        self.rows, self.width, self.units = rows, rows * plan.n, units
        self.fast = plan.fast and units // 4 == width
        if self.fast:
            flat = jnp.concatenate([split.reshape(4 * rows, width), fc_out], axis=0)
            full = lax.all_gather(flat, ALL, axis=0, tiled=True)
            self.fc_in = full.reshape(plan.n, 8, rows, width)
            self.fc_out = full.reshape(plan.n // 2, 2, 8, rows, width)
        else:
            full = lax.all_gather(split, ALL, axis=2, tiled=True)
            self.fc_in = full.reshape(1, 4, self.width, units // 4)
            full = lax.all_gather(fc_out, ALL, axis=0, tiled=True)
            full = full.reshape(plan.n // 2, 2, own, width)
            self.fc_out = jnp.transpose(full, (1, 0, 2, 3)).reshape(2, units // 2, width)

    def in_spec(self, parts, index):
        shape = self.fc_in.shape

        def place(step, places):
            core, upper, part = index(step, places)
            return (0, core * 2 + upper, 0, part)

        return pl.BlockSpec((shape[0], 1, shape[2], shape[3] // parts), place)

    def out_spec(self, parts, index):
        shape = self.fc_out.shape

        def place(step, places):
            core, upper, part = index(step, places)
            where = upper * parts + part
            return (where, core, 1, 0, 0) if self.fast else (core, where, 0)

        if self.fast:
            return pl.BlockSpec((shape[0] // 2 // parts, 1, 4, shape[3], shape[4]), place)
        return pl.BlockSpec((1, shape[1] // 2 // parts, shape[2]), place)


def ffn_forward_kernel(count, place_ref, *refs):
    parts = refs[:count]
    vectors_ref, w_in_ref, w_out_ref = refs[count : count + 3]
    (
        result_ref, low_ref, mid_low_ref, normed_attn_ref, inverse_attn_ref, normed_ffn_ref,
        inverse_ffn_ref, send_ref, keep_ref, mid_ref, total_ref,
    ) = refs[count + 3 :]
    step = pl.program_id(0)
    width = mid_ref.shape[1]
    chunk = send_ref.shape[2]

    @pl.when(step == 0)
    def _():
        summed = parts[0][...].astype(F32)
        for part in parts[1:]:
            summed = summed + part[...].astype(F32)
        normed, inverse = norm_rows(summed)
        normed_attn_ref[...] = normed
        inverse_attn_ref[...] = inverse
        middle = normed * vectors_ref[0:1, :] + vectors_ref[1:2, :]
        mid_ref[...] = middle
        mid_low_ref[...] = middle.astype(BF)
        total_ref[...] = middle

    before = mm(mid_low_ref[...], w_in_ref[...].reshape(width, chunk))
    bell = 0.5 * (1.0 + lax.erf(before * inv_root_two))
    active = (before * bell).astype(BF)
    slope = (bell + before * jnp.exp(-0.5 * before * before) * inv_root_two_pi).astype(BF)

    @pl.when(step < 2)
    def _():
        send_ref[0] = active
        send_ref[1] = slope

    @pl.when(step >= 2)
    def _():
        keep_ref[0] = active
        keep_ref[1] = slope

    total_ref[...] += mm(active, w_out_ref[...].reshape(chunk, width))

    @pl.when(step == 3)
    def _():
        normed, inverse = norm_rows(total_ref[...])
        normed_ffn_ref[...] = normed
        inverse_ffn_ref[...] = inverse
        result = normed * vectors_ref[2:3, :] + vectors_ref[3:4, :]
        result_ref[...] = result
        low_ref[...] = result.astype(BF)


def ffn_forward(places, parts, vectors, packed):
    rows = parts[0].shape[0]
    width, chunk = packed.width, packed.units // 4

    def chunks(step, places):
        return ((step // 2 + 1 + places[0]) % 2, step % 2, 0)

    block = (rows, width)
    kept = (2, rows, chunk)
    return pl.pallas_call(
        functools.partial(ffn_forward_kernel, len(parts)),
        grid_spec=pltpu.PrefetchScalarGridSpec(
            num_scalar_prefetch=1,
            grid=(4,),
            in_specs=[whole(block)] * len(parts)
            + [whole(vectors.shape), packed.in_spec(1, chunks), packed.out_spec(1, chunks)],
            out_specs=[
                whole(block), whole(block), whole(block),
                whole(block), whole((rows, 1)), whole(block), whole((rows, 1)),
                pl.BlockSpec(kept, lambda i, p: (0, 0, jnp.minimum(i, 1))),
                pl.BlockSpec(kept, lambda i, p: (0, 0, jnp.maximum(i - 2, 0))),
            ],
            scratch_shapes=[pltpu.VMEM(block, F32), pltpu.VMEM(block, F32)],
        ),
        out_shape=[
            struct(block, F32), struct(block, BF), struct(block, BF),
            struct(block, F32), struct((rows, 1), F32), struct(block, F32), struct((rows, 1), F32),
            struct((2, rows, 2 * chunk), BF), struct((2, rows, 2 * chunk), BF),
        ],
        compiler_params=PARAMS,
        cost_estimate=FREE,
    )(places, *parts, vectors, packed.fc_in, packed.fc_out)


def ffn_backward_kernel(place_ref, *refs):
    g_own, g_sib, m_own, m_sib, a_own, a_sib, w_in_ref, w_out_ref = refs[:8]
    own_ref, sib_ref, in_send, in_keep, out_send, out_keep, total_ref = refs[8:]
    step = pl.program_id(0)
    rows, width = g_own.shape
    chunk = a_own.shape[2]
    grads = jnp.concatenate([g_own[...], g_sib[...]], axis=0)
    w_in = w_in_ref[...].reshape(width, chunk)
    slope = jnp.concatenate([a_own[1], a_sib[1]], axis=0).astype(F32)
    before_grad = (mm_t(grads, w_out_ref[...].reshape(chunk, width)) * slope).astype(BF)
    part = mm_t(before_grad, w_in)

    @pl.when(step == 0)
    def _():
        total_ref[...] = part

    @pl.when(step > 0)
    def _():
        total_ref[...] += part

    half = width // 2
    for mine, ref in ((1 - place_ref[1], in_send), (place_ref[1], in_keep)):
        lanes = pl.ds(pl.multiple_of(mine * half, half), half)
        middle = jnp.concatenate([m_own[:, lanes], m_sib[:, lanes]], axis=0)
        ref[...] = mm_outer(middle, before_grad, BF).reshape(ref.shape)
    active = jnp.concatenate([a_own[0], a_sib[0]], axis=0)
    out_grad = mm_outer(active, grads, BF)

    @pl.when(step < 2)
    def _():
        out_send[0] = out_grad

    @pl.when(step >= 2)
    def _():
        out_keep[0] = out_grad

    @pl.when(step == 3)
    def _():
        own_ref[...] = total_ref[:rows, :]
        sib_ref[...] = total_ref[rows:, :].astype(BF)


def ffn_backward(places, grads, middles, actives, packed):
    rows, width = grads[0].shape
    chunk = packed.units // 8

    def chunks(step, places):
        return (places[0], step % 2, (step // 2 + 1 + places[2]) % 2)

    def column(step, places):
        return step % 2 * 2 + (step // 2 + 1 + places[2]) % 2

    block = (rows, width)
    kept = pl.BlockSpec((2, rows, chunk), lambda i, p: (0, 0, column(i, p)))
    rows_each = packed.rows * 2
    groups = width // 2 // rows_each if rows_each % 16 == 0 else 1
    tall = (groups, 2, width // 2 // groups, 2 * chunk)
    side = pl.BlockSpec(
        (groups, 1, tall[2], chunk), lambda i, p: (0, column(i, p) // 2, 0, column(i, p) % 2)
    )
    return pl.pallas_call(
        ffn_backward_kernel,
        grid_spec=pltpu.PrefetchScalarGridSpec(
            num_scalar_prefetch=1,
            grid=(4,),
            in_specs=[whole(block)] * 4
            + [kept, kept, packed.in_spec(2, chunks), packed.out_spec(2, chunks)],
            out_specs=[
                whole(block), whole(block), side, side,
                pl.BlockSpec((1, chunk, width), lambda i, p: (jnp.minimum(i, 1), 0, 0)),
                pl.BlockSpec((1, chunk, width), lambda i, p: (jnp.maximum(i - 2, 0), 0, 0)),
            ],
            scratch_shapes=[pltpu.VMEM((2 * rows, width), F32)],
        ),
        out_shape=[
            struct(block, F32), struct(block, BF),
            struct(tall, BF), struct(tall, BF),
            struct((2, chunk, width), BF), struct((2, chunk, width), BF),
        ],
        compiler_params=PARAMS,
        cost_estimate=FREE,
    )(places, *grads, *middles, *actives, packed.fc_in, packed.fc_out)


def scatter_ffn(plan, order, early, in_send, in_keep, out_send, out_keep):
    hi, lo, half = ("fsdp", plan.hi), ("fsdp", plan.lo), ("seq", plan.ranks)
    inner = [("fsdp", b) for b in reversed(plan.f_bits) if b not in (plan.hi, plan.lo)]
    z_names = [("seq", b) for b in reversed(plan.z_bits)]
    tail = (*inner, half, *z_names)
    width = out_keep.shape[-1]
    count = 2 ** (1 + len(tail))
    if in_keep.shape[0] == 1:
        shape = in_keep.shape

        def spread_rows(value):
            value = value.reshape(2, count, shape[2] // count, width)
            return jnp.swapaxes(value, 0, 1)

        in_send, in_keep = spread_rows(in_send), spread_rows(in_keep)

    def summed(first, keep, there):
        shape = (2,) * (1 + len(tail)) + (-1, width)
        return Sum(plan, order, (first, *tail), [keep.reshape(shape), there.reshape(shape)])

    first = summed(lo, in_keep, plan.swap(in_send, *hi))
    second = summed(hi, out_keep, plan.swap(out_send, *lo))
    yield
    first_names = [lo, *inner, *z_names]
    if early:
        first_names = [*z_names, lo, *inner]
    steps = list(zip(first_names, [hi, *inner, *z_names])) + [(half, half)]
    for one, two in steps:
        if one == two:
            first.tie()
            second.tie()
            send = jnp.stack([first.sending(one), second.sending(one)])
            there = plan.swap(order.done(send), *one)
            first.receive(there[0])
            second.receive(there[1])
        else:
            first.step(one)
            second.step(two)
        yield
        if not early and one not in (lo, hi):
            first.settle()
            second.settle()
            yield
    first.tie()
    second.tie()
    total = order.done(second.total())
    return first.total().astype(BF).reshape(2, 2, -1, width), total


def finish_ffn(plan, order, totals):
    fc_in = jnp.stack([a for a, _ in totals])
    here, send = choose(plan.core, fc_in, 2)
    there = plan.swap(order.done(send), "seq", 1)
    yield
    here, there = order.tie(here, there)
    layers, _, rows, _ = here.shape
    pair = [jnp.swapaxes(v, 1, 2).reshape(layers, rows, plan.n // 2, -1) for v in (here, there)]
    fc_in = stack_by(plan.core, *pair, 3)
    fc_in = order.done(fc_in.reshape(layers, rows, -1).astype(F32))
    return fc_in, jnp.stack([b for _, b in totals])


def gather_vectors(plan, order, vectors):
    layers, count, own = vectors.shape
    value = order.done(vectors.reshape(1, -1))
    names = [("seq", b) for b in [1] + plan.z_bits + [plan.ranks]]
    names += [("fsdp", b) for b in plan.f_bits]
    for name in names:
        there = plan.swap(value, *name)
        yield
        value, there = order.tie(value, there)
        mine = bit_of(plan.f if name[0] == "fsdp" else plan.s, name[1])
        value = order.done(stack_by(mine, value, there, 0).reshape(-1, value.shape[-1]))
    value = value.reshape(plan.n, layers, count, own)
    return jnp.transpose(value, (1, 2, 0, 3)).reshape(layers, count, -1).astype(F32)


def sum_vectors(plan, vectors):
    count, width = vectors.shape
    value = vectors.reshape(count, plan.n, width // plan.n)
    value = jnp.transpose(value, (1, 0, 2)).reshape(plan.n, -1)
    value = lax.all_to_all(value, ALL, split_axis=0, concat_axis=0, tiled=True)
    return jnp.sum(value, axis=0).reshape(count, width // plan.n)


def local(
    mesh_shape,
    inputs,
    segment_ids,
    query_weight,
    key_weight,
    value_weight,
    out_weight,
    fc_in_weight,
    fc_out_weight,
    attn_gain,
    attn_shift,
    ffn_gain,
    ffn_shift,
    cotangent,
):
    layers, _, width = query_weight.shape
    plan = Plan(mesh_shape, width, fc_in_weight.shape[2])
    places = plan.scalars()
    head_dim = width // HEADS

    def to_halves(value):
        mine, other = choose(plan.half, value, 0)
        return jnp.concatenate([mine, plan.swap(other, "seq", plan.ranks)], axis=0)

    def from_halves(value):
        size = value.shape[0] // 2
        there = plan.swap(value[size:].astype(BF), "seq", plan.ranks).astype(F32)
        return stack_by(plan.half, value[:size], there, 0)

    order, tasks = Order(), Tasks()
    matrices = (query_weight, key_weight, value_weight, out_weight)
    if plan.fast:
        columns = tasks.add(rank_columns(plan, order, matrices))
    x_low = to_halves(inputs)
    packed = [Packed(plan, fc_in_weight[k], fc_out_weight[k]) for k in range(layers)]
    if plan.fast:
        tasks.drain(columns)
        here, there, out = columns.result

        def fetch(layer):
            parts = (here[layer], there[layer], out[layer])
            return tasks.add(gather_attention(plan, order, places, parts))

        attention = [fetch(0)]
    (x_low,) = order.tie(x_low)
    x_pieces = group_pieces(plan, order.done(x_low))
    ids = jnp.concatenate(group_pieces(plan, to_halves(segment_ids)), axis=0)
    vectors = jnp.stack([attn_gain, attn_shift, ffn_gain, ffn_shift], axis=1)
    vectors = tasks.add(gather_vectors(plan, order, vectors))
    upstream = [to_halves(cotangent)]
    tokens = x_low.shape[0]
    if plan.fast:
        tasks.run(attention[0])
        tasks.run(vectors)
        tasks.drain(attention[0])
        attention += [fetch(k) for k in range(1, layers)]
    else:
        attention = [Task.finished(m) for m in gather_attention_whole(plan, matrices)]

    hidden = x_low
    records = []
    for layer in range(layers):
        tasks.drain(attention[layer])
        w_qkv, w_out = attention[layer].result
        tied = order.tie(*x_pieces, w_qkv, w_out, ids)
        x_pieces = tied[:-3]
        qkv, att, keep, send = attn_forward(x_pieces, *tied[-3:], head_dim)
        order.done(send)
        parts = group_sum(plan, order, keep, plan.swap(send, "seq", 1))
        tasks.drain(vectors)
        if layer + 1 < layers:
            tasks.run(attention[layer + 1])
        tied = order.tie(hidden, *parts, *upstream)
        upstream = tied[1 + len(parts) :]
        (
            hidden, x_low, mid_low, normed_attn, inverse_attn, normed_ffn, inverse_ffn, send, keep,
        ) = ffn_forward(places, tied[: 1 + len(parts)], vectors.result[layer], packed[layer])
        order.done(x_low)
        next_pieces = group_pieces(plan, x_low) if layer + 1 < layers else None
        middles = (mid_low, plan.swap(mid_low, "seq", 1))
        actives = (keep, plan.swap(send, "seq", 1))
        records.append(
            (x_pieces, qkv, att, normed_attn, inverse_attn, normed_ffn, inverse_ffn, actives, middles)
        )
        x_pieces = next_pieces
    outputs = from_halves(hidden)

    grads, vector_grads = [None] * layers, [None] * layers
    older = ()
    for layer in reversed(range(layers)):
        (
            x_pieces, qkv, att, normed_attn, inverse_attn, normed_ffn, inverse_ffn, actives, middles,
        ) = records[layer]
        gains = vectors.result[layer]
        w_qkv, w_out = attention[layer].result
        sum_grad, ff_grad, gain_ffn_grad, shift_ffn_grad = norm_backward(
            order.tie(*upstream), normed_ffn, inverse_ffn, gains[2:3]
        )
        order.done(ff_grad)
        ff_sibling = plan.swap(ff_grad, "seq", 1)
        if older:
            older[0].run()
        tied = order.tie(ff_grad, ff_sibling, *middles, *actives)
        own, sibling, *ffn_grads = ffn_backward(
            places, tied[:2], tied[2:4], tied[4:], packed[layer]
        )
        order.done(sibling)
        ffn_task = tasks.add(scatter_ffn(plan, order, layer == 0, *ffn_grads))
        sibling = plan.swap(sibling, "seq", 1)
        if older:
            older[0].run()
            older[1].run()
        tied = order.tie(sum_grad, own, sibling)
        attn_sum_grad, branch_grad, gain_attn_grad, shift_attn_grad = norm_backward(
            tied, normed_attn, inverse_attn, gains[0:1]
        )
        order.done(branch_grad)
        g_pieces = group_pieces(plan, branch_grad)
        vector_grads[layer] = (gain_attn_grad, shift_attn_grad, gain_ffn_grad, shift_ffn_grad)
        extra = jnp.zeros((8, 16, width // plan.ranks), BF)
        if layer == 0:
            summed = jnp.concatenate([v for member in vector_grads for v in member], axis=0)
            if plan.fast:
                extra = summed.reshape(4 * layers, 8, plan.ranks, -1)
                extra = jnp.transpose(extra, (1, 2, 0, 3)).reshape(8, plan.ranks, -1)
                extra = jnp.pad(extra.astype(BF), ((0, 0), (0, 16 - plan.ranks), (0, 0)))
        g_pieces = order.tie(*g_pieces)
        order.done(g_pieces[-1])
        if older:
            older[0].run()
        else:
            (outputs,) = order.tie(outputs)
            order.done(outputs)
        tied = order.tie(*g_pieces, qkv)
        g_pieces = tied[:-1]
        dqkv, keep, send = attn_backward(g_pieces, tied[-1], w_qkv, w_out, ids, head_dim)
        order.done(send)
        if older:
            older[0].run()
            (send,) = order.tie(send)
        there = plan.swap(send, "seq", 1)
        ffn_task.run()
        upstream = [attn_sum_grad] + group_sum(plan, order, keep, there)
        if plan.fast:
            attn_task = tasks.add(
                scatter_attention(
                    plan, order, places, x_pieces, g_pieces, dqkv, att, extra, layer == 0
                )
            )
        else:
            attn_task = Task.finished(scatter_attention_whole(plan, x_pieces, g_pieces, dqkv, att))
        grads[layer] = (ffn_task, attn_task)
        if layer > 0:
            older = grads[layer]
    rows_grad = add_parts(order.tie(*upstream), tokens)
    order.done(rows_grad)
    input_grad = from_halves(rows_grad)
    ffn_task.run()
    if older:
        older[1].run()
    attn_task.run()
    (input_grad,) = order.tie(input_grad)
    order.done(input_grad)
    ffn_task.run()
    attn_task.run()
    if older:
        older[1].run()
        older[0].run()
        older[1].run()
    tasks.drain(ffn_task)
    for member in grads:
        tasks.drain(member[0])
    fc_task = tasks.add(finish_ffn(plan, order, [f.result for f, _ in grads]))
    for member in grads:
        tasks.drain(member[1])
    if plan.fast:
        attn_task = tasks.add(finish_attention(plan, order, [a.result for _, a in grads]))
        tasks.finish()
        attn_grads, summed = attn_task.result
    else:
        tasks.finish()
        summed = sum_vectors(plan, summed)
        attn_grads = [jnp.stack([a.result[k] for _, a in grads]) for k in range(4)]
    fc_in_grad, fc_out_grad = fc_task.result
    summed = summed.reshape(layers, 4, -1)
    return (
        outputs, input_grad, *attn_grads, fc_in_grad, fc_out_grad, *(summed[:, k] for k in range(4)),
    )


def solution(mesh):
    tokens = P("fsdp", "seq", None)
    matrix = P(None, ("fsdp", "seq"), None)
    vector = P(None, ("fsdp", "seq"))
    return jax.shard_map(
        functools.partial(local, dict(mesh.shape)),
        mesh=mesh,
        in_specs=(tokens, P("fsdp", "seq"), *[matrix] * 6, *[vector] * 4, tokens),
        out_specs=(tokens, tokens, *[matrix] * 6, *[vector] * 4),
        check_vma=False,
    )
```

```python
import functools

import jax
import jax.numpy as jnp
from jax import lax
from jax.experimental import pallas as pl
from jax.experimental.pallas import tpu as pltpu
from jax.sharding import PartitionSpec as P

HEADS = 16
NEG_FILL = -1e30
NORM_EPS = 1e-05
inv_root_two = 0.7071067811865476
inv_root_two_pi = 0.3989422804014327
BF = jnp.bfloat16
F32 = jnp.float32
ALL = ("fsdp", "seq")
PARAMS = pltpu.CompilerParams(vmem_limit_bytes=56 * 1024 * 1024)


def mm(a, b, out=F32):
    return lax.dot_general(a, b, (((1,), (0,)), ((), ())), preferred_element_type=F32).astype(out)


def mm_t(a, b, out=F32):
    return lax.dot_general(a, b, (((1,), (1,)), ((), ())), preferred_element_type=F32).astype(out)


def mm_outer(a, b, out=F32):
    return lax.dot_general(a, b, (((0,), (0,)), ((), ())), preferred_element_type=F32).astype(out)


def struct(shape, dtype):
    return jax.ShapeDtypeStruct(shape, dtype)


def whole(shape):
    return pl.BlockSpec(shape, lambda *_: (0,) * len(shape))


FREE = pl.CostEstimate(flops=0, bytes_accessed=0, transcendentals=0)


class Plan:
    def __init__(self, mesh_shape, width, hidden_units):
        self.n_f, self.n_s = mesh_shape["fsdp"], mesh_shape["seq"]
        self.n = self.n_f * self.n_s
        self.ranks = self.n_s // 2
        self.f = lax.axis_index("fsdp")
        self.s = lax.axis_index("seq")
        self.half = self.s // self.ranks
        self.rank = self.s % self.ranks
        self.core = self.s % 2
        self.f_bits = [1 << k for k in range(self.n_f.bit_length() - 1)]
        self.z_bits = [1 << k for k in range(1, self.ranks.bit_length() - 1)]
        self.hi, self.lo = self.f_bits[-1], self.f_bits[-2]
        self.f_hi, self.f_lo = bit_of(self.f, self.hi), bit_of(self.f, self.lo)
        self.fast = (
            self.n_f == 4
            and self.n_s == 8
            and (width // self.n) % 32 == 0
            and (hidden_units // self.n) % 128 == 0
        )

    def swap(self, value, axis_name, bit):
        count = self.n_f if axis_name == "fsdp" else self.n_s
        return lax.ppermute(value, axis_name, [(i, i ^ bit) for i in range(count)])

    def scalars(self):
        return jnp.stack([self.core, self.f_hi, self.f_lo, self.f * 2 + self.half, self.rank]).astype(
            jnp.int32
        )


def bit_of(index, bit):
    return (index // bit) % 2


def stack_by(mine, here, there, axis):
    return jnp.where(
        mine == 0, jnp.stack([here, there], axis=axis), jnp.stack([there, here], axis=axis)
    )


def choose(mine, value, axis):
    first = lax.index_in_dim(value, 0, axis, keepdims=False)
    second = lax.index_in_dim(value, 1, axis, keepdims=False)
    return jnp.where(mine == 0, first, second), jnp.where(mine == 0, second, first)


def group_pieces(plan, value):
    pieces = [value]
    for bit in plan.z_bits:
        pieces = pieces + [plan.swap(p, "seq", bit) for p in pieces]
    return pieces + [plan.swap(p, "seq", 1) for p in pieces]


def group_sum(plan, order, keep, there):
    parts = [keep, there]
    size = keep.shape[0]
    for bit in reversed(plan.z_bits):
        size = size // 2
        tied = order.tie(*parts)
        out = sum(p[size : 2 * size].astype(F32) for p in tied).astype(BF)
        parts = parts + [plan.swap(order.done(out), "seq", bit)]
    return parts


def add_parts(parts, rows):
    return sum(p[:rows].astype(F32) for p in parts)


class Order:
    def __init__(self):
        self.last = None

    def tie(self, *values):
        if self.last is None:
            return values
        return lax.optimization_barrier((*values, self.last))[:-1]

    def done(self, value):
        self.last = value
        return value


class Task:
    def __init__(self, steps):
        self.steps, self.result, self.running = steps, None, True
        self.run()

    @staticmethod
    def finished(result):
        task = Task(iter(()))
        task.result = result
        return task

    def run(self):
        if self.running:
            try:
                next(self.steps)
            except StopIteration as stop:
                self.running, self.result = False, stop.value


class Tasks:
    def __init__(self):
        self.open = []

    def add(self, steps):
        task = Task(steps)
        self.open.append(task)
        return task

    def run(self, task):
        task.run()

    def drain(self, task):
        while task.running:
            task.run()

    def slot(self, count):
        self.open = [t for t in self.open if t.running]
        for task in self.open[:count]:
            task.run()

    def finish(self):
        while self.open:
            self.slot(len(self.open))


class Sum:
    def __init__(self, plan, order, names, parts):
        self.plan, self.order, self.names = plan, order, tuple(names)
        self.parts = [(p, self.names) for p in parts]
        self.chosen = {}

    def pick(self, part, chosen):
        value, names = part
        rest = value.shape[len(names) :]
        zero = jnp.zeros((), jnp.int32)
        start = [chosen.get(n, zero) for n in names] + [zero] * len(rest)
        size = [1 if n in chosen else 2 for n in names] + list(rest)
        left = [d for n, d in zip(names, size) if n not in chosen]
        return lax.dynamic_slice(value, start, size).reshape(*left, *rest)

    def tie(self):
        tied = self.order.tie(*[p for p, _ in self.parts])
        self.parts = [(p, names) for p, (_, names) in zip(tied, self.parts)]

    def sending(self, name, kind=BF):
        plan = self.plan
        mine = bit_of(plan.f if name[0] == "fsdp" else plan.s, name[1]).astype(jnp.int32)
        there = {**self.chosen, name: 1 - mine}
        out = sum(self.pick(p, there).astype(F32) for p in self.parts).astype(kind)
        self.chosen[name] = mine
        return out

    def receive(self, value):
        left = [n for n in self.names if n not in self.chosen]
        self.parts.append((value, tuple(left)))

    def step(self, name):
        self.tie()
        send = self.order.done(self.sending(name))
        self.receive(self.plan.swap(send, *name))

    def settle(self):
        self.tie()
        self.order.done(self.parts[-1][0])

    def total(self):
        return sum(self.pick(p, self.chosen).astype(F32) for p in self.parts)


def norm_rows(summed):
    center = jnp.mean(summed, axis=-1, keepdims=True)
    offset = summed - center
    spread = jnp.mean(offset * offset, axis=-1, keepdims=True)
    inverse = lax.rsqrt(spread + NORM_EPS)
    return offset * inverse, inverse


def norm_forward_kernel(count, *refs):
    parts, (gain_ref, shift_ref) = refs[:count], refs[count : count + 2]
    out_ref, low_ref, normed_ref, inverse_ref = refs[count + 2 :]
    summed = parts[0][...].astype(F32)
    for part in parts[1:]:
        summed = summed + part[...].astype(F32)
    normed, inverse = norm_rows(summed)
    result = normed * gain_ref[...] + shift_ref[...]
    out_ref[...] = result
    low_ref[...] = result.astype(BF)
    normed_ref[...] = normed
    inverse_ref[...] = inverse


def norm_forward(parts, gain, shift, rows):
    width = gain.shape[1]
    block = (rows, width)
    return pl.pallas_call(
        functools.partial(norm_forward_kernel, len(parts)),
        grid=(1,),
        in_specs=[whole(block)] * len(parts) + [whole((1, width))] * 2,
        out_specs=[whole(block)] * 3 + [whole((rows, 1))],
        out_shape=[
            struct(block, F32), struct(block, BF), struct(block, F32), struct((rows, 1), F32),
        ],
        compiler_params=PARAMS,
        cost_estimate=FREE,
    )(*parts, gain, shift)


def norm_backward_kernel(count, *refs):
    parts, (normed_ref, inverse_ref, gain_ref) = refs[:count], refs[count : count + 3]
    out_ref, low_ref, gain_grad_ref, shift_grad_ref = refs[count + 3 :]
    upstream = parts[0][...].astype(F32)
    for part in parts[1:]:
        upstream = upstream + part[...].astype(F32)
    normed = normed_ref[...]
    gain_grad_ref[...] = jnp.sum(upstream * normed, axis=0, keepdims=True)
    shift_grad_ref[...] = jnp.sum(upstream, axis=0, keepdims=True)
    scaled = upstream * gain_ref[...]
    inner = (
        scaled
        - jnp.mean(scaled, axis=-1, keepdims=True)
        - normed * jnp.mean(scaled * normed, axis=-1, keepdims=True)
    )
    result = inner * inverse_ref[...]
    out_ref[...] = result
    low_ref[...] = result.astype(BF)


def norm_backward(parts, normed, inverse, gain):
    rows, width = normed.shape
    return pl.pallas_call(
        functools.partial(norm_backward_kernel, len(parts)),
        grid=(1,),
        in_specs=[whole((rows, width))] * (len(parts) + 1) + [whole((rows, 1)), whole((1, width))],
        out_specs=[whole((rows, width))] * 2 + [whole((1, width))] * 2,
        out_shape=[
            struct((rows, width), F32), struct((rows, width), BF),
            struct((1, width), F32), struct((1, width), F32),
        ],
        compiler_params=PARAMS,
        cost_estimate=FREE,
    )(*parts, normed, inverse, gain)


def pick_head(lanes, head, head_dim):
    return (lanes >= head * head_dim) & (lanes < (head + 1) * head_dim)


def attn_forward_kernel(head_dim, count, *refs):
    pieces = refs[:count]
    w_qkv_ref, w_out_ref, ids_q_ref, ids_k_ref = refs[count : count + 4]
    qkv_ref, att_ref, keep_ref, send_ref = refs[count + 4 :]
    step = pl.program_id(0)
    rows, width = att_ref.shape

    @pl.when(step == 0)
    def _():
        w_qkv = w_qkv_ref[...]
        for index, piece in enumerate(pieces):
            qkv = mm(piece[...], w_qkv).astype(BF)
            part = pl.ds(index * rows, rows)
            qkv_ref[part, :width] = (qkv[:, :width].astype(F32) * head_dim**-0.5).astype(BF)
            qkv_ref[part, width:] = qkv[:, width:]

    queries = qkv_ref[pl.ds(pl.multiple_of(step * rows, rows), rows), :width]
    keys, values = qkv_ref[:, width : 2 * width], qkv_ref[:, 2 * width :]
    lanes = lax.broadcasted_iota(jnp.int32, (1, width), 1)
    allowed = ids_q_ref[...] == ids_k_ref[...]
    total = jnp.zeros((rows, width), F32)
    for head in range(width // head_dim):
        here = pick_head(lanes, head, head_dim)
        scores = mm_t(jnp.where(here, queries, jnp.zeros_like(queries)), keys)
        scores = jnp.where(allowed, scores, NEG_FILL)
        weights = jnp.exp(scores - jnp.max(scores, axis=1, keepdims=True))
        norm = 1.0 / jnp.sum(weights, axis=1, keepdims=True)
        total = jnp.where(here, mm(weights.astype(BF), values) * norm, total)
    attended = total.astype(BF)
    att_ref[...] = attended
    branch = mm(attended, w_out_ref[...])

    @pl.when(step < count // 2)
    def _():
        keep_ref[...] = branch

    @pl.when(step >= count // 2)
    def _():
        send_ref[...] = branch.astype(BF)


def attn_forward(pieces, w_qkv, w_out, ids, head_dim):
    count, features = len(pieces), pieces[0].shape[1]
    rows = ids.shape[0] // count
    tokens, width = count * rows, w_out.shape[0]
    half = count // 2
    heads = width // head_dim
    return pl.pallas_call(
        functools.partial(attn_forward_kernel, head_dim, count),
        grid=(count,),
        in_specs=[whole((rows, features))] * count
        + [
            whole(w_qkv.shape),
            whole(w_out.shape),
            pl.BlockSpec((rows, 1), lambda i: (i, 0)),
            whole((1, tokens)),
        ],
        out_specs=[
            whole((tokens, 3 * width)),
            pl.BlockSpec((rows, width), lambda i: (i, 0)),
            pl.BlockSpec((rows, features), lambda i: (jnp.minimum(i, half - 1), 0)),
            pl.BlockSpec((rows, features), lambda i: (jnp.maximum(i - half, 0), 0)),
        ],
        out_shape=[
            struct((tokens, 3 * width), BF),
            struct((tokens, width), BF),
            struct((half * rows, features), F32),
            struct((half * rows, features), BF),
        ],
        compiler_params=PARAMS,
        cost_estimate=FREE,
    )(*pieces, w_qkv, w_out, ids.reshape(tokens, 1), ids.reshape(1, tokens))


def attn_backward_kernel(head_dim, count, *refs):
    pieces = refs[:count]
    qkv_ref, w_qkv_ref, w_out_ref, ids_q_ref, ids_k_ref = refs[count : count + 5]
    dqkv_ref, keep_ref, send_ref, grad_ref, dk_ref, dv_ref = refs[count + 5 :]
    step = pl.program_id(0)
    rows = pieces[0].shape[0]
    width = grad_ref.shape[1]

    @pl.when(step == 0)
    def _():
        w_out = w_out_ref[...]
        for index, piece in enumerate(pieces):
            grad_ref[pl.ds(index * rows, rows), :] = mm_t(piece[...], w_out, BF)
        dk_ref[...] = jnp.zeros_like(dk_ref)
        dv_ref[...] = jnp.zeros_like(dv_ref)

    place = pl.ds(pl.multiple_of(step * rows, rows), rows)
    queries, grads = qkv_ref[place, :width], grad_ref[place, :]
    keys, values = qkv_ref[:, width : 2 * width], qkv_ref[:, 2 * width :]
    lanes = lax.broadcasted_iota(jnp.int32, (1, width), 1)
    allowed = ids_q_ref[...] == ids_k_ref[...]
    dq = jnp.zeros((rows, width), F32)
    for head in range(width // head_dim):
        here = pick_head(lanes, head, head_dim)
        q_head = jnp.where(here, queries, jnp.zeros_like(queries))
        g_head = jnp.where(here, grads, jnp.zeros_like(grads))
        scores = mm_t(q_head, keys)
        scores = jnp.where(allowed, scores, NEG_FILL)
        weights = jnp.exp(scores - jnp.max(scores, axis=1, keepdims=True))
        probs = weights * (1.0 / jnp.sum(weights, axis=1, keepdims=True))
        prob_grad = mm_t(g_head, values)
        product = probs * prob_grad
        delta = jnp.sum(product, axis=1, keepdims=True)
        score_grad = (product - probs * delta).astype(BF)
        dq = jnp.where(here, mm(score_grad, keys), dq)
        dk_ref[...] += mm_outer(score_grad, q_head)
        dv_ref[...] += mm_outer(probs.astype(BF), g_head)
    dqkv_ref[place, :width] = (dq * head_dim**-0.5).astype(BF)

    @pl.when(step == count - 1)
    def _():
        dqkv_ref[:, width : 2 * width] = dk_ref[...].astype(BF)
        dqkv_ref[:, 2 * width :] = dv_ref[...].astype(BF)
        w_qkv = w_qkv_ref[...]
        half = count // 2
        for index in range(count):
            part = mm_t(dqkv_ref[pl.ds(index * rows, rows), :], w_qkv)
            if index < half:
                keep_ref[pl.ds(index * rows, rows), :] = part
            else:
                send_ref[pl.ds((index - half) * rows, rows), :] = part.astype(BF)


def attn_backward(pieces, qkv, w_qkv, w_out, ids, head_dim):
    count = len(pieces)
    rows, features = pieces[0].shape
    tokens, width = count * rows, w_out.shape[0]
    heads = width // head_dim
    half = tokens // 2
    return pl.pallas_call(
        functools.partial(attn_backward_kernel, head_dim, count),
        grid=(count,),
        in_specs=[whole((rows, features))] * count
        + [
            whole(qkv.shape),
            whole(w_qkv.shape),
            whole(w_out.shape),
            pl.BlockSpec((rows, 1), lambda i: (i, 0)),
            whole((1, tokens)),
        ],
        out_specs=[
            whole((tokens, 3 * width)), whole((half, features)), whole((half, features)),
        ],
        out_shape=[
            struct((tokens, 3 * width), BF), struct((half, features), F32),
            struct((half, features), BF),
        ],
        scratch_shapes=[
            pltpu.VMEM((tokens, width), BF),
            pltpu.VMEM((tokens, width), F32),
            pltpu.VMEM((tokens, width), F32),
        ],
        compiler_params=PARAMS,
        cost_estimate=FREE,
    )(*pieces, qkv, w_qkv, w_out, ids.reshape(tokens, 1), ids.reshape(1, tokens))


def attn_weights_kernel(count, place_ref, *refs):
    x_refs, g_refs = refs[:count], refs[count : 2 * count]
    dqkv_ref, att_ref, extra_ref = refs[2 * count : 2 * count + 3]
    a_send, a_keep, b_send, b_keep, out_ref = refs[2 * count + 3 :]
    block = pl.program_id(0)
    rows = g_refs[0].shape[0]
    width = att_ref.shape[1]
    small = out_ref.shape[0] // pl.num_programs(0)
    height = 4 * small

    @pl.when(block == 0)
    def _():
        total = None
        for index in range(count):
            part = mm_outer(att_ref[pl.ds(index * rows, rows), :], g_refs[index][...])
            total = part if total is None else total + part
        out_ref[...] = total.astype(BF)

    lanes = pl.ds(pl.multiple_of(block * height, height), height)
    grad = None
    for index in range(count):
        part = mm_outer(x_refs[index][:, lanes], dqkv_ref[pl.ds(index * rows, rows), :])
        grad = part if grad is None else grad + part
    grad = grad.astype(BF)
    hi, lo, low = block // 4, (block // 2) % 2, block % 2

    def put_a(ref, place):
        ref[place, :height, :] = grad[:, :width]
        ref[place, height : 2 * height, :] = grad[:, width : 2 * width]

    def put_b(ref, place):
        ref[place, :height, :] = grad[:, 2 * width :]
        part = out_ref[pl.ds(pl.multiple_of(block * small, small), small), :]
        for piece in range(4):
            start = height + piece * small
            ref[place, start : start + small, :] = part[:, piece * width : (piece + 1) * width]
        ref[place, 2 * height :, :] = extra_ref[0]

    pl.when(hi != place_ref[1])(lambda: put_a(a_send, lo * 2 + low))
    pl.when(hi == place_ref[1])(lambda: put_a(a_keep, lo * 2 + low))
    pl.when(lo != place_ref[2])(lambda: put_b(b_send, hi * 2 + low))
    pl.when(lo == place_ref[2])(lambda: put_b(b_keep, hi * 2 + low))


def attn_weights(places, x_pieces, g_pieces, dqkv, att, extra):
    count = len(x_pieces)
    rows, features = g_pieces[0].shape
    width = att.shape[1]
    high = 2 * features // 8
    parts = [(4, high, width)] * 2 + [(4, high + extra.shape[1], width)] * 2
    return pl.pallas_call(
        functools.partial(attn_weights_kernel, count),
        grid_spec=pltpu.PrefetchScalarGridSpec(
            num_scalar_prefetch=1,
            grid=(8,),
            in_specs=[whole((rows, features))] * (2 * count)
            + [
                whole(dqkv.shape),
                whole(att.shape),
                pl.BlockSpec((1,) + extra.shape[1:], lambda i, p: (i, 0, 0)),
            ],
            out_specs=[whole(p) for p in parts],
            scratch_shapes=[pltpu.VMEM((width, features), BF)],
        ),
        out_shape=[struct(p, BF) for p in parts],
        compiler_params=PARAMS,
        cost_estimate=FREE,
    )(places, *x_pieces, *g_pieces, dqkv, att, extra)


def assemble_kernel(place_ref, a_own, a_other, b_own, b_other, qkv_ref, out_ref, *extra_ref):
    own, rank = place_ref[3], place_ref[4]
    height, width = a_own.shape[1] // 8, a_own.shape[2]
    ranks = 4
    for block in range(8):
        a_ref = a_own if block < 4 else a_other
        b_ref = b_own if block < 4 else b_other
        b_block = (block % 4) // 2 * 4 + block // 4 * 2 + block % 2
        if extra_ref:
            rows = b_ref[block % 4, 8 * height :, :].astype(F32)
        for inner in range(4):
            rank_there = rank ^ ((inner // 2) + (inner % 2) * 2)
            start = ((own ^ block) * ranks + rank_there) * height
            place = pl.ds(pl.multiple_of(start, height), height)
            qkv_ref[place, :width] = a_ref[block % 4, inner * height : (inner + 1) * height, :]
            first = (4 + inner) * height
            qkv_ref[place, width : 2 * width] = a_ref[block % 4, first : first + height, :]
            device = (own ^ b_block) * ranks + rank_there
            place = pl.ds(pl.multiple_of(device * height, height), height)
            qkv_ref[place, 2 * width :] = b_ref[block % 4, inner * height : (inner + 1) * height, :]
            place = pl.ds(pl.multiple_of((own ^ b_block) * height, height), height)
            out_ref[place, inner * width : (inner + 1) * width] = b_ref[
                block % 4, first : first + height, :
            ]
            if extra_ref:
                extra_ref[0][pl.ds(device, 1), :] = rows[inner : inner + 1, :]


def assemble(places, a_own, a_other, b_own, b_other):
    _, high, width = a_own.shape
    features = 4 * high
    shapes = [struct((features, 3 * width), BF), struct((width, features), BF)]
    if b_own.shape[1] > high:
        shapes.append(struct((32, width), F32))
    return pl.pallas_call(
        assemble_kernel,
        grid_spec=pltpu.PrefetchScalarGridSpec(
            num_scalar_prefetch=1,
            grid=(1,),
            in_specs=[whole(a_own.shape)] * 2 + [whole(b_own.shape)] * 2,
            out_specs=[whole(p.shape) for p in shapes],
        ),
        out_shape=shapes,
        compiler_params=PARAMS,
        cost_estimate=FREE,
    )(places, a_own, a_other, b_own, b_other)


def spread_pairs(plan):
    pairs = []
    for shard in range(plan.n):
        rank, block = shard // (2 * plan.n_f), shard % (2 * plan.n_f)
        pairs.append((shard, block // 2 * plan.n_s + block % 2 * plan.ranks + rank))
    return pairs


def gather_attention_whole(plan, matrices):
    layers, _, cols = matrices[0].shape
    size = cols // plan.ranks
    result = []
    for layer in range(layers):
        full = [lax.all_gather(m[layer], ALL, axis=0, tiled=True) for m in matrices]
        qkv = [lax.dynamic_slice_in_dim(m, plan.rank * size, size, 1) for m in full[:3]]
        w_out = lax.dynamic_slice_in_dim(full[3], plan.rank * size, size, 0)
        result.append((jnp.concatenate(qkv, axis=1), w_out))
    return result


def rank_columns(plan, order, matrices, vectors):
    query, key, value, out = matrices
    layers, rows, cols = query.shape
    half = cols // 2
    quarter = half // 2
    upper = bit_of(plan.s, 2) == 1
    send = [jnp.where(upper, m[..., :half], m[..., half:]) for m in (query, key, value)]
    extra = jnp.pad(vectors, ((0, 15), (0, half - vectors.shape[1])))
    send = jnp.concatenate([jnp.stack(send, axis=1).reshape(-1, half), extra], axis=0)
    there = plan.swap(order.done(send), "seq", 2)
    out = lax.ppermute(out, ALL, spread_pairs(plan))
    yield
    query, key, value, there = order.tie(query, key, value, there)
    here = [jnp.where(upper, m[..., half:], m[..., :half]) for m in (query, key, value)]
    more = there[-16:-15, :quarter]
    there = there[:-16].reshape(layers, 3, rows, half)
    both = jnp.stack([jnp.stack(here, axis=1), there], axis=2)
    upper = plan.core == 1
    send = jnp.where(upper, both[..., :quarter], both[..., quarter:])
    shape = send.shape
    vectors = jnp.concatenate([vectors, more], axis=0)
    extra = jnp.pad(vectors, ((0, 14), (0, 0)))
    send = jnp.concatenate([send.reshape(-1, quarter), extra], axis=0)
    there = plan.swap(order.done(send), "seq", 1)
    here = jnp.where(upper, both[..., quarter:], both[..., :quarter])
    yield
    vectors = jnp.concatenate([vectors, there[-16:-14]], axis=0)
    return here, there[:-16].reshape(shape), out, vectors


def gather_attention(plan, order, places, columns):
    columns = order.tie(*columns)
    here, there, out = columns[:3]
    quarter = here.shape[-1]
    qkv = jnp.stack([here, there], axis=1).reshape(-1, quarter)
    w_out = jnp.stack([out[:, k * quarter : (k + 1) * quarter] for k in range(4)])
    extra = [jnp.pad(v, ((0, 16 - v.shape[0]), (0, 0))) for v in columns[3:]]
    bundle = jnp.concatenate([qkv, w_out.reshape(-1, quarter), *extra], axis=0)
    other = plan.swap(order.done(bundle), "seq", plan.ranks)
    yield
    bundle, other = order.tie(bundle, other)
    size = qkv.shape[0] * 2 // 3
    part_a = order.done(jnp.stack([bundle[:size], other[:size]]))
    part_b = order.done(jnp.stack([bundle[size:], other[size:]]))
    other_a = plan.swap(part_a, "fsdp", plan.lo)
    other_b = plan.swap(part_b, "fsdp", plan.hi)
    yield
    part_a, other_a, part_b, other_b = order.tie(part_a, other_a, part_b, other_b)
    part_a = order.done(jnp.concatenate([part_a, other_a], axis=0))
    part_b = order.done(jnp.concatenate([part_b, other_b], axis=0))
    other_a = plan.swap(part_a, "fsdp", plan.hi)
    other_b = plan.swap(part_b, "fsdp", plan.lo)
    yield
    result = assemble(places, *order.tie(part_a, other_a, part_b, other_b))
    order.done(result[1])
    return result


def scatter_attention_whole(plan, x_pieces, g_pieces, dqkv, att):
    size = dqkv.shape[0] // len(x_pieces)
    x_pieces = [x[:size] for x in x_pieces]
    w_qkv = sum(mm_outer(x, d) for x, d in zip(x_pieces, jnp.split(dqkv, len(x_pieces))))
    w_out = sum(mm_outer(a, g) for a, g in zip(jnp.split(att, len(g_pieces)), g_pieces))
    width, features = w_out.shape
    grads = []
    for grad, axis in [(g, 1) for g in jnp.split(w_qkv, 3, axis=1)] + [(w_out, 0)]:
        full = jnp.zeros((features, features), F32)
        full = lax.dynamic_update_slice_in_dim(full, grad, plan.rank * width, axis)
        grads.append(lax.psum_scatter(full, ALL, scatter_dimension=0, tiled=True))
    return grads


def scatter_attention(plan, order, places, x_pieces, g_pieces, dqkv, att, extra, last):
    count = len(x_pieces)
    tied = order.tie(*x_pieces, *g_pieces, dqkv, att)
    grads = attn_weights(places, tied[:count], tied[count : 2 * count], *tied[2 * count :], extra)
    order.done(grads[-1])
    half = ("seq", plan.ranks)
    a_send, a_keep, b_send, b_keep = grads
    hi, lo = ("fsdp", plan.hi), ("fsdp", plan.lo)

    def summed(first, keep, there):
        parts = [p.reshape(2, 2, *keep.shape[1:]) for p in (keep, there)]
        return Sum(plan, order, (first, half), parts)

    part_a = summed(lo, a_keep, plan.swap(a_send, *hi))
    part_b = summed(hi, b_keep, plan.swap(b_send, *lo))
    yield
    part_a.step(lo)
    part_b.step(hi)
    yield
    part_a.tie()
    part_b.tie()
    send = jnp.concatenate([part_a.sending(half), part_b.sending(half)], axis=0)
    there = plan.swap(order.done(send), *half)
    high = a_send.shape[1]
    part_a.receive(there[:high])
    part_b.receive(there[high:])
    yield
    if not last:
        part_a.settle()
        yield
    part_a.tie()
    part_b.tie()
    total_b = order.done(part_b.total().astype(BF))
    return part_a.total().astype(BF), total_b


def finish_attention(plan, order, totals):
    layers = len(totals)
    high, width = totals[0][0].shape
    rows = high // 8
    parts_a = jnp.stack([a for a, _ in totals]).reshape(layers, 2, 2, 2, rows, width)
    parts_b = jnp.stack([b[:high] for _, b in totals]).reshape(layers, 2, 4, rows, width)
    out = jnp.concatenate([parts_b[:, 1, k] for k in range(4)], axis=2)
    out = lax.ppermute(out, ALL, [(b, a) for a, b in spread_pairs(plan)])
    value = parts_b[:, 0].reshape(layers, 1, 2, 2, rows, width)
    qkv = jnp.concatenate([parts_a, value], axis=1)
    extra = totals[0][1][high : high + 4].reshape(2, 2, width)

    def trade(qkv, extra, mine, axis, bit):
        here, send = choose(mine, qkv, axis)
        extra, extra_send = choose(mine, extra, 0)
        extra_send = extra_send.reshape(-1, width)
        pad = jnp.zeros((16 - extra_send.shape[0], width), BF)
        send_all = jnp.concatenate([send.reshape(-1, width), extra_send, pad], axis=0)
        there = plan.swap(order.done(send_all), "seq", bit)
        return here, extra, there

    def take(here, extra, there):
        here, extra, there = order.tie(here, extra, there)
        size = here.size // width
        count = extra.size // width
        more = there[size : size + count].reshape(extra.shape)
        return here, there[:size].reshape(here.shape), extra.astype(F32) + more.astype(F32)

    upper = bit_of(plan.s, 2)
    traded = trade(qkv, extra, upper, 2, 2)
    yield
    here, there, extra = take(*traded)
    qkv = stack_by(upper, here, there, 0)
    traded = trade(qkv, extra.astype(BF), plan.core, 3, 1)
    yield
    here, there, extra = take(*traded)
    (out,) = order.tie(out)
    qkv = stack_by(plan.core, here, there, 1)
    qkv = jnp.concatenate([qkv[0, 0], qkv[0, 1], qkv[1, 0], qkv[1, 1]], axis=3).astype(F32)
    return [qkv[:, 0], qkv[:, 1], qkv[:, 2], out.astype(F32)], extra


def split_units(plan, fc_in):
    layers, rows, units = fc_in.shape
    value = fc_in.reshape(layers, rows, 2, plan.n // 4, 2, units // plan.n)
    value = jnp.transpose(value, (0, 4, 2, 1, 3, 5))
    return value.reshape(layers, 2, 2, rows, units // 4)


def gather_ffn_whole(plan, fc_in, fc_out):
    full = lax.all_gather(split_units(plan, fc_in[None])[0], ALL, axis=2, tiled=True)
    first, _ = choose(plan.core, full, 0)
    full = lax.all_gather(fc_out, ALL, axis=0, tiled=True)
    full = full.reshape(plan.n // 2, 2, fc_out.shape[0], fc_out.shape[1])
    second, _ = choose(plan.core, full, 1)
    return first, second.reshape(-1, fc_out.shape[1])


def gather_ffn(plan, order, here, there, fc_out):
    width = fc_out.shape[1]
    here, there, fc_out = order.tie(here, there, fc_out)
    value = [here.reshape(-1, width), there.reshape(-1, width), fc_out]
    value = order.done(jnp.concatenate(value, axis=0))
    other = plan.swap(value, "seq", plan.ranks)
    yield
    value, other = order.tie(value, other)
    value = order.done(jnp.stack([value, other]))
    other = plan.swap(value, "seq", 2)
    yield
    value, other = order.tie(value, other)
    size = fc_out.shape[0]
    first = jnp.concatenate([value[:, :-size], other[:, :-size]], axis=0)
    second = jnp.concatenate([value[:, -size:], other[:, -size:]], axis=0)
    first, second = order.done(first), order.done(second)
    first_there = plan.swap(first, "fsdp", plan.lo)
    second_there = plan.swap(second, "fsdp", plan.hi)
    yield
    first, second, first_there, second_there = order.tie(first, second, first_there, second_there)
    first = order.done(jnp.concatenate([first, first_there], axis=0))
    second = order.done(jnp.concatenate([second, second_there], axis=0))
    first_there = plan.swap(first, "fsdp", plan.hi)
    second_there = plan.swap(second, "fsdp", plan.lo)
    yield
    return first, second, first_there, second_there


def place_weights(place_ref, weights, w_in_ref, w_out_ref):
    if len(weights) == 2:
        w_in_ref[...] = weights[0][...]
        w_out_ref[...] = weights[1][...]
        return
    core, own = place_ref[0], place_ref[3]
    f, half, z = own // 2, own % 2, place_ref[4] // 2
    for number, ref in enumerate(weights):
        height = ref.shape[1]
        for block in range(8):
            one, other = block // 4, number // 2
            f_there = f ^ (one + 2 * other if number % 2 == 0 else 2 * one + other)
            device = f_there * 4 + (half ^ (block % 2)) * 2 + (z ^ (block // 2 % 2))
            if number % 2 == 1:
                place = pl.ds(pl.multiple_of(device * height, height), height)
                w_out_ref[place, :] = ref[block]
                continue
            rows = height // 4
            for piece in range(4):
                start = (device * 2 + (core ^ (piece // 2))) * rows
                place = pl.ds(pl.multiple_of(start, rows), rows)
                w_in_ref[piece % 2, place, :] = ref[block, piece * rows : (piece + 1) * rows, :]


def ffn_forward_kernel(count, place_ref, *refs):
    m_own, m_sib = refs[:2]
    weights = refs[2 : 2 + count]
    own_ref, sib_ref, kept_ref, w_in_ref, w_out_ref, total_ref = refs[2 + count :]
    step = pl.program_id(0)
    rows = m_own.shape[0]
    chunk = kept_ref.shape[2]

    @pl.when(step == 0)
    def _():
        place_weights(place_ref, weights, w_in_ref, w_out_ref)
        total_ref[...] = jnp.zeros_like(total_ref)

    middle = jnp.concatenate([m_own[...], m_sib[...]], axis=0)
    lanes = pl.ds(pl.multiple_of(step % 2 * chunk, chunk), chunk)
    before = mm(middle, w_in_ref[step // 2, :, lanes])
    bell = 0.5 * (1.0 + lax.erf(before * inv_root_two))
    active = (before * bell).astype(BF)
    kept_ref[0] = active
    kept_ref[1] = (bell + before * jnp.exp(-0.5 * before * before) * inv_root_two_pi).astype(BF)
    total_ref[...] += mm(active, w_out_ref[pl.ds(pl.multiple_of(step * chunk, chunk), chunk), :])

    @pl.when(step == 3)
    def _():
        own_ref[...] = total_ref[:rows, :]
        sib_ref[...] = total_ref[rows:, :].astype(BF)


def ffn_forward(places, middles, weights, units):
    rows, width = middles[0].shape
    chunk = units // 8
    block = (rows, width)
    return pl.pallas_call(
        functools.partial(ffn_forward_kernel, len(weights)),
        grid_spec=pltpu.PrefetchScalarGridSpec(
            num_scalar_prefetch=1,
            grid=(4,),
            in_specs=[whole(block)] * 2 + [whole(w.shape) for w in weights],
            out_specs=[
                whole(block), whole(block),
                pl.BlockSpec((2, 2 * rows, chunk), lambda i, p: (0, 0, i)),
            ],
            scratch_shapes=[
                pltpu.VMEM((2, width, 2 * chunk), BF),
                pltpu.VMEM((4 * chunk, width), BF),
                pltpu.VMEM((2 * rows, width), F32),
            ],
        ),
        out_shape=[
            struct(block, F32), struct(block, BF), struct((2, 2 * rows, 4 * chunk), BF),
        ],
        compiler_params=PARAMS,
        cost_estimate=FREE,
    )(places, *middles, *weights)


def ffn_backward_kernel(count, place_ref, *refs):
    g_own, g_sib, m_own, m_sib, kept_ref = refs[:5]
    weights = refs[5 : 5 + count]
    own_ref, sib_ref, in_send, in_keep, out_send, out_keep = refs[5 + count : 11 + count]
    w_in_ref, w_out_ref, total_ref = refs[11 + count :]
    step = pl.program_id(0)
    rows, width = g_own.shape
    chunk = kept_ref.shape[2]

    @pl.when(step == 0)
    def _():
        place_weights(place_ref, weights, w_in_ref, w_out_ref)
        total_ref[...] = jnp.zeros_like(total_ref)

    upper, part = step % 2, (step // 2 + 1 + place_ref[2]) % 2
    grads = jnp.concatenate([g_own[...], g_sib[...]], axis=0)
    units = pl.ds(pl.multiple_of((upper * 2 + part) * chunk, chunk), chunk)
    before_grad = (mm_t(grads, w_out_ref[units, :]) * kept_ref[1].astype(F32)).astype(BF)
    lanes = pl.ds(pl.multiple_of(part * chunk, chunk), chunk)
    total_ref[...] += mm_t(before_grad, w_in_ref[upper, :, lanes])
    half = width // 2
    for mine, ref in ((1 - place_ref[1], in_send), (place_ref[1], in_keep)):
        lanes = pl.ds(pl.multiple_of(mine * half, half), half)
        middle = jnp.concatenate([m_own[:, lanes], m_sib[:, lanes]], axis=0)
        ref[...] = mm_outer(middle, before_grad, BF).reshape(ref.shape)
    out_grad = mm_outer(kept_ref[0], grads, BF)

    @pl.when(step < 2)
    def _():
        out_send[0] = out_grad

    @pl.when(step >= 2)
    def _():
        out_keep[0] = out_grad

    @pl.when(step == 3)
    def _():
        own_ref[...] = total_ref[:rows, :]
        sib_ref[...] = total_ref[rows:, :].astype(BF)


def ffn_backward(places, grads, middles, kept, weights, rows_each):
    rows, width = grads[0].shape
    chunk = kept.shape[2] // 4

    def column(step, places):
        return step % 2 * 2 + (step // 2 + 1 + places[2]) % 2

    block = (rows, width)
    groups = width // 2 // rows_each if rows_each % 16 == 0 else 1
    tall = (groups, 2, width // 2 // groups, 2 * chunk)
    side = pl.BlockSpec(
        (groups, 1, tall[2], chunk), lambda i, p: (0, column(i, p) // 2, 0, column(i, p) % 2)
    )
    return pl.pallas_call(
        functools.partial(ffn_backward_kernel, len(weights)),
        grid_spec=pltpu.PrefetchScalarGridSpec(
            num_scalar_prefetch=1,
            grid=(4,),
            in_specs=[whole(block)] * 4
            + [pl.BlockSpec((2, 2 * rows, chunk), lambda i, p: (0, 0, column(i, p)))]
            + [whole(w.shape) for w in weights],
            out_specs=[
                whole(block), whole(block), side, side,
                pl.BlockSpec((1, chunk, width), lambda i, p: (jnp.minimum(i, 1), 0, 0)),
                pl.BlockSpec((1, chunk, width), lambda i, p: (jnp.maximum(i - 2, 0), 0, 0)),
            ],
            scratch_shapes=[
                pltpu.VMEM((2, width, 2 * chunk), BF),
                pltpu.VMEM((4 * chunk, width), BF),
                pltpu.VMEM((2 * rows, width), F32),
            ],
        ),
        out_shape=[
            struct(block, F32), struct(block, BF),
            struct(tall, BF), struct(tall, BF),
            struct((2, chunk, width), BF), struct((2, chunk, width), BF),
        ],
        compiler_params=PARAMS,
        cost_estimate=FREE,
    )(places, *grads, *middles, kept, *weights)


def scatter_ffn(plan, order, early, in_send, in_keep, out_send, out_keep):
    hi, lo, half = ("fsdp", plan.hi), ("fsdp", plan.lo), ("seq", plan.ranks)
    inner = [("fsdp", b) for b in reversed(plan.f_bits) if b not in (plan.hi, plan.lo)]
    z_names = [("seq", b) for b in reversed(plan.z_bits)]
    tail = (*inner, half, *z_names)
    width = out_keep.shape[-1]
    count = 2 ** (1 + len(tail))
    if in_keep.shape[0] == 1:
        shape = in_keep.shape

        def spread_rows(value):
            value = value.reshape(2, count, shape[2] // count, width)
            return jnp.swapaxes(value, 0, 1)

        in_send, in_keep = spread_rows(in_send), spread_rows(in_keep)

    def summed(first, keep, there):
        shape = (2,) * (1 + len(tail)) + (-1, width)
        return Sum(plan, order, (first, *tail), [keep.reshape(shape), there.reshape(shape)])

    first = summed(lo, in_keep, plan.swap(in_send, *hi))
    second = summed(hi, out_keep, plan.swap(out_send, *lo))
    yield
    first_names = [lo, *inner, *z_names]
    if early:
        first_names = [*z_names, lo, *inner]
    steps = list(zip(first_names, [hi, *inner, *z_names])) + [(half, half)]
    for one, two in steps:
        if one == two:
            first.tie()
            second.tie()
            send = jnp.stack([first.sending(one), second.sending(one)])
            there = plan.swap(order.done(send), *one)
            first.receive(there[0])
            second.receive(there[1])
        else:
            first.step(one)
            second.step(two)
        yield
        if not early and one not in (lo, hi):
            first.settle()
            second.settle()
            yield
    first.tie()
    second.tie()
    total = order.done(second.total())
    return first.total().astype(BF).reshape(2, 2, -1, width), total


def finish_ffn(plan, order, totals):
    fc_in = jnp.stack([a for a, _ in totals])
    here, send = choose(plan.core, fc_in, 2)
    there = plan.swap(order.done(send), "seq", 1)
    yield
    here, there = order.tie(here, there)
    layers, _, rows, _ = here.shape
    pair = [jnp.swapaxes(v, 1, 2).reshape(layers, rows, plan.n // 2, -1) for v in (here, there)]
    fc_in = stack_by(plan.core, *pair, 3)
    fc_in = order.done(fc_in.reshape(layers, rows, -1).astype(F32))
    return fc_in, jnp.stack([b for _, b in totals])


def gather_vectors(plan, order, vectors):
    layers, count, own = vectors.shape
    value = order.done(vectors.reshape(1, -1))
    names = [("seq", b) for b in [1] + plan.z_bits + [plan.ranks]]
    names += [("fsdp", b) for b in plan.f_bits]
    for name in names:
        there = plan.swap(value, *name)
        yield
        value, there = order.tie(value, there)
        mine = bit_of(plan.f if name[0] == "fsdp" else plan.s, name[1])
        value = order.done(stack_by(mine, value, there, 0).reshape(-1, value.shape[-1]))
    return natural_vectors(plan, value, layers, count)


def natural_vectors(plan, value, layers, count):
    value = value.reshape(plan.n, layers, count, -1)
    return jnp.transpose(value, (1, 2, 0, 3)).reshape(layers, count, -1).astype(F32)


def sum_vectors(plan, vectors):
    count, width = vectors.shape
    value = vectors.reshape(count, plan.n, width // plan.n)
    value = jnp.transpose(value, (1, 0, 2)).reshape(plan.n, -1)
    value = lax.all_to_all(value, ALL, split_axis=0, concat_axis=0, tiled=True)
    return jnp.sum(value, axis=0).reshape(count, width // plan.n)


def local(
    mesh_shape,
    inputs,
    segment_ids,
    query_weight,
    key_weight,
    value_weight,
    out_weight,
    fc_in_weight,
    fc_out_weight,
    attn_gain,
    attn_shift,
    ffn_gain,
    ffn_shift,
    cotangent,
):
    layers, _, width = query_weight.shape
    plan = Plan(mesh_shape, width, fc_in_weight.shape[2])
    places = plan.scalars()
    head_dim = width // HEADS

    def to_halves(value):
        mine, other = choose(plan.half, value, 0)
        return jnp.concatenate([mine, plan.swap(other, "seq", plan.ranks)], axis=0)

    def from_halves(value):
        size = value.shape[0] // 2
        there = plan.swap(value[size:].astype(BF), "seq", plan.ranks).astype(F32)
        return stack_by(plan.half, value[:size], there, 0)

    order, tasks = Order(), Tasks()
    matrices = (query_weight, key_weight, value_weight, out_weight)
    vectors = jnp.stack([attn_gain, attn_shift, ffn_gain, ffn_shift], axis=1)
    tokens, units = 2 * inputs.shape[1], fc_in_weight.shape[2]
    marks = jnp.pad(
        segment_ids.astype(BF)[:, None, :], ((0, 0), (0, 15), (0, width - inputs.shape[1]))
    )

    def with_marks(value):
        mine, other = choose(plan.half, value, 0)
        there = plan.swap(other, "seq", plan.ranks)
        there, mine = order.tie(there, mine)
        size = tokens // 2
        low = jnp.concatenate([mine[:size], there[:size]], axis=0)
        row = jnp.concatenate([mine[size:, :size], there[size:, :size]], axis=1)
        row = jnp.pad(row, ((0, 0), (0, width - tokens)))
        return order.done(jnp.concatenate([low, row], axis=0)), low

    marked = jnp.concatenate([inputs, marks], axis=1)
    if plan.fast:
        columns = tasks.add(rank_columns(plan, order, matrices, vectors.reshape(1, -1)))
        fc_here, fc_send = choose(plan.core, split_units(plan, fc_in_weight), 1)
        fc_there = plan.swap(order.done(fc_send), "seq", 1)

        def fetch(layer):
            parts = (here[layer], there[layer], out[layer]) + ((rows,) if layer == 0 else ())
            return tasks.add(gather_attention(plan, order, places, parts))

        def fetch_ffn(layer):
            parts = (fc_here[layer], fc_there[layer], fc_out_weight[layer])
            return tasks.add(gather_ffn(plan, order, *parts))

        ffn = [fetch_ffn(0)]
        tasks.drain(columns)
        here, there, out, rows = columns.result
        attention = [fetch(0)]
        marked, x_low = with_marks(marked)
        x_pieces = group_pieces(plan, marked)
        ffn[0].run()
        attention[0].run()
        attention[0].run()
        ffn.append(fetch_ffn(1))
        tasks.drain(attention[0])
        ffn[0].run()
    else:
        marked, x_low = with_marks(marked)
        x_pieces = group_pieces(plan, marked)
        upstream = to_halves(cotangent)
        ffn = [
            Task.finished(gather_ffn_whole(plan, fc_in_weight[k], fc_out_weight[k]))
            for k in range(layers)
        ]
        vectors = tasks.add(gather_vectors(plan, order, vectors))
        tasks.drain(vectors)
        vectors = vectors.result
        attention = [Task.finished(m) for m in gather_attention_whole(plan, matrices)]
    ids = jnp.concatenate([p[tokens, :tokens] for p in x_pieces]).astype(jnp.int32)

    hidden = x_low
    records = []
    for layer in range(layers):
        tasks.drain(attention[layer])
        if plan.fast and layer == 0:
            vectors = natural_vectors(plan, attention[0].result[2], layers, 4)
        gains = [vectors[layer, k][None] for k in range(4)]
        w_qkv, w_out = attention[layer].result[:2]
        tied = order.tie(*x_pieces, w_qkv, w_out, ids)
        x_pieces = tied[:-3]
        qkv, att, keep, send = attn_forward(x_pieces, *tied[-3:], head_dim)
        order.done(send)
        if plan.fast and layer == 0:
            ffn[0].run()
            ffn[1].run()
            (send,) = order.tie(send)
        parts = group_sum(plan, order, keep, plan.swap(send, "seq", 1))
        if plan.fast and layer == 0:
            attention.append(fetch(1))
        if layer > 0:
            tasks.drain(ffn[layer])
            weights = order.tie(*ffn[layer].result)
            order.done(weights[-1])
        middle, mid_low, normed_attn, inverse_attn = norm_forward(
            order.tie(hidden, *parts), gains[0], gains[1], tokens
        )
        order.done(mid_low)
        middles = (mid_low, plan.swap(mid_low, "seq", 1))
        if plan.fast and layer == 0:
            attention[1].run()
        if layer == 0:
            tasks.drain(ffn[layer])
            weights = ffn[layer].result
        tied = order.tie(*middles, *weights)
        own, sibling, kept = ffn_forward(places, tied[:2], tied[2:], units)
        order.done(sibling)
        sibling = plan.swap(sibling, "seq", 1)
        if plan.fast and layer == 0:
            attention[1].run()
            ffn[1].run()
            (cotangent,) = order.tie(cotangent)
            upstream = to_halves(cotangent)
        hidden, x_low, normed_ffn, inverse_ffn = norm_forward(
            order.tie(middle, own, sibling), gains[2], gains[3], tokens
        )
        order.done(x_low)
        next_pieces = group_pieces(plan, x_low) if layer + 1 < layers else None
        if plan.fast and layer == 0:
            ffn[1].run()
            tasks.drain(attention[1])
            (upstream,) = order.tie(upstream)
            order.done(upstream)
        records.append(
            (x_pieces, qkv, att, normed_attn, inverse_attn, normed_ffn, inverse_ffn, kept, middles)
        )
        x_pieces = next_pieces
    upstream = [upstream]
    outputs = from_halves(hidden)

    grads, vector_grads = [None] * layers, [None] * layers
    older = ()
    for layer in reversed(range(layers)):
        (
            x_pieces, qkv, att, normed_attn, inverse_attn, normed_ffn, inverse_ffn, kept, middles,
        ) = records[layer]
        gains = vectors[layer]
        w_qkv, w_out = attention[layer].result[:2]
        sum_grad, ff_grad, gain_ffn_grad, shift_ffn_grad = norm_backward(
            order.tie(*upstream), normed_ffn, inverse_ffn, gains[2:3]
        )
        order.done(ff_grad)
        ff_sibling = plan.swap(ff_grad, "seq", 1)
        if older:
            older[0].run()
        tied = order.tie(ff_grad, ff_sibling, *middles, kept)
        own, sibling, *ffn_grads = ffn_backward(
            places, tied[:2], tied[2:4], tied[4], ffn[layer].result, 2 * fc_in_weight.shape[1]
        )
        order.done(sibling)
        ffn_task = tasks.add(scatter_ffn(plan, order, layer == 0, *ffn_grads))
        sibling = plan.swap(sibling, "seq", 1)
        if older:
            older[0].run()
            older[1].run()
        tied = order.tie(sum_grad, own, sibling)
        attn_sum_grad, branch_grad, gain_attn_grad, shift_attn_grad = norm_backward(
            tied, normed_attn, inverse_attn, gains[0:1]
        )
        order.done(branch_grad)
        g_pieces = group_pieces(plan, branch_grad)
        vector_grads[layer] = (gain_attn_grad, shift_attn_grad, gain_ffn_grad, shift_ffn_grad)
        extra = jnp.zeros((8, 16, width // plan.ranks), BF)
        if layer == 0:
            summed = jnp.concatenate([v for member in vector_grads for v in member], axis=0)
            if plan.fast:
                extra = summed.reshape(4 * layers, 8, plan.ranks, -1)
                extra = jnp.transpose(extra, (1, 2, 0, 3)).reshape(8, plan.ranks, -1)
                extra = jnp.pad(extra.astype(BF), ((0, 0), (0, 16 - plan.ranks), (0, 0)))
        g_pieces = order.tie(*g_pieces)
        order.done(g_pieces[-1])
        if older:
            older[0].run()
        else:
            (outputs,) = order.tie(outputs)
            order.done(outputs)
        tied = order.tie(*g_pieces, qkv)
        g_pieces = tied[:-1]
        dqkv, keep, send = attn_backward(g_pieces, tied[-1], w_qkv, w_out, ids, head_dim)
        order.done(send)
        if older:
            older[0].run()
            (send,) = order.tie(send)
        there = plan.swap(send, "seq", 1)
        ffn_task.run()
        upstream = [attn_sum_grad] + group_sum(plan, order, keep, there)
        if plan.fast:
            attn_task = tasks.add(
                scatter_attention(
                    plan, order, places, x_pieces, g_pieces, dqkv, att, extra, layer == 0
                )
            )
        else:
            attn_task = Task.finished(scatter_attention_whole(plan, x_pieces, g_pieces, dqkv, att))
        grads[layer] = (ffn_task, attn_task)
        if layer > 0:
            older = grads[layer]
    rows_grad = add_parts(order.tie(*upstream), tokens)
    order.done(rows_grad)
    input_grad = from_halves(rows_grad)
    ffn_task.run()
    if older:
        older[1].run()
    attn_task.run()
    (input_grad,) = order.tie(input_grad)
    order.done(input_grad)
    ffn_task.run()
    attn_task.run()
    if older:
        older[1].run()
        older[0].run()
        older[1].run()
    tasks.drain(ffn_task)
    for member in grads:
        tasks.drain(member[0])
    fc_task = tasks.add(finish_ffn(plan, order, [f.result for f, _ in grads]))
    for member in grads:
        tasks.drain(member[1])
    if plan.fast:
        attn_task = tasks.add(finish_attention(plan, order, [a.result for _, a in grads]))
        tasks.finish()
        attn_grads, summed = attn_task.result
    else:
        tasks.finish()
        summed = sum_vectors(plan, summed)
        attn_grads = [jnp.stack([a.result[k] for _, a in grads]) for k in range(4)]
    fc_in_grad, fc_out_grad = fc_task.result
    summed = summed.reshape(layers, 4, -1)
    return (
        outputs, input_grad, *attn_grads, fc_in_grad, fc_out_grad, *(summed[:, k] for k in range(4)),
    )


def solution(mesh):
    tokens = P("fsdp", "seq", None)
    matrix = P(None, ("fsdp", "seq"), None)
    vector = P(None, ("fsdp", "seq"))
    return jax.shard_map(
        functools.partial(local, dict(mesh.shape)),
        mesh=mesh,
        in_specs=(tokens, P("fsdp", "seq"), *[matrix] * 6, *[vector] * 4, tokens),
        out_specs=(tokens, tokens, *[matrix] * 6, *[vector] * 4),
        check_vma=False,
    )
```

```python
import functools

import jax
import jax.numpy as jnp
from jax import lax
from jax.experimental import pallas as pl
from jax.experimental.pallas import tpu as pltpu
from jax.sharding import PartitionSpec as P

HEADS = 16
NEG_FILL = -1e30
NORM_EPS = 1e-05
inv_root_two = 0.7071067811865476
inv_root_two_pi = 0.3989422804014327
BF = jnp.bfloat16
F32 = jnp.float32
ALL = ("fsdp", "seq")
PARAMS = pltpu.CompilerParams(vmem_limit_bytes=56 * 1024 * 1024)


def mm(a, b, out=F32):
    return lax.dot_general(a, b, (((1,), (0,)), ((), ())), preferred_element_type=F32).astype(out)


def mm_t(a, b, out=F32):
    return lax.dot_general(a, b, (((1,), (1,)), ((), ())), preferred_element_type=F32).astype(out)


def mm_outer(a, b, out=F32):
    return lax.dot_general(a, b, (((0,), (0,)), ((), ())), preferred_element_type=F32).astype(out)


def struct(shape, dtype):
    return jax.ShapeDtypeStruct(shape, dtype)


def whole(shape):
    return pl.BlockSpec(shape, lambda *_: (0,) * len(shape))


FREE = pl.CostEstimate(flops=0, bytes_accessed=0, transcendentals=0)


class Plan:
    def __init__(self, mesh_shape, width, hidden_units):
        self.n_f, self.n_s = mesh_shape["fsdp"], mesh_shape["seq"]
        self.n = self.n_f * self.n_s
        self.ranks = self.n_s // 2
        self.f = lax.axis_index("fsdp")
        self.s = lax.axis_index("seq")
        self.half = self.s // self.ranks
        self.rank = self.s % self.ranks
        self.core = self.s % 2
        self.f_bits = [1 << k for k in range(self.n_f.bit_length() - 1)]
        self.z_bits = [1 << k for k in range(1, self.ranks.bit_length() - 1)]
        self.hi, self.lo = self.f_bits[-1], self.f_bits[-2]
        self.f_hi, self.f_lo = bit_of(self.f, self.hi), bit_of(self.f, self.lo)
        self.fast = (
            self.n_f == 4
            and self.n_s == 8
            and (width // self.n) % 32 == 0
            and (hidden_units // self.n) % 128 == 0
        )

    def swap(self, value, axis_name, bit):
        count = self.n_f if axis_name == "fsdp" else self.n_s
        return lax.ppermute(value, axis_name, [(i, i ^ bit) for i in range(count)])

    def scalars(self):
        return jnp.stack([self.core, self.f_hi, self.f_lo, self.f * 2 + self.half, self.rank]).astype(
            jnp.int32
        )


def bit_of(index, bit):
    return (index // bit) % 2


def stack_by(mine, here, there, axis):
    return jnp.where(
        mine == 0, jnp.stack([here, there], axis=axis), jnp.stack([there, here], axis=axis)
    )


def choose(mine, value, axis):
    first = lax.index_in_dim(value, 0, axis, keepdims=False)
    second = lax.index_in_dim(value, 1, axis, keepdims=False)
    return jnp.where(mine == 0, first, second), jnp.where(mine == 0, second, first)


def group_pieces(plan, value):
    pieces = [value]
    for bit in plan.z_bits:
        pieces = pieces + [plan.swap(p, "seq", bit) for p in pieces]
    return pieces + [plan.swap(p, "seq", 1) for p in pieces]


def group_sum(plan, order, keep, there):
    parts = [keep, there]
    size = keep.shape[0]
    for bit in reversed(plan.z_bits):
        size = size // 2
        tied = order.tie(*parts)
        out = sum(p[size : 2 * size].astype(F32) for p in tied).astype(BF)
        parts = parts + [plan.swap(order.done(out), "seq", bit)]
    return parts


STEPS = {
    "start": ["f0", "a0", "x", "a0", "F1", "A0", "f0"],
    "after_attention": ["f0", "f1", "B1"],
    "attention_sum": [],
    "after_norm": ["a1"],
    "ffn_sum": ["a1", "f1", "cot"],
    "next_rows": ["f1", "A1", "cotD"],
    "weights_early": [0, 1],
    "upper": [
        [],
        [],
        ["OD"],
        [],
        ["c0", "Z", "W"],
    ],
    "lowest": [
        ["o0"],
        ["o0", "o1"],
        ["o0", "c0"],
        ["o0", "c0"],
        ["W", "Z", "c1", "c0", "o1", "c1", "G", "o1", "o0", "o1"],
    ],
}


def add_parts(parts, rows):
    return sum(p[:rows].astype(F32) for p in parts)


class Order:
    def __init__(self):
        self.last = None

    def tie(self, *values):
        if self.last is None:
            return values
        return lax.optimization_barrier((*values, self.last))[:-1]

    def done(self, value):
        self.last = value
        return value


class Task:
    def __init__(self, steps):
        self.steps, self.result, self.running = steps, None, True
        self.run()

    @staticmethod
    def finished(result):
        task = Task(iter(()))
        task.result = result
        return task

    def run(self):
        if self.running:
            try:
                next(self.steps)
            except StopIteration as stop:
                self.running, self.result = False, stop.value


class Tasks:
    def __init__(self):
        self.open = []

    def add(self, steps):
        task = Task(steps)
        self.open.append(task)
        return task

    def run(self, task):
        task.run()

    def drain(self, task):
        while task.running:
            task.run()

    def slot(self, count):
        self.open = [t for t in self.open if t.running]
        for task in self.open[:count]:
            task.run()

    def finish(self):
        while self.open:
            self.slot(len(self.open))


class Sum:
    def __init__(self, plan, order, names, parts):
        self.plan, self.order, self.names = plan, order, tuple(names)
        self.parts = [(p, self.names) for p in parts]
        self.chosen = {}

    def pick(self, part, chosen):
        value, names = part
        rest = value.shape[len(names) :]
        zero = jnp.zeros((), jnp.int32)
        start = [chosen.get(n, zero) for n in names] + [zero] * len(rest)
        size = [1 if n in chosen else 2 for n in names] + list(rest)
        left = [d for n, d in zip(names, size) if n not in chosen]
        return lax.dynamic_slice(value, start, size).reshape(*left, *rest)

    def tie(self):
        tied = self.order.tie(*[p for p, _ in self.parts])
        self.parts = [(p, names) for p, (_, names) in zip(tied, self.parts)]

    def sending(self, name, kind=BF):
        plan = self.plan
        mine = bit_of(plan.f if name[0] == "fsdp" else plan.s, name[1]).astype(jnp.int32)
        there = {**self.chosen, name: 1 - mine}
        out = sum(self.pick(p, there).astype(F32) for p in self.parts).astype(kind)
        self.chosen[name] = mine
        return out

    def receive(self, value):
        left = [n for n in self.names if n not in self.chosen]
        self.parts.append((value, tuple(left)))

    def step(self, name):
        self.tie()
        send = self.order.done(self.sending(name))
        self.receive(self.plan.swap(send, *name))

    def settle(self):
        self.tie()
        self.order.done(self.parts[-1][0])

    def total(self):
        return sum(self.pick(p, self.chosen).astype(F32) for p in self.parts)


def norm_rows(summed):
    center = jnp.mean(summed, axis=-1, keepdims=True)
    offset = summed - center
    spread = jnp.mean(offset * offset, axis=-1, keepdims=True)
    inverse = lax.rsqrt(spread + NORM_EPS)
    return offset * inverse, inverse


def norm_forward_kernel(count, *refs):
    parts, (gain_ref, shift_ref) = refs[:count], refs[count : count + 2]
    out_ref, low_ref, normed_ref, inverse_ref = refs[count + 2 :]
    summed = parts[0][...].astype(F32)
    for part in parts[1:]:
        summed = summed + part[...].astype(F32)
    normed, inverse = norm_rows(summed)
    result = normed * gain_ref[...] + shift_ref[...]
    out_ref[...] = result
    low_ref[...] = result.astype(BF)
    normed_ref[...] = normed
    inverse_ref[...] = inverse


def norm_forward(parts, gain, shift, rows):
    width = gain.shape[1]
    block = (rows, width)
    return pl.pallas_call(
        functools.partial(norm_forward_kernel, len(parts)),
        grid=(1,),
        in_specs=[whole(block)] * len(parts) + [whole((1, width))] * 2,
        out_specs=[whole(block)] * 3 + [whole((rows, 1))],
        out_shape=[
            struct(block, F32), struct(block, BF), struct(block, F32), struct((rows, 1), F32),
        ],
        compiler_params=PARAMS,
        cost_estimate=FREE,
    )(*parts, gain, shift)


def norm_backward_kernel(count, *refs):
    parts, (normed_ref, inverse_ref, gain_ref) = refs[:count], refs[count : count + 3]
    out_ref, low_ref, gain_grad_ref, shift_grad_ref = refs[count + 3 :]
    upstream = parts[0][...].astype(F32)
    for part in parts[1:]:
        upstream = upstream + part[...].astype(F32)
    normed = normed_ref[...]
    gain_grad_ref[...] = jnp.sum(upstream * normed, axis=0, keepdims=True)
    shift_grad_ref[...] = jnp.sum(upstream, axis=0, keepdims=True)
    scaled = upstream * gain_ref[...]
    inner = (
        scaled
        - jnp.mean(scaled, axis=-1, keepdims=True)
        - normed * jnp.mean(scaled * normed, axis=-1, keepdims=True)
    )
    result = inner * inverse_ref[...]
    out_ref[...] = result
    low_ref[...] = result.astype(BF)


def norm_backward(parts, normed, inverse, gain):
    rows, width = normed.shape
    return pl.pallas_call(
        functools.partial(norm_backward_kernel, len(parts)),
        grid=(1,),
        in_specs=[whole((rows, width))] * (len(parts) + 1) + [whole((rows, 1)), whole((1, width))],
        out_specs=[whole((rows, width))] * 2 + [whole((1, width))] * 2,
        out_shape=[
            struct((rows, width), F32), struct((rows, width), BF),
            struct((1, width), F32), struct((1, width), F32),
        ],
        compiler_params=PARAMS,
        cost_estimate=FREE,
    )(*parts, normed, inverse, gain)


def pick_head(lanes, head, head_dim):
    return (lanes >= head * head_dim) & (lanes < (head + 1) * head_dim)


def attn_forward_kernel(head_dim, count, *refs):
    pieces = refs[:count]
    w_qkv_ref, w_out_ref, ids_q_ref, ids_k_ref = refs[count : count + 4]
    qkv_ref, att_ref, lse_ref, keep_ref, send_ref = refs[count + 4 :]
    step = pl.program_id(0)
    rows, width = att_ref.shape

    @pl.when(step == 0)
    def _():
        w_qkv = w_qkv_ref[...]
        for index, piece in enumerate(pieces):
            qkv = mm(piece[...], w_qkv).astype(BF)
            part = pl.ds(index * rows, rows)
            qkv_ref[part, :width] = (qkv[:, :width].astype(F32) * head_dim**-0.5).astype(BF)
            qkv_ref[part, width:] = qkv[:, width:]

    queries = qkv_ref[pl.ds(pl.multiple_of(step * rows, rows), rows), :width]
    keys, values = qkv_ref[:, width : 2 * width], qkv_ref[:, 2 * width :]
    lanes = lax.broadcasted_iota(jnp.int32, (1, width), 1)
    allowed = ids_q_ref[...] == ids_k_ref[...]
    total = jnp.zeros((rows, width), F32)
    log_total = jnp.zeros(lse_ref.shape, F32)
    columns = lax.broadcasted_iota(jnp.int32, (1, lse_ref.shape[1]), 1)
    for head in range(width // head_dim):
        here = pick_head(lanes, head, head_dim)
        scores = mm_t(jnp.where(here, queries, jnp.zeros_like(queries)), keys)
        scores = jnp.where(allowed, scores, NEG_FILL)
        largest = jnp.max(scores, axis=1, keepdims=True)
        weights = jnp.exp(scores - largest)
        added = jnp.sum(weights, axis=1, keepdims=True)
        total = jnp.where(here, mm(weights.astype(BF), values) * (1.0 / added), total)
        log_total = jnp.where(columns == head, largest + jnp.log(added), log_total)
    lse_ref[...] = log_total
    attended = total.astype(BF)
    att_ref[...] = attended
    branch = mm(attended, w_out_ref[...])

    @pl.when(step < count // 2)
    def _():
        keep_ref[...] = branch

    @pl.when(step >= count // 2)
    def _():
        send_ref[...] = branch.astype(BF)


def attn_forward(pieces, w_qkv, w_out, ids, head_dim):
    count, features = len(pieces), pieces[0].shape[1]
    rows = ids.shape[0] // count
    tokens, width = count * rows, w_out.shape[0]
    half = count // 2
    heads = width // head_dim
    return pl.pallas_call(
        functools.partial(attn_forward_kernel, head_dim, count),
        grid=(count,),
        in_specs=[whole((rows, features))] * count
        + [
            whole(w_qkv.shape),
            whole(w_out.shape),
            pl.BlockSpec((rows, 1), lambda i: (i, 0)),
            whole((1, tokens)),
        ],
        out_specs=[
            whole((tokens, 3 * width)),
            pl.BlockSpec((rows, width), lambda i: (i, 0)),
            pl.BlockSpec((rows, 128), lambda i: (i, 0)),
            pl.BlockSpec((rows, features), lambda i: (jnp.minimum(i, half - 1), 0)),
            pl.BlockSpec((rows, features), lambda i: (jnp.maximum(i - half, 0), 0)),
        ],
        out_shape=[
            struct((tokens, 3 * width), BF),
            struct((tokens, width), BF),
            struct((tokens, 128), F32),
            struct((half * rows, features), F32),
            struct((half * rows, features), BF),
        ],
        compiler_params=PARAMS,
        cost_estimate=FREE,
    )(*pieces, w_qkv, w_out, ids.reshape(tokens, 1), ids.reshape(1, tokens))


def attn_backward_kernel(head_dim, count, *refs):
    pieces = refs[:count]
    qkv_ref, att_ref, lse_ref, w_qkv_ref, w_out_ref, ids_q_ref, ids_k_ref = refs[count : count + 7]
    dqkv_ref, keep_ref, send_ref, grad_ref, dk_ref, dv_ref = refs[count + 7 :]
    step = pl.program_id(0)
    rows = pieces[0].shape[0]
    width = grad_ref.shape[1]

    @pl.when(step == 0)
    def _():
        w_out = w_out_ref[...]
        for index, piece in enumerate(pieces):
            grad_ref[pl.ds(index * rows, rows), :] = mm_t(piece[...], w_out, BF)
        dk_ref[...] = jnp.zeros_like(dk_ref)
        dv_ref[...] = jnp.zeros_like(dv_ref)

    place = pl.ds(pl.multiple_of(step * rows, rows), rows)
    queries, grads = qkv_ref[place, :width], grad_ref[place, :]
    keys, values = qkv_ref[:, width : 2 * width], qkv_ref[:, 2 * width :]
    lanes = lax.broadcasted_iota(jnp.int32, (1, width), 1)
    allowed = ids_k_ref[...] == ids_q_ref[...]
    log_total = lse_ref[...].T
    through = grads.astype(F32) * att_ref[...].astype(F32)
    shape = (width, lse_ref.shape[1])
    heads = lax.broadcasted_iota(jnp.int32, shape, 0) // head_dim
    heads = heads == lax.broadcasted_iota(jnp.int32, shape, 1)
    delta = lax.dot_general(
        jnp.where(heads, 1.0, 0.0), through, (((0,), (1,)), ((), ())),
        preferred_element_type=F32, precision=lax.Precision.HIGHEST,
    )
    dq = jnp.zeros((rows, width), F32)
    for head in range(width // head_dim):
        here = pick_head(lanes, head, head_dim)
        q_head = jnp.where(here, queries, jnp.zeros_like(queries))
        g_head = jnp.where(here, grads, jnp.zeros_like(grads))
        scores = mm_t(keys, q_head) - log_total[head : head + 1, :]
        probs = jnp.exp(jnp.where(allowed, scores, NEG_FILL))
        prob_grad = mm_t(values, g_head)
        score_grad = (probs * (prob_grad - delta[head : head + 1, :])).astype(BF)
        dk_ref[...] += mm(score_grad, q_head)
        dv_ref[...] += mm(probs.astype(BF), g_head)
        dq = jnp.where(here, mm_outer(score_grad, keys), dq)
    dqkv_ref[place, :width] = (dq * head_dim**-0.5).astype(BF)

    @pl.when(step == count - 1)
    def _():
        dqkv_ref[:, width : 2 * width] = dk_ref[...].astype(BF)
        dqkv_ref[:, 2 * width :] = dv_ref[...].astype(BF)
        w_qkv = w_qkv_ref[...]
        half = count // 2
        for index in range(count):
            part = mm_t(dqkv_ref[pl.ds(index * rows, rows), :], w_qkv)
            if index < half:
                keep_ref[pl.ds(index * rows, rows), :] = part
            else:
                send_ref[pl.ds((index - half) * rows, rows), :] = part.astype(BF)


def attn_backward(pieces, qkv, att, lse, w_qkv, w_out, ids, head_dim):
    count = len(pieces)
    rows, features = pieces[0].shape
    tokens, width = count * rows, w_out.shape[0]
    half = tokens // 2
    return pl.pallas_call(
        functools.partial(attn_backward_kernel, head_dim, count),
        grid=(count,),
        in_specs=[whole((rows, features))] * count
        + [
            whole(qkv.shape),
            pl.BlockSpec((rows, width), lambda i: (i, 0)),
            pl.BlockSpec((rows, lse.shape[1]), lambda i: (i, 0)),
            whole(w_qkv.shape),
            whole(w_out.shape),
            pl.BlockSpec((1, rows), lambda i: (0, i)),
            whole((tokens, 1)),
        ],
        out_specs=[
            whole((tokens, 3 * width)), whole((half, features)), whole((half, features)),
        ],
        out_shape=[
            struct((tokens, 3 * width), BF), struct((half, features), F32),
            struct((half, features), BF),
        ],
        scratch_shapes=[
            pltpu.VMEM((tokens, width), BF),
            pltpu.VMEM((tokens, width), F32),
            pltpu.VMEM((tokens, width), F32),
        ],
        compiler_params=PARAMS,
        cost_estimate=FREE,
    )(*pieces, qkv, att, lse, w_qkv, w_out, ids.reshape(1, tokens), ids.reshape(tokens, 1))


def attn_weights_kernel(count, place_ref, *refs):
    x_refs, g_refs = refs[:count], refs[count : 2 * count]
    dqkv_ref, att_ref, extra_ref = refs[2 * count : 2 * count + 3]
    a_send, a_keep, b_send, b_keep = refs[2 * count + 3 :]
    width = att_ref.shape[1]
    x_all = jnp.concatenate([r[...] for r in x_refs], axis=0)
    g_all = jnp.concatenate([r[...] for r in g_refs], axis=0)
    grad = mm_outer(x_all, dqkv_ref[...], BF)
    out = mm_outer(att_ref[...], g_all, BF)
    height, small = grad.shape[0] // 8, out.shape[0] // 8

    def put_a(block, ref):
        place = block % 4
        rows = grad[block * height : (block + 1) * height]
        ref[place, :height, :] = rows[:, :width]
        ref[place, height : 2 * height, :] = rows[:, width : 2 * width]

    def put_b(block, ref):
        place = block // 4 * 2 + block % 2
        ref[place, :height, :] = grad[block * height : (block + 1) * height, 2 * width :]
        part = out[block * small : (block + 1) * small]
        for piece in range(4):
            start = height + piece * small
            ref[place, start : start + small, :] = part[:, piece * width : (piece + 1) * width]
        ref[place, 2 * height :, :] = extra_ref[block]

    for block in range(8):
        hi, lo = block // 4, (block // 2) % 2
        pl.when(place_ref[1] != hi)(functools.partial(put_a, block, a_send))
        pl.when(place_ref[1] == hi)(functools.partial(put_a, block, a_keep))
        pl.when(place_ref[2] != lo)(functools.partial(put_b, block, b_send))
        pl.when(place_ref[2] == lo)(functools.partial(put_b, block, b_keep))


def attn_weights(places, x_pieces, g_pieces, dqkv, att, extra):
    count = len(x_pieces)
    rows, features = g_pieces[0].shape
    width = att.shape[1]
    high = 2 * features // 8
    parts = [(4, high, width)] * 2 + [(4, high + extra.shape[1], width)] * 2
    return pl.pallas_call(
        functools.partial(attn_weights_kernel, count),
        grid_spec=pltpu.PrefetchScalarGridSpec(
            num_scalar_prefetch=1,
            grid=(1,),
            in_specs=[whole((rows, features))] * (2 * count)
            + [
                whole(dqkv.shape),
                whole(att.shape),
                whole(extra.shape),
            ],
            out_specs=[whole(p) for p in parts],
        ),
        out_shape=[struct(p, BF) for p in parts],
        compiler_params=PARAMS,
        cost_estimate=FREE,
    )(places, *x_pieces, *g_pieces, dqkv, att, extra)


def assemble_kernel(place_ref, a_own, a_other, b_own, b_other, qkv_ref, out_ref, *extra_ref):
    own, rank = place_ref[3], place_ref[4]
    height, width = a_own.shape[1] // 8, a_own.shape[2]
    ranks = 4
    for block in range(8):
        a_ref = a_own if block < 4 else a_other
        b_ref = b_own if block < 4 else b_other
        b_block = (block % 4) // 2 * 4 + block // 4 * 2 + block % 2
        if extra_ref:
            rows = b_ref[block % 4, 8 * height :, :].astype(F32)
        for inner in range(4):
            rank_there = rank ^ ((inner // 2) + (inner % 2) * 2)
            start = ((own ^ block) * ranks + rank_there) * height
            place = pl.ds(pl.multiple_of(start, height), height)
            qkv_ref[place, :width] = a_ref[block % 4, inner * height : (inner + 1) * height, :]
            first = (4 + inner) * height
            qkv_ref[place, width : 2 * width] = a_ref[block % 4, first : first + height, :]
            device = (own ^ b_block) * ranks + rank_there
            place = pl.ds(pl.multiple_of(device * height, height), height)
            qkv_ref[place, 2 * width :] = b_ref[block % 4, inner * height : (inner + 1) * height, :]
            place = pl.ds(pl.multiple_of((own ^ b_block) * height, height), height)
            out_ref[place, inner * width : (inner + 1) * width] = b_ref[
                block % 4, first : first + height, :
            ]
            if extra_ref:
                extra_ref[0][pl.ds(device, 1), :] = rows[inner : inner + 1, :]


def assemble(places, a_own, a_other, b_own, b_other):
    _, high, width = a_own.shape
    features = 4 * high
    shapes = [struct((features, 3 * width), BF), struct((width, features), BF)]
    if b_own.shape[1] > high:
        shapes.append(struct((32, width), F32))
    return pl.pallas_call(
        assemble_kernel,
        grid_spec=pltpu.PrefetchScalarGridSpec(
            num_scalar_prefetch=1,
            grid=(1,),
            in_specs=[whole(a_own.shape)] * 2 + [whole(b_own.shape)] * 2,
            out_specs=[whole(p.shape) for p in shapes],
        ),
        out_shape=shapes,
        compiler_params=PARAMS,
        cost_estimate=FREE,
    )(places, a_own, a_other, b_own, b_other)


def spread_pairs(plan):
    pairs = []
    for shard in range(plan.n):
        rank, block = shard // (2 * plan.n_f), shard % (2 * plan.n_f)
        pairs.append((shard, block // 2 * plan.n_s + block % 2 * plan.ranks + rank))
    return pairs


def gather_attention_whole(plan, matrices):
    layers, _, cols = matrices[0].shape
    size = cols // plan.ranks
    result = []
    for layer in range(layers):
        full = [lax.all_gather(m[layer], ALL, axis=0, tiled=True) for m in matrices]
        qkv = [lax.dynamic_slice_in_dim(m, plan.rank * size, size, 1) for m in full[:3]]
        w_out = lax.dynamic_slice_in_dim(full[3], plan.rank * size, size, 0)
        result.append((jnp.concatenate(qkv, axis=1), w_out))
    return result


def rank_columns(plan, order, matrices, vectors):
    query, key, value, out = matrices
    layers, rows, cols = query.shape
    half = cols // 2
    quarter = half // 2
    upper = bit_of(plan.s, 2) == 1
    send = [jnp.where(upper, m[..., :half], m[..., half:]) for m in (query, key, value)]
    extra = jnp.pad(vectors, ((0, 15), (0, half - vectors.shape[1])))
    send = jnp.concatenate([jnp.stack(send, axis=1).reshape(-1, half), extra], axis=0)
    there = plan.swap(order.done(send), "seq", 2)
    out = lax.ppermute(out, ALL, spread_pairs(plan))
    yield
    query, key, value, there = order.tie(query, key, value, there)
    here = [jnp.where(upper, m[..., half:], m[..., :half]) for m in (query, key, value)]
    more = there[-16:-15, :quarter]
    there = there[:-16].reshape(layers, 3, rows, half)
    both = jnp.stack([jnp.stack(here, axis=1), there], axis=2)
    upper = plan.core == 1
    send = jnp.where(upper, both[..., :quarter], both[..., quarter:])
    shape = send.shape
    vectors = jnp.concatenate([vectors, more], axis=0)
    extra = jnp.pad(vectors, ((0, 14), (0, 0)))
    send = jnp.concatenate([send.reshape(-1, quarter), extra], axis=0)
    there = plan.swap(order.done(send), "seq", 1)
    here = jnp.where(upper, both[..., quarter:], both[..., :quarter])
    yield
    vectors = jnp.concatenate([vectors, there[-16:-14]], axis=0)
    return here, there[:-16].reshape(shape), out, vectors


def gather_attention(plan, order, places, columns):
    columns = order.tie(*columns)
    here, there, out = columns[:3]
    quarter = here.shape[-1]
    qkv = jnp.stack([here, there], axis=1).reshape(-1, quarter)
    w_out = jnp.stack([out[:, k * quarter : (k + 1) * quarter] for k in range(4)])
    extra = [jnp.pad(v, ((0, 16 - v.shape[0]), (0, 0))) for v in columns[3:]]
    bundle = jnp.concatenate([qkv, w_out.reshape(-1, quarter), *extra], axis=0)
    other = plan.swap(order.done(bundle), "seq", plan.ranks)
    yield
    bundle, other = order.tie(bundle, other)
    size = qkv.shape[0] * 2 // 3
    part_a = order.done(jnp.stack([bundle[:size], other[:size]]))
    part_b = order.done(jnp.stack([bundle[size:], other[size:]]))
    other_a = plan.swap(part_a, "fsdp", plan.lo)
    other_b = plan.swap(part_b, "fsdp", plan.hi)
    yield
    part_a, other_a, part_b, other_b = order.tie(part_a, other_a, part_b, other_b)
    part_a = order.done(jnp.concatenate([part_a, other_a], axis=0))
    part_b = order.done(jnp.concatenate([part_b, other_b], axis=0))
    other_a = plan.swap(part_a, "fsdp", plan.hi)
    other_b = plan.swap(part_b, "fsdp", plan.lo)
    yield
    result = assemble(places, *order.tie(part_a, other_a, part_b, other_b))
    order.done(result[1])
    return result


def scatter_attention_whole(plan, x_pieces, g_pieces, dqkv, att):
    size = dqkv.shape[0] // len(x_pieces)
    x_pieces = [x[:size] for x in x_pieces]
    w_qkv = sum(mm_outer(x, d) for x, d in zip(x_pieces, jnp.split(dqkv, len(x_pieces))))
    w_out = sum(mm_outer(a, g) for a, g in zip(jnp.split(att, len(g_pieces)), g_pieces))
    width, features = w_out.shape
    grads = []
    for grad, axis in [(g, 1) for g in jnp.split(w_qkv, 3, axis=1)] + [(w_out, 0)]:
        full = jnp.zeros((features, features), F32)
        full = lax.dynamic_update_slice_in_dim(full, grad, plan.rank * width, axis)
        grads.append(lax.psum_scatter(full, ALL, scatter_dimension=0, tiled=True))
    return grads


def scatter_attention(plan, order, places, x_pieces, g_pieces, dqkv, att, extra, last):
    count = len(x_pieces)
    tied = order.tie(*x_pieces, *g_pieces, dqkv, att)
    grads = attn_weights(places, tied[:count], tied[count : 2 * count], *tied[2 * count :], extra)
    order.done(grads[-1])
    half = ("seq", plan.ranks)
    a_send, a_keep, b_send, b_keep = grads
    hi, lo = ("fsdp", plan.hi), ("fsdp", plan.lo)

    def summed(first, keep, there):
        parts = [p.reshape(2, 2, *keep.shape[1:]) for p in (keep, there)]
        return Sum(plan, order, (first, half), parts)

    part_a = summed(lo, a_keep, plan.swap(a_send, *hi))
    part_b = summed(hi, b_keep, plan.swap(b_send, *lo))
    yield
    part_a.step(lo)
    part_b.step(hi)
    yield
    part_a.tie()
    part_b.tie()
    send = jnp.concatenate([part_a.sending(half), part_b.sending(half)], axis=0)
    there = plan.swap(order.done(send), *half)
    high = a_send.shape[1]
    part_a.receive(there[:high])
    part_b.receive(there[high:])
    yield
    if not last:
        part_a.settle()
        yield
    part_a.tie()
    part_b.tie()
    total_b = order.done(part_b.total().astype(BF))
    return part_a.total().astype(BF), total_b


def finish_attention(plan, order, totals):
    layers = len(totals)
    high, width = totals[0][0].shape
    rows = high // 8
    parts_a = jnp.stack([a for a, _ in totals]).reshape(layers, 2, 2, 2, rows, width)
    parts_b = jnp.stack([b[:high] for _, b in totals]).reshape(layers, 2, 4, rows, width)
    out = jnp.concatenate([parts_b[:, 1, k] for k in range(4)], axis=2)
    out = lax.ppermute(out, ALL, [(b, a) for a, b in spread_pairs(plan)])
    value = parts_b[:, 0].reshape(layers, 1, 2, 2, rows, width)
    qkv = jnp.concatenate([parts_a, value], axis=1)
    extra = totals[0][1][high : high + 4].reshape(2, 2, width)

    def trade(qkv, extra, mine, axis, bit):
        here, send = choose(mine, qkv, axis)
        extra, extra_send = choose(mine, extra, 0)
        extra_send = extra_send.reshape(-1, width)
        pad = jnp.zeros((16 - extra_send.shape[0], width), BF)
        send_all = jnp.concatenate([send.reshape(-1, width), extra_send, pad], axis=0)
        there = plan.swap(order.done(send_all), "seq", bit)
        return here, extra, there

    def take(here, extra, there):
        here, extra, there = order.tie(here, extra, there)
        size = here.size // width
        count = extra.size // width
        more = there[size : size + count].reshape(extra.shape)
        return here, there[:size].reshape(here.shape), extra.astype(F32) + more.astype(F32)

    upper = bit_of(plan.s, 2)
    traded = trade(qkv, extra, upper, 2, 2)
    yield
    here, there, extra = take(*traded)
    qkv = stack_by(upper, here, there, 0)
    traded = trade(qkv, extra.astype(BF), plan.core, 3, 1)
    yield
    here, there, extra = take(*traded)
    (out,) = order.tie(out)
    qkv = stack_by(plan.core, here, there, 1)
    qkv = jnp.concatenate([qkv[0, 0], qkv[0, 1], qkv[1, 0], qkv[1, 1]], axis=3).astype(F32)
    return [qkv[:, 0], qkv[:, 1], qkv[:, 2], out.astype(F32)], extra


def split_units(plan, fc_in):
    layers, rows, units = fc_in.shape
    value = fc_in.reshape(layers, rows, 2, plan.n // 4, 2, units // plan.n)
    value = jnp.transpose(value, (0, 4, 2, 1, 3, 5))
    return value.reshape(layers, 2, 2, rows, units // 4)


def gather_ffn_whole(plan, fc_in, fc_out):
    full = lax.all_gather(split_units(plan, fc_in[None])[0], ALL, axis=2, tiled=True)
    first, _ = choose(plan.core, full, 0)
    full = lax.all_gather(fc_out, ALL, axis=0, tiled=True)
    full = full.reshape(plan.n // 2, 2, fc_out.shape[0], fc_out.shape[1])
    second, _ = choose(plan.core, full, 1)
    return first, second.reshape(-1, fc_out.shape[1])


def gather_ffn(plan, order, here, there, fc_out):
    width = fc_out.shape[1]
    here, there, fc_out = order.tie(here, there, fc_out)
    value = [here.reshape(-1, width), there.reshape(-1, width), fc_out]
    value = order.done(jnp.concatenate(value, axis=0))
    other = plan.swap(value, "seq", plan.ranks)
    yield
    value, other = order.tie(value, other)
    value = order.done(jnp.stack([value, other]))
    other = plan.swap(value, "seq", 2)
    yield
    value, other = order.tie(value, other)
    size = fc_out.shape[0]
    first = jnp.concatenate([value[:, :-size], other[:, :-size]], axis=0)
    second = jnp.concatenate([value[:, -size:], other[:, -size:]], axis=0)
    first, second = order.done(first), order.done(second)
    first_there = plan.swap(first, "fsdp", plan.lo)
    second_there = plan.swap(second, "fsdp", plan.hi)
    yield
    first, second, first_there, second_there = order.tie(first, second, first_there, second_there)
    first = order.done(jnp.concatenate([first, first_there], axis=0))
    second = order.done(jnp.concatenate([second, second_there], axis=0))
    first_there = plan.swap(first, "fsdp", plan.hi)
    second_there = plan.swap(second, "fsdp", plan.lo)
    yield
    return first, second, first_there, second_there


def place_weights(place_ref, weights, w_in_ref, w_out_ref):
    if len(weights) == 2:
        w_in_ref[...] = weights[0][...]
        w_out_ref[...] = weights[1][...]
        return
    core, own = place_ref[0], place_ref[3]
    f, half, z = own // 2, own % 2, place_ref[4] // 2
    for number, ref in enumerate(weights):
        height = ref.shape[1]
        for block in range(8):
            one, other = block // 4, number // 2
            f_there = f ^ (one + 2 * other if number % 2 == 0 else 2 * one + other)
            device = f_there * 4 + (half ^ (block % 2)) * 2 + (z ^ (block // 2 % 2))
            if number % 2 == 1:
                place = pl.ds(pl.multiple_of(device * height, height), height)
                w_out_ref[place, :] = ref[block]
                continue
            rows = height // 4
            for piece in range(4):
                start = (device * 2 + (core ^ (piece // 2))) * rows
                place = pl.ds(pl.multiple_of(start, rows), rows)
                w_in_ref[piece % 2, place, :] = ref[block, piece * rows : (piece + 1) * rows, :]


def ffn_forward_kernel(count, place_ref, *refs):
    m_own, m_sib = refs[:2]
    weights = refs[2 : 2 + count]
    own_ref, sib_ref, kept_ref, w_in_ref, w_out_ref, total_ref = refs[2 + count :]
    step = pl.program_id(0)
    rows = m_own.shape[0]
    chunk = kept_ref.shape[2]

    @pl.when(step == 0)
    def _():
        place_weights(place_ref, weights, w_in_ref, w_out_ref)
        total_ref[...] = jnp.zeros_like(total_ref)

    middle = jnp.concatenate([m_own[...], m_sib[...]], axis=0)
    lanes = pl.ds(pl.multiple_of(step % 2 * chunk, chunk), chunk)
    before = mm(middle, w_in_ref[step // 2, :, lanes])
    bell = 0.5 * (1.0 + lax.erf(before * inv_root_two))
    active = (before * bell).astype(BF)
    kept_ref[0] = active
    kept_ref[1] = (bell + before * jnp.exp(-0.5 * before * before) * inv_root_two_pi).astype(BF)
    total_ref[...] += mm(active, w_out_ref[pl.ds(pl.multiple_of(step * chunk, chunk), chunk), :])

    @pl.when(step == 3)
    def _():
        own_ref[...] = total_ref[:rows, :]
        sib_ref[...] = total_ref[rows:, :].astype(BF)


def ffn_forward(places, middles, weights, units):
    rows, width = middles[0].shape
    chunk = units // 8
    block = (rows, width)
    return pl.pallas_call(
        functools.partial(ffn_forward_kernel, len(weights)),
        grid_spec=pltpu.PrefetchScalarGridSpec(
            num_scalar_prefetch=1,
            grid=(4,),
            in_specs=[whole(block)] * 2 + [whole(w.shape) for w in weights],
            out_specs=[
                whole(block), whole(block),
                pl.BlockSpec((2, 2 * rows, chunk), lambda i, p: (0, 0, i)),
            ],
            scratch_shapes=[
                pltpu.VMEM((2, width, 2 * chunk), BF),
                pltpu.VMEM((4 * chunk, width), BF),
                pltpu.VMEM((2 * rows, width), F32),
            ],
        ),
        out_shape=[
            struct(block, F32), struct(block, BF), struct((2, 2 * rows, 4 * chunk), BF),
        ],
        compiler_params=PARAMS,
        cost_estimate=FREE,
    )(places, *middles, *weights)


def ffn_backward_kernel(count, place_ref, *refs):
    g_own, g_sib, m_own, m_sib, kept_ref = refs[:5]
    weights = refs[5 : 5 + count]
    own_ref, sib_ref, in_send, in_keep, out_send, out_keep = refs[5 + count : 11 + count]
    w_in_ref, w_out_ref, total_ref = refs[11 + count :]
    step = pl.program_id(0)
    rows, width = g_own.shape
    chunk = kept_ref.shape[2]

    @pl.when(step == 0)
    def _():
        place_weights(place_ref, weights, w_in_ref, w_out_ref)
        total_ref[...] = jnp.zeros_like(total_ref)

    upper, part = step % 2, (step // 2 + 1 + place_ref[2]) % 2
    grads = jnp.concatenate([g_own[...], g_sib[...]], axis=0)
    units = pl.ds(pl.multiple_of((upper * 2 + part) * chunk, chunk), chunk)
    before_grad = (mm_t(grads, w_out_ref[units, :]) * kept_ref[1].astype(F32)).astype(BF)
    lanes = pl.ds(pl.multiple_of(part * chunk, chunk), chunk)
    total_ref[...] += mm_t(before_grad, w_in_ref[upper, :, lanes])
    half = width // 2
    for mine, ref in ((1 - place_ref[1], in_send), (place_ref[1], in_keep)):
        lanes = pl.ds(pl.multiple_of(mine * half, half), half)
        middle = jnp.concatenate([m_own[:, lanes], m_sib[:, lanes]], axis=0)
        ref[...] = mm_outer(middle, before_grad, BF).reshape(ref.shape)
    out_grad = mm_outer(kept_ref[0], grads, BF)

    @pl.when(step < 2)
    def _():
        out_send[0] = out_grad

    @pl.when(step >= 2)
    def _():
        out_keep[0] = out_grad

    @pl.when(step == 3)
    def _():
        own_ref[...] = total_ref[:rows, :]
        sib_ref[...] = total_ref[rows:, :].astype(BF)


def ffn_backward(places, grads, middles, kept, weights, rows_each):
    rows, width = grads[0].shape
    chunk = kept.shape[2] // 4

    def column(step, places):
        return step % 2 * 2 + (step // 2 + 1 + places[2]) % 2

    block = (rows, width)
    groups = width // 2 // rows_each if rows_each % 16 == 0 else 1
    tall = (groups, 2, width // 2 // groups, 2 * chunk)
    side = pl.BlockSpec(
        (groups, 1, tall[2], chunk), lambda i, p: (0, column(i, p) // 2, 0, column(i, p) % 2)
    )
    return pl.pallas_call(
        functools.partial(ffn_backward_kernel, len(weights)),
        grid_spec=pltpu.PrefetchScalarGridSpec(
            num_scalar_prefetch=1,
            grid=(4,),
            in_specs=[whole(block)] * 4
            + [pl.BlockSpec((2, 2 * rows, chunk), lambda i, p: (0, 0, column(i, p)))]
            + [whole(w.shape) for w in weights],
            out_specs=[
                whole(block), whole(block), side, side,
                pl.BlockSpec((1, chunk, width), lambda i, p: (jnp.minimum(i, 1), 0, 0)),
                pl.BlockSpec((1, chunk, width), lambda i, p: (jnp.maximum(i - 2, 0), 0, 0)),
            ],
            scratch_shapes=[
                pltpu.VMEM((2, width, 2 * chunk), BF),
                pltpu.VMEM((4 * chunk, width), BF),
                pltpu.VMEM((2 * rows, width), F32),
            ],
        ),
        out_shape=[
            struct(block, F32), struct(block, BF),
            struct(tall, BF), struct(tall, BF),
            struct((2, chunk, width), BF), struct((2, chunk, width), BF),
        ],
        compiler_params=PARAMS,
        cost_estimate=FREE,
    )(places, *grads, *middles, kept, *weights)


def scatter_ffn(plan, order, last, in_send, in_keep, out_send, out_keep):
    hi, lo, half = ("fsdp", plan.hi), ("fsdp", plan.lo), ("seq", plan.ranks)
    inner = [("fsdp", b) for b in reversed(plan.f_bits) if b not in (plan.hi, plan.lo)]
    z_names = [("seq", b) for b in reversed(plan.z_bits)]
    tail = (*inner, half, *z_names)
    width = out_keep.shape[-1]
    count = 2 ** (1 + len(tail))
    if in_keep.shape[0] == 1:
        shape = in_keep.shape

        def spread_rows(value):
            value = value.reshape(2, count, shape[2] // count, width)
            return jnp.swapaxes(value, 0, 1)

        in_send, in_keep = spread_rows(in_send), spread_rows(in_keep)

    def summed(first, keep, there):
        shape = (2,) * (1 + len(tail)) + (-1, width)
        return Sum(plan, order, (first, *tail), [keep.reshape(shape), there.reshape(shape)])

    first = summed(lo, in_keep, plan.swap(in_send, *hi))
    second = summed(hi, out_keep, plan.swap(out_send, *lo))
    yield
    first_names = [lo, *inner, *z_names]
    steps = list(zip(first_names, [hi, *inner, *z_names])) + [(half, half)]
    for one, two in steps:
        if one == two:
            first.tie()
            second.tie()
            send = jnp.stack([first.sending(one), second.sending(one)])
            there = plan.swap(order.done(send), *one)
            first.receive(there[0])
            second.receive(there[1])
        else:
            first.step(one)
            second.step(two)
        yield
        if not last and one not in (lo, hi):
            first.settle()
            second.settle()
            yield
    first.tie()
    second.tie()
    total = order.done(second.total())
    return first.total().astype(BF).reshape(2, 2, -1, width), total


def finish_ffn(plan, order, totals):
    fc_in = jnp.stack([a for a, _ in totals])
    here, send = choose(plan.core, fc_in, 2)
    there = plan.swap(order.done(send), "seq", 1)
    yield
    here, there = order.tie(here, there)
    layers, _, rows, _ = here.shape
    pair = [jnp.swapaxes(v, 1, 2).reshape(layers, rows, plan.n // 2, -1) for v in (here, there)]
    fc_in = stack_by(plan.core, *pair, 3)
    fc_in = order.done(fc_in.reshape(layers, rows, -1).astype(F32))
    return fc_in, jnp.stack([b for _, b in totals])


def gather_vectors(plan, order, vectors):
    layers, count, own = vectors.shape
    value = order.done(vectors.reshape(1, -1))
    names = [("seq", b) for b in [1] + plan.z_bits + [plan.ranks]]
    names += [("fsdp", b) for b in plan.f_bits]
    for name in names:
        there = plan.swap(value, *name)
        yield
        value, there = order.tie(value, there)
        mine = bit_of(plan.f if name[0] == "fsdp" else plan.s, name[1])
        value = order.done(stack_by(mine, value, there, 0).reshape(-1, value.shape[-1]))
    return natural_vectors(plan, value, layers, count)


def natural_vectors(plan, value, layers, count):
    value = value.reshape(plan.n, layers, count, -1)
    return jnp.transpose(value, (1, 2, 0, 3)).reshape(layers, count, -1).astype(F32)


def sum_vectors(plan, vectors):
    count, width = vectors.shape
    value = vectors.reshape(count, plan.n, width // plan.n)
    value = jnp.transpose(value, (1, 0, 2)).reshape(plan.n, -1)
    value = lax.all_to_all(value, ALL, split_axis=0, concat_axis=0, tiled=True)
    return jnp.sum(value, axis=0).reshape(count, width // plan.n)


def local(
    mesh_shape,
    inputs,
    segment_ids,
    query_weight,
    key_weight,
    value_weight,
    out_weight,
    fc_in_weight,
    fc_out_weight,
    attn_gain,
    attn_shift,
    ffn_gain,
    ffn_shift,
    cotangent,
):
    layers, _, width = query_weight.shape
    plan = Plan(mesh_shape, width, fc_in_weight.shape[2])
    places = plan.scalars()
    head_dim = width // HEADS

    def to_halves(value):
        mine, other = choose(plan.half, value, 0)
        return jnp.concatenate([mine, plan.swap(other, "seq", plan.ranks)], axis=0)

    def from_halves(value):
        size = value.shape[0] // 2
        there = plan.swap(value[size:].astype(BF), "seq", plan.ranks).astype(F32)
        return stack_by(plan.half, value[:size], there, 0)

    order, tasks = Order(), Tasks()
    matrices = (query_weight, key_weight, value_weight, out_weight)
    vectors = jnp.stack([attn_gain, attn_shift, ffn_gain, ffn_shift], axis=1)
    tokens, units = 2 * inputs.shape[1], fc_in_weight.shape[2]
    marks = jnp.pad(
        segment_ids.astype(BF)[:, None, :], ((0, 0), (0, 15), (0, width - inputs.shape[1]))
    )

    def with_marks(value):
        mine, other = choose(plan.half, value, 0)
        there = plan.swap(other, "seq", plan.ranks)
        there, mine = order.tie(there, mine)
        size = tokens // 2
        low = jnp.concatenate([mine[:size], there[:size]], axis=0)
        row = jnp.concatenate([mine[size:, :size], there[size:, :size]], axis=1)
        row = jnp.pad(row, ((0, 0), (0, width - tokens)))
        return order.done(jnp.concatenate([low, row], axis=0)), low

    marked = jnp.concatenate([inputs, marks], axis=1)
    if plan.fast:
        columns = tasks.add(rank_columns(plan, order, matrices, vectors.reshape(1, -1)))
        fc_here, fc_send = choose(plan.core, split_units(plan, fc_in_weight), 1)
        fc_there = plan.swap(order.done(fc_send), "seq", 1)

        def fetch(layer):
            parts = (here[layer], there[layer], out[layer]) + ((rows,) if layer == 0 else ())
            return tasks.add(gather_attention(plan, order, places, parts))

        def fetch_ffn(layer):
            parts = (fc_here[layer], fc_there[layer], fc_out_weight[layer])
            return tasks.add(gather_ffn(plan, order, *parts))

        ffn = [fetch_ffn(0)]
        tasks.drain(columns)
        here, there, out, rows = columns.result
        attention = [fetch(0)]
        marked, x_low = with_marks(marked)
        x_pieces = group_pieces(plan, marked)
        cell = {"x": x_pieces}

        def act(names):
            for name in names:
                if name == "f0":
                    ffn[0].run()
                elif name == "f1":
                    ffn[1].run()
                elif name == "F1":
                    ffn.append(fetch_ffn(1))
                elif name == "a0":
                    attention[0].run()
                elif name == "a1":
                    attention[1].run()
                elif name == "A0":
                    tasks.drain(attention[0])
                elif name == "A1":
                    tasks.drain(attention[1])
                elif name == "B1":
                    attention.append(fetch(1))
                elif name == "x":
                    cell["x"] = order.tie(*cell["x"])
                    order.done(cell["x"][-1])
                elif name == "cot":
                    (value,) = order.tie(cotangent)
                    cell["up"] = to_halves(value)
                elif name == "cotD":
                    (cell["up"],) = order.tie(cell["up"])
                    order.done(cell["up"])

        act(STEPS["start"])
        x_pieces = cell["x"]
    else:
        marked, x_low = with_marks(marked)
        x_pieces = group_pieces(plan, marked)
        upstream = to_halves(cotangent)
        ffn = [
            Task.finished(gather_ffn_whole(plan, fc_in_weight[k], fc_out_weight[k]))
            for k in range(layers)
        ]
        vectors = tasks.add(gather_vectors(plan, order, vectors))
        tasks.drain(vectors)
        vectors = vectors.result
        attention = [Task.finished(m) for m in gather_attention_whole(plan, matrices)]
    ids = jnp.concatenate([p[tokens, :tokens] for p in x_pieces]).astype(jnp.int32)

    hidden = x_low
    records = []
    for layer in range(layers):
        tasks.drain(attention[layer])
        if plan.fast and layer == 0:
            vectors = natural_vectors(plan, attention[0].result[2], layers, 4)
        gains = [vectors[layer, k][None] for k in range(4)]
        w_qkv, w_out = attention[layer].result[:2]
        tied = order.tie(*x_pieces, w_qkv, w_out, ids)
        x_pieces = tied[:-3]
        qkv, att, lse, keep, send = attn_forward(x_pieces, *tied[-3:], head_dim)
        order.done(send)
        on = plan.fast
        if on:
            act(STEPS["after_attention"] if layer == 0 else [])
            (send,) = order.tie(send)
        parts = group_sum(plan, order, keep, plan.swap(send, "seq", 1))
        if on and layer == 0:
            act(STEPS["attention_sum"])
        if STEPS["weights_early"][layer]:
            tasks.drain(ffn[layer])
            weights = order.tie(*ffn[layer].result)
            order.done(weights[-1])
        middle, mid_low, normed_attn, inverse_attn = norm_forward(
            order.tie(hidden, *parts), gains[0], gains[1], tokens
        )
        order.done(mid_low)
        middles = (mid_low, plan.swap(mid_low, "seq", 1))
        if on and layer == 0:
            act(STEPS["after_norm"])
        if not STEPS["weights_early"][layer]:
            tasks.drain(ffn[layer])
            weights = ffn[layer].result
        tied = order.tie(*middles, *weights)
        own, sibling, kept = ffn_forward(places, tied[:2], tied[2:], units)
        order.done(sibling)
        sibling = plan.swap(sibling, "seq", 1)
        if on and layer == 0:
            act(STEPS["ffn_sum"])
        hidden, x_low, normed_ffn, inverse_ffn = norm_forward(
            order.tie(middle, own, sibling), gains[2], gains[3], tokens
        )
        order.done(x_low)
        next_pieces = group_pieces(plan, x_low) if layer + 1 < layers else None
        if on and layer == 0:
            act(STEPS["next_rows"])
        records.append(
            (x_pieces, qkv, att, lse, normed_attn, inverse_attn, normed_ffn, inverse_ffn, kept, middles)
        )
        x_pieces = next_pieces
    upstream = [cell["up"]] if plan.fast else [upstream]
    outputs = from_halves(hidden)

    grads, vector_grads = [None] * layers, [None] * layers
    older = ()
    for layer in reversed(range(layers)):
        (
            x_pieces, qkv, att, lse, normed_attn, inverse_attn, normed_ffn, inverse_ffn, kept, middles,
        ) = records[layer]
        gains = vectors[layer]
        w_qkv, w_out = attention[layer].result[:2]
        sum_grad, ff_grad, gain_ffn_grad, shift_ffn_grad = norm_backward(
            order.tie(*upstream), normed_ffn, inverse_ffn, gains[2:3]
        )
        order.done(ff_grad)
        ff_sibling = plan.swap(ff_grad, "seq", 1)
        now = {}

        def back(names):
            for name in names:
                if name == "o0":
                    older[0].run()
                elif name == "o1":
                    older[1].run()
                elif name == "c0":
                    now["ffn"].run()
                elif name == "c1":
                    now["attn"].run()
                elif name == "W":
                    now["attn"] = scatter()
                elif name == "Z":
                    now["up"] = [attn_sum_grad] + group_sum(plan, order, keep, there)
                elif name == "G":
                    rows_grad = add_parts(order.tie(*now["up"]), tokens)
                    order.done(rows_grad)
                    now["in"] = from_halves(rows_grad)
                elif name == "GD":
                    (now["in"],) = order.tie(now["in"])
                    order.done(now["in"])
                elif name == "OD":
                    (now["out"],) = order.tie(outputs)
                    order.done(now["out"])

        slots = STEPS["lowest" if layer == 0 else "upper"]
        back(slots[0])
        tied = order.tie(ff_grad, ff_sibling, *middles, kept)
        own, sibling, *ffn_grads = ffn_backward(
            places, tied[:2], tied[2:4], tied[4], ffn[layer].result, 2 * fc_in_weight.shape[1]
        )
        order.done(sibling)
        now["ffn"] = ffn_task = tasks.add(
            scatter_ffn(plan, order, layer == 0, *ffn_grads)
        )
        sibling = plan.swap(sibling, "seq", 1)
        back(slots[1])
        tied = order.tie(sum_grad, own, sibling)
        attn_sum_grad, branch_grad, gain_attn_grad, shift_attn_grad = norm_backward(
            tied, normed_attn, inverse_attn, gains[0:1]
        )
        order.done(branch_grad)
        g_pieces = group_pieces(plan, branch_grad)
        vector_grads[layer] = (gain_attn_grad, shift_attn_grad, gain_ffn_grad, shift_ffn_grad)
        extra = jnp.zeros((8, 16, width // plan.ranks), BF)
        if layer == 0:
            summed = jnp.concatenate([v for member in vector_grads for v in member], axis=0)
            if plan.fast:
                extra = summed.reshape(4 * layers, 8, plan.ranks, -1)
                extra = jnp.transpose(extra, (1, 2, 0, 3)).reshape(8, plan.ranks, -1)
                extra = jnp.pad(extra.astype(BF), ((0, 0), (0, 16 - plan.ranks), (0, 0)))
        g_pieces = order.tie(*g_pieces)
        order.done(g_pieces[-1])
        back(slots[2])
        tied = order.tie(*g_pieces, qkv)
        g_pieces = tied[:-1]
        dqkv, keep, send = attn_backward(
            g_pieces, tied[-1], att, lse, w_qkv, w_out, ids, head_dim
        )
        order.done(send)
        if slots[3]:
            back(slots[3])
            (send,) = order.tie(send)
        there = plan.swap(send, "seq", 1)

        def scatter():
            if not plan.fast:
                return Task.finished(scatter_attention_whole(plan, x_pieces, g_pieces, dqkv, att))
            parts = (x_pieces, g_pieces, dqkv, att, extra, layer == 0)
            return tasks.add(scatter_attention(plan, order, places, *parts))

        back(slots[4])
        attn_task = now["attn"]
        grads[layer] = (ffn_task, attn_task)
        if layer > 0:
            older = grads[layer]
            upstream = now["up"]
        else:
            input_grad = now["in"]
        if "out" in now:
            outputs = now["out"]
    tasks.drain(ffn_task)
    for member in grads:
        tasks.drain(member[0])
    fc_task = tasks.add(finish_ffn(plan, order, [f.result for f, _ in grads]))
    for member in grads:
        tasks.drain(member[1])
    if plan.fast:
        attn_task = tasks.add(finish_attention(plan, order, [a.result for _, a in grads]))
        tasks.finish()
        attn_grads, summed = attn_task.result
    else:
        tasks.finish()
        summed = sum_vectors(plan, summed)
        attn_grads = [jnp.stack([a.result[k] for _, a in grads]) for k in range(4)]
    fc_in_grad, fc_out_grad = fc_task.result
    summed = summed.reshape(layers, 4, -1)
    return (
        outputs, input_grad, *attn_grads, fc_in_grad, fc_out_grad, *(summed[:, k] for k in range(4)),
    )


def solution(mesh):
    tokens = P("fsdp", "seq", None)
    matrix = P(None, ("fsdp", "seq"), None)
    vector = P(None, ("fsdp", "seq"))
    return jax.shard_map(
        functools.partial(local, dict(mesh.shape)),
        mesh=mesh,
        in_specs=(tokens, P("fsdp", "seq"), *[matrix] * 6, *[vector] * 4, tokens),
        out_specs=(tokens, tokens, *[matrix] * 6, *[vector] * 4),
        check_vma=False,
    )
```
